32 devices in a mesh: dp: 8 (over z, y), expert: 4 (over x, core).
Axes of the slice: x: 2, y: 2, z: 4, core: 2. Of those that a mesh axis runs over, the one named last changes fastest.
Arguments:
- inputs: bfloat16 [8, 1024, 768], P('dp', 'expert'), may hold values from -6 to 6
- norm1_gain: bfloat16 [768], P('dp'), may hold values from 0.5 to 1.5
- qkv_weight: bfloat16 [768, 2304], P('dp'), may hold values from -0.21875 to 0.21875
- out_weight: bfloat16 [768, 768], P('dp'), may hold values from -2.5 to 2.5
- norm2_gain: bfloat16 [768], P('dp'), may hold values from 0.5 to 1.5
- router_weight: bfloat16 [768, 4], P('dp'), may hold values from -0.21875 to 0.21875
- shared_gate: bfloat16 [768, 2048], P('dp'), may hold values from -0.21875 to 0.21875
- shared_up: bfloat16 [768, 2048], P('dp'), may hold values from -0.21875 to 0.21875
- shared_down: bfloat16 [2048, 768], P('dp'), may hold values from -0.125 to 0.125
- expert_gate: bfloat16 [4, 768, 2048], P('expert'), may hold values from -0.21875 to 0.21875
- expert_up: bfloat16 [4, 768, 2048], P('expert'), may hold values from -0.21875 to 0.21875
- expert_down: bfloat16 [4, 2048, 768], P('expert'), may hold values from -0.125 to 0.125
- expert_ids: int32 [8, 1024, 2], P('dp', 'expert'), may hold values from 0 to 3, all different within a row; in each aligned block of 256 rows (0 to 255, 256 to 511, ..., all dimensions but the last counted through in order) at most 256 rows name the same one
- piece_starts: int32 [8, 2], P('dp'), may hold values from 0 to 768, as said below
- cotangent: bfloat16 [8, 1024, 768], P('dp', 'expert'), may hold values from -6 to 6
Outputs:
- outputs: bfloat16 [8, 1024, 768], P('dp', 'expert')
- input_grad: bfloat16 [8, 1024, 768], P('dp', 'expert')
- grad_norm1_gain: float32 [768], P(('dp', 'expert'))
- grad_qkv_weight: float32 [768, 2304], P(('dp', 'expert'))
- grad_out_weight: float32 [768, 768], P(('dp', 'expert'))
- grad_norm2_gain: float32 [768], P(('dp', 'expert'))
- grad_router_weight: float32 [768, 4], P(('dp', 'expert'))
- grad_shared_gate: float32 [768, 2048], P(('dp', 'expert'))
- grad_shared_up: float32 [768, 2048], P(('dp', 'expert'))
- grad_shared_down: float32 [2048, 768], P(('dp', 'expert'))
- grad_expert_gate: float32 [4, 768, 2048], P('expert', 'dp')
- grad_expert_up: float32 [4, 768, 2048], P('expert', 'dp')
- grad_expert_down: float32 [4, 2048, 768], P('expert', 'dp')
The draws below stay inside these ranges and needn't reach their ends.
Inputs may be any that keep to these rules, and one draw needn't show every extreme that they name: `expert_ids`: each token names 2 different experts. Among the rows of one device no expert is named by more than 256 rows, and in every draw some expert is named by exactly 256 rows of some device. `piece_starts`: the j-th start of a sequence lies in 2 * 256 * j to 2 * 256 * (j + 1) - 256, so pieces never intersect.
All inputs are finite; a program needn't handle non-finite values.
Results may differ from the reference program's by a relative error of at most 0.017.
Values may be sent and summed in bfloat16 or wider, within the bound.
No kernel may reach another device: no remote copies, remote signals or barrier semaphores. Data moves between devices by JAX's collectives and lax.ppermute only.
A program may use at most 256 MiB of HBM per device.

```python
import math
import jax
import jax.numpy as jnp
import numpy as np
from jax import lax

D = 768
HEAD_DIM = 64
FF_EXPERT = 2048
FF_SHARED = 2048
TOP = 2
TOK_DEV = 256
PIECE = 256
EXPERTS = 4
SEQS = 8
LENGTH = 1024
NPIECE = 2
CAP = 256
N_EXPERT = 4


def draw_piece_starts(key, part):
    key = jax.random.fold_in(key, 7)
    offsets = jax.random.randint(key, (SEQS, NPIECE), 0, 2 * TOK_DEV - PIECE + 1, dtype=jnp.int32)
    bases = jnp.arange(NPIECE, dtype=jnp.int32) * (2 * TOK_DEV)
    return (bases[None, :] + offsets).astype(jnp.int32)


def with_spikes(values, key, source, target, shards_of, factor):
    owner, partner = [(jnp.arange(values.shape[dim]) // (values.shape[dim] // shards_of)).reshape([-1 if axis == dim else 1 for axis in range(values.ndim)]) for dim in (source, target)]
    chosen = jax.random.permutation(key, shards_of)[partner]
    strong = (owner == chosen) | (owner == (partner + shards_of // 2) % shards_of)
    return jnp.where(strong, factor * values, values)


def steps_of(rng, dims, cuts, least, top_value):
    factor_of, own = 1.0, jax.random.fold_in(rng, 6)
    for position, blocks in cuts:
        heights = jnp.exp(jax.random.uniform(jax.random.fold_in(own, position), (blocks,), jnp.float32, least / len(cuts), top_value / len(cuts)))
        factor_of = factor_of * jnp.repeat(heights, dims[position] // blocks).reshape([-1 if axis == position else 1 for axis in range(len(dims))])
    return factor_of


def assign_block(own_key, own, number, rows, number_of, top, limit, slope):
    sequence = jax.random.permutation(own_key, number_of)
    heavy_load, usual = load_shares(number_of, rows * top, limit, slope, True), load_shares(number_of, rows * top, limit, slope, False)
    places = jnp.arange(number_of)

    def named(sizes, rotation):
        used = int((sizes > 0).sum())
        fixed = max(1, used // 4)
        moved = fixed + (places - fixed + rotation * (used - fixed)) % max(1, number_of - fixed)
        return jnp.zeros((number_of,), jnp.int32).at[sequence[jnp.where(places < fixed, places, moved)]].set(jnp.asarray(sizes, jnp.int32))

    sizes = jnp.where(number % 4 == 0, named(heavy_load, number // 4), named(usual, number - number // 4 - 1))
    mixed = jax.random.permutation(jax.random.fold_in(own, 3), number_of)
    source_of, receiver = mixed[0:number_of // 2 * 2:2], mixed[1:number_of // 2 * 2:2]
    margin = jnp.minimum(sizes[source_of] - 1, limit - sizes[receiver]) // 2
    margin = jnp.where((source_of == sequence[0]) | (receiver == sequence[0]) | (sizes[receiver] == 0), 0, jnp.maximum(margin, 0))
    moved = jax.random.randint(jax.random.fold_in(own, 4), (number_of // 2,), 0, 1 << 20) % (margin + 1)
    sizes = sizes.at[source_of].add(-moved).at[receiver].add(moved)
    members = jnp.searchsorted(jnp.cumsum(sizes), jnp.arange(rows * top), side="right").astype(jnp.int32)
    listing = members.reshape(top, rows).T
    listing = listing[jax.random.permutation(jax.random.fold_in(own, 1), rows)]
    rotation = jax.random.randint(jax.random.fold_in(own, 2), (rows, 1), 0, top)
    return jnp.take_along_axis(listing, (jnp.arange(top)[None, :] + rotation) % top, axis=1)


def load_shares(number_of, total, bound, slope, full):
    loads = [(1 << 20) // math.isqrt(grade ** slope) + 1 for grade in range(1, number_of + 1)]
    largest = bound if full else min(bound, max(-(-total // number_of), total * loads[0] // sum(loads)))
    least = 1 if total - largest >= number_of - 1 else 0
    holding, surplus = [largest] + [least] * (number_of - 1), total - largest - least * (number_of - 1)
    while surplus > 0:
        candidates = [i for i in range(1, number_of) if holding[i] < largest] or [i for i in range(1, number_of) if holding[i] < bound]
        pool, left = sum([loads[i] for i in candidates]), surplus
        for i in candidates:
            more = min(bound - holding[i], max(1, left * loads[i] // pool), surplus)
            holding[i] = holding[i] + more
            surplus = surplus - more
    return np.array(holding)


def scatter_about(key, shape, scale, reach, cuts=(), kind=jnp.bfloat16):
    entries = scale * jax.random.normal(key, shape, jnp.float32)
    if cuts:
        entries = entries * steps_of(key, shape, cuts, -0.22, 0.18)
    return jnp.clip(entries, -reach, reach).astype(kind)


def bell_draw_with(own_key, shape, scale, reach, split, heavy, held_as=jnp.bfloat16):
    values = scale * jax.random.normal(own_key, shape, jnp.float32)
    if split:
        values = values * steps_of(own_key, shape, split, -0.22, 0.18)
    return jnp.clip(with_spikes(values, jax.random.fold_in(own_key, 3), *heavy), -reach, reach).astype(held_as)


def setup_inputs(seed: int = 0) -> dict:
    key_of = jax.random.split(jax.random.key(seed), 16)
    inputs = scatter_about(key_of[0], (SEQS, LENGTH, D), 1.0, 6.0, ((0, 8), (1, 4)))
    norm1_gain = jnp.clip(1.0 + 0.1 * jax.random.normal(key_of[1], (D,), jnp.float32), 0.5, 1.5).astype(jnp.bfloat16)
    qkv_weight = scatter_about(key_of[2], (D, 3 * D), D ** -0.5, 0.21875, ((0, 8),))
    out_weight = scatter_about(key_of[3], (D, D), (D // 128) ** -0.5, 2.5, ((0, 8),))
    norm2_gain = jnp.clip(1.0 + 0.1 * jax.random.normal(key_of[4], (D,), jnp.float32), 0.5, 1.5).astype(jnp.bfloat16)
    router_weight = scatter_about(key_of[5], (D, EXPERTS), D ** -0.5, 0.21875, ((0, 8),))
    shared_gate = scatter_about(key_of[6], (D, FF_SHARED), D ** -0.5, 0.21875, ((0, 8),))
    shared_up = scatter_about(key_of[7], (D, FF_SHARED), D ** -0.5, 0.21875, ((0, 8),))
    shared_down = scatter_about(key_of[8], (FF_SHARED, D), FF_SHARED ** -0.5, 0.125, ((0, 8),))
    expert_gate = scatter_about(key_of[9], (EXPERTS, D, FF_EXPERT), D ** -0.5, 0.21875, ((0, 4),))
    expert_up = scatter_about(key_of[10], (EXPERTS, D, FF_EXPERT), D ** -0.5, 0.21875, ((0, 4),))
    expert_down = scatter_about(key_of[11], (EXPERTS, FF_EXPERT, D), FF_EXPERT ** -0.5, 0.125, ((0, 4),))
    expert_ids_keys = jax.random.split(jax.random.fold_in(key_of[12], 1), SEQS * LENGTH // TOK_DEV)
    expert_ids_turns = jax.random.permutation(jax.random.fold_in(key_of[12], 3), SEQS * LENGTH // TOK_DEV)
    expert_ids = jax.vmap(lambda own, number: assign_block(jax.random.fold_in(key_of[12], 2), own, number, TOK_DEV, EXPERTS, TOP, CAP, 2))(expert_ids_keys, expert_ids_turns).reshape((SEQS, LENGTH, TOP))
    piece_starts = draw_piece_starts(jax.random.fold_in(key_of[15], 71), 0)
    cotangent = bell_draw_with(key_of[14], (SEQS, LENGTH, D), 1.0, 6.0, ((0, 8), (1, 4)), (0, 2, 8, 2.0))
    return {"inputs": inputs, "norm1_gain": norm1_gain, "qkv_weight": qkv_weight, "out_weight": out_weight, "norm2_gain": norm2_gain, "router_weight": router_weight, "shared_gate": shared_gate, "shared_up": shared_up, "shared_down": shared_down, "expert_gate": expert_gate, "expert_up": expert_up, "expert_down": expert_down, "expert_ids": expert_ids, "piece_starts": piece_starts, "cotangent": cotangent}


precise_setting = lax.Precision.HIGHEST

@jax.custom_vjp
def low(v):
    return lax.optimization_barrier(v.astype(jnp.bfloat16)).astype(jnp.float32)

@jax.custom_vjp
def reduced_backward(v):
    return v

def low_keep(v):
    return (low(v), None)

def low_pass(kept, grad):
    return (grad,)

def back_keep(v):
    return (v, None)

def back_low(kept, grad):
    return (low(grad),)
low.defvjp(low_keep, low_pass)
reduced_backward.defvjp(back_keep, back_low)

def rounded_both(values):
    return low(reduced_backward(values))

def normalize(values, gain_vector):
    return values * lax.rsqrt(lax.optimization_barrier(jnp.mean(values * values, -1, keepdims=True)) + 1e-06) * gain_vector

def rotary_tables(positions):
    halfway = HEAD_DIM // 2
    frequency = jnp.power(10000.0, -jnp.arange(halfway, dtype=jnp.float32) / halfway)
    angles = positions.astype(jnp.float32)[:, None] * frequency[None, :]
    return (jnp.cos(angles), jnp.sin(angles))

def rotate(values, cosines, sines):
    halfway = cosines.shape[1]
    first_half = values[..., :halfway]
    second_half = values[..., halfway:]
    cos_part = cosines[:, None, :]
    sin_part = sines[:, None, :]
    return jnp.concatenate([first_half * cos_part - second_half * sin_part, second_half * cos_part + first_half * sin_part], -1)

def allowed(query_pos, key_pos, starts):
    query_in = (query_pos[:, None] >= starts[None, :]) & (query_pos[:, None] < starts[None, :] + PIECE)
    key_in = (key_pos[:, None] >= starts[None, :]) & (key_pos[:, None] < starts[None, :] + PIECE)
    same_piece = jnp.any(query_in[:, None, :] & key_in[None, :, :], -1)
    return (key_pos[None, :] <= query_pos[:, None]) | same_piece

def layer_one(parameters, sequence_in, routes, starts):
    leading_norm_gain, query_key_value_weight, output_weight, trailing_norm_gain, routing_weight, shared_gate_weight, shared_up_weight, shared_down_weight, expert_gate_weights, expert_up_weights, expert_down_weights = parameters
    width = sequence_in.shape[1]
    heads = width // HEAD_DIM
    top_count = routes.shape[1]
    experts = routing_weight.shape[1]
    positions = jnp.arange(LENGTH, dtype=jnp.int32)
    normed1 = low(normalize(sequence_in, leading_norm_gain))
    projected = reduced_backward(jnp.dot(normed1, query_key_value_weight, precision=precise_setting))
    cosines, sines = rotary_tables(positions)
    queries = low(rotate(projected[:, :width].reshape(LENGTH, heads, HEAD_DIM), cosines, sines))
    keys = low(rotate(projected[:, width:2 * width].reshape(LENGTH, heads, HEAD_DIM), cosines, sines))
    values = low(projected[:, 2 * width:]).reshape(LENGTH, heads, HEAD_DIM)
    scores = reduced_backward(jnp.einsum('qhd,khd->hqk', queries, keys, precision=precise_setting) * HEAD_DIM ** (-0.5))
    allowed_keys = allowed(positions, positions, starts)
    weights = low(jax.nn.softmax(jnp.where(allowed_keys[None], scores, -1e+30), axis=-1))
    mixed = rounded_both(jnp.einsum('hqk,khd->qhd', weights, values, precision=precise_setting).reshape(LENGTH, width))
    attended = reduced_backward(jnp.dot(mixed, output_weight, precision=precise_setting))
    resid2 = sequence_in + attended
    normed2 = low(normalize(resid2, trailing_norm_gain))
    logits = reduced_backward(jnp.dot(normed2, routing_weight, precision=precise_setting))
    choose = (routes[:, :, None] == jnp.arange(experts, dtype=jnp.int32)[None, None, :]).astype(jnp.float32)
    gates = jax.nn.softmax(lax.optimization_barrier(jnp.sum(choose * logits[:, None, :], -1)), axis=-1)
    shared_gate_pre = reduced_backward(jnp.dot(normed2, shared_gate_weight, precision=precise_setting))
    shared_up_pre = reduced_backward(jnp.dot(normed2, shared_up_weight, precision=precise_setting))
    shared_hidden = low(jax.nn.silu(shared_gate_pre) * shared_up_pre)
    shared_out = jnp.dot(shared_hidden, shared_down_weight, precision=precise_setting)
    block_count = N_EXPERT
    block_tokens = LENGTH // block_count
    block_routes = routes.reshape(block_count, block_tokens * top_count)
    onehot = (block_routes[:, :, None] == jnp.arange(experts, dtype=jnp.int32)[None, None, :]).astype(jnp.int32)
    before = jnp.cumsum(onehot, 1) - onehot
    where_to = (block_routes * CAP + lax.optimization_barrier(jnp.sum(before * onehot, -1))).astype(jnp.int32)
    source_rows = jnp.repeat(normed2.reshape(block_count, block_tokens, width), top_count, axis=1)

    def place(rows_in, targets):
        return jnp.zeros((experts * CAP, width), jnp.float32).at[targets].set(rows_in)
    buffers = jax.vmap(place)(source_rows, where_to).reshape(block_count, experts, CAP, width)
    routed_token_rows = reduced_backward(buffers)
    gate_pre = reduced_backward(jnp.einsum('lozi,oik->lozk', routed_token_rows, expert_gate_weights, precision=precise_setting))
    up_before_activation = reduced_backward(jnp.einsum('lozi,oik->lozk', routed_token_rows, expert_up_weights, precision=precise_setting))
    expert_hidden = low(jax.nn.silu(gate_pre) * up_before_activation)
    expert_out = rounded_both(jnp.einsum('cerf,efd->cerd', expert_hidden, expert_down_weights, precision=precise_setting))
    expert_out = expert_out.reshape(block_count, experts * CAP, width)

    def pick(block_out, targets):
        return block_out[targets]
    picked = jax.vmap(pick)(expert_out, where_to).reshape(LENGTH, top_count, width)
    mixture = lax.optimization_barrier(jnp.sum(gates[:, :, None] * picked, 1))
    return resid2 + mixture + shared_out

def reference(inputs, norm1_gain, qkv_weight, out_weight, norm2_gain, router_weight, shared_gate, shared_up, shared_down, expert_gate, expert_up, expert_down, expert_ids, piece_starts, cotangent):
    parameters = (norm1_gain.astype(jnp.float32), qkv_weight.astype(jnp.float32), out_weight.astype(jnp.float32), norm2_gain.astype(jnp.float32), router_weight.astype(jnp.float32), shared_gate.astype(jnp.float32), shared_up.astype(jnp.float32), shared_down.astype(jnp.float32), expert_gate.astype(jnp.float32), expert_up.astype(jnp.float32), expert_down.astype(jnp.float32))
    inputs_float = inputs.astype(jnp.float32)
    layer_step = jax.checkpoint(layer_one)

    def forward(weights_in, activations):

        def one_sequence(bundle):
            return layer_step(weights_in, bundle[0], bundle[1], bundle[2])
        return lax.map(one_sequence, (activations, expert_ids, piece_starts))
    result, pullback = jax.vjp(forward, parameters, inputs_float)
    grads, grad_inputs = pullback(cotangent.astype(jnp.float32))
    return (result.astype(jnp.bfloat16), grad_inputs.astype(jnp.bfloat16), grads[0], grads[1], grads[2], grads[3], grads[4], grads[5], grads[6], grads[7], grads[8], grads[9], grads[10])
```

```python
import jax
import jax.numpy as jnp
from jax import lax
from jax.sharding import PartitionSpec as P

HEAD_DIM = 64
PIECE = 256
F32 = jnp.float32
BF16 = jnp.bfloat16


def swap(value, axis, distance):
    count = lax.axis_size(axis)
    return lax.ppermute(value, axis, [(i, i ^ distance) for i in range(count)])


def bits_of(count):
    return [1 << k for k in range(count.bit_length() - 1)]


def blocks_over_dp(value):
    count = lax.axis_size("dp")
    found = {0: value}
    for far in range(2, count, 2):
        found[far] = swap(value, "dp", far)
    for far in range(0, count, 2):
        found[far ^ 1] = swap(found[far], "dp", 1)
    return [found[r] for r in range(count)]


def blocks_over_expert(value):
    count = lax.axis_size("expert")
    found = {0: value}
    for far in range(2, count, 2):
        found[far] = swap(value, "expert", far)
    for far in range(0, count, 2):
        found[far ^ 1] = swap(found[far], "expert", 1)
    return [found[r] for r in range(count)]


def in_order(blocks, axis):
    me = lax.axis_index(axis)
    rows = blocks[0].shape[0]
    whole = jnp.zeros((rows * len(blocks),) + blocks[0].shape[1:], blocks[0].dtype)
    for r, block in enumerate(blocks):
        whole = lax.dynamic_update_slice_in_dim(whole, block, (me ^ r) * rows, 0)
    return whole


def reduce_scatter(value, axis, order):
    count = lax.axis_size(axis)
    me = lax.axis_index(axis)
    left = sorted(order, reverse=True)
    rest = (value.shape[0] // count,) + value.shape[1:]
    current = value.reshape((2,) * len(left) + rest)
    for bit in order:
        place = left.index(bit)
        left.remove(bit)
        mine = (me // bit) % 2
        keep = lax.dynamic_index_in_dim(current, mine, place, keepdims=False)
        send = lax.dynamic_index_in_dim(current, 1 - mine, place, keepdims=False)
        arrived = swap(send.astype(BF16), axis, bit)
        current = keep.astype(F32) + arrived.astype(F32)
        if left:
            current = current.astype(BF16)
    return current


def own_rows(value, axis, count):
    return lax.dynamic_slice_in_dim(value, lax.axis_index(axis) * count, count, 0)


def rows_to_owners(value):
    count = lax.axis_size("expert")
    me = lax.axis_index("expert")
    parts = value.reshape((count, value.shape[0] // count) + value.shape[1:])
    found = []
    for r in range(count):
        part = lax.dynamic_index_in_dim(parts, me ^ r, 0, keepdims=False)
        found.append((swap(part, "expert", r) if r else part)[None])
    return in_order(found, "expert")


def normalize(values, gain_vector):
    factor = lax.rsqrt(jnp.mean(values * values, -1, keepdims=True) + 1e-06)
    normal_part = values * factor
    return (normal_part * gain_vector, normal_part, factor)


def normalize_back(grad_normed, normal_part, factor, gain_vector):
    grad_unit = grad_normed * gain_vector
    return factor * (
        grad_unit - normal_part * jnp.mean(grad_unit * normal_part, -1, keepdims=True)
    )


def rotary_tables(count):
    halfway = HEAD_DIM // 2
    frequency = jnp.power(10000.0, -jnp.arange(halfway, dtype=F32) / halfway)
    angles = jnp.arange(count, dtype=F32)[:, None] * frequency[None, :]
    return (jnp.cos(angles), jnp.sin(angles))


def rotate(values, cosines, sines, direction):
    halfway = cosines.shape[1]
    first_half = values[..., :halfway]
    second_half = values[..., halfway:]
    cos_part = cosines[:, None, :]
    sin_part = sines[:, None, :] * direction
    return jnp.concatenate(
        [
            first_half * cos_part - second_half * sin_part,
            second_half * cos_part + first_half * sin_part,
        ],
        -1,
    )


def allowed_keys(length, starts):
    pos = jnp.arange(length, dtype=jnp.int32)
    inside = (pos[:, None] >= starts[None, :]) & (pos[:, None] < starts[None, :] + PIECE)
    same_piece = jnp.any(inside[:, None, :] & inside[None, :, :], -1)
    return (pos[None, :] <= pos[:, None]) | same_piece


def dot(left, right, spec):
    return jnp.einsum(spec, left, right, preferred_element_type=F32)


def gated_units(rows, cotangents, gate_matrix, up_matrix, down_matrix, scale):
    gate_pre = dot(rows, gate_matrix, "td,df->tf")
    up_pre = dot(rows, up_matrix, "td,df->tf")
    logistic = jax.nn.sigmoid(gate_pre)
    swish = gate_pre * logistic
    slope = logistic * (1.0 + gate_pre * (1.0 - logistic))
    hidden = swish * up_pre
    scaled = (hidden * scale).astype(BF16)
    result = dot(scaled, down_matrix, "tf,fd->td")
    raw = dot(cotangents, down_matrix, "td,fd->tf")
    grad_scale = jnp.sum(hidden * raw, -1)
    raw = raw * scale
    grad_gate_pre = (raw * up_pre * slope).astype(BF16)
    grad_up_pre = (raw * swish).astype(BF16)
    grad_down = dot(scaled, cotangents, "tf,td->fd").astype(BF16)
    grad_gate = dot(rows, grad_gate_pre, "td,tf->df").astype(BF16)
    grad_up = dot(rows, grad_up_pre, "td,tf->df").astype(BF16)
    grad_rows = dot(grad_gate_pre, gate_matrix, "tf,df->td") + dot(
        grad_up_pre, up_matrix, "tf,df->td"
    )
    return result, grad_rows, grad_scale, grad_gate, grad_up, grad_down


def shards(
    inputs,
    norm1_gain,
    qkv_weight,
    out_weight,
    norm2_gain,
    router_weight,
    shared_gate,
    shared_up,
    shared_down,
    expert_gate,
    expert_up,
    expert_down,
    expert_ids,
    piece_starts,
    cotangent,
):
    tokens, width = inputs.shape[1:]
    heads = width // HEAD_DIM
    experts = lax.axis_size("expert")
    copies = lax.axis_size("dp")
    me = lax.axis_index("expert")
    length = tokens * experts
    slab = width // copies
    own_heads = -(-heads // experts)
    columns = own_heads * HEAD_DIM
    padded = experts * columns
    starts = piece_starts[0]

    def head_columns(weight):
        weight = jnp.pad(weight, ((0, 0), (0, padded - width)))
        return lax.dynamic_slice_in_dim(weight, me * columns, columns, 1)

    qkv_slab = jnp.concatenate(
        [head_columns(qkv_weight[:, i * width : (i + 1) * width]) for i in range(3)], 1
    )
    qkv_own = in_order(blocks_over_dp(qkv_slab), "dp")
    units = shared_down.shape[0] // experts

    def unit_columns(weight):
        split = weight.reshape(slab, copies, experts, units)
        return lax.dynamic_index_in_dim(split, me, 2, keepdims=False).reshape(slab, copies * units)

    gains = in_order(blocks_over_dp(jnp.stack([norm1_gain, norm2_gain], 1)), "dp").astype(F32)
    gain1, gain2 = gains[:, 0], gains[:, 1]
    x_all = in_order(blocks_over_expert(inputs[0]), "expert").astype(F32)
    router = in_order(blocks_over_dp(router_weight), "dp")
    out_matrix = in_order(blocks_over_dp(out_weight), "dp")
    shared_in = in_order(
        blocks_over_dp(jnp.concatenate([unit_columns(shared_gate), unit_columns(shared_up)], 1)),
        "dp",
    )
    shared_out = in_order(
        blocks_over_dp(lax.dynamic_slice_in_dim(shared_down, me * units, units, 0)), "dp"
    )
    dy_all = in_order(blocks_over_expert(cotangent[0]), "expert")
    named = jnp.any(
        expert_ids[0][:, :, None] == jnp.arange(experts, dtype=jnp.int32)[None, None, :], 1
    ).astype(BF16)
    named_all = in_order(blocks_over_expert(named), "expert").astype(F32)

    normed1, unit1, factor1 = normalize(x_all, gain1)
    normed1 = normed1.astype(BF16)
    projected = dot(normed1, qkv_own, "td,de->te")
    cosines, sines = rotary_tables(length)
    queries, keys = (
        rotate(projected[:, i * columns : (i + 1) * columns].reshape(length, own_heads, HEAD_DIM), cosines, sines, 1.0).astype(BF16)
        for i in range(2)
    )
    values = projected[:, 2 * columns :].astype(BF16).reshape(length, own_heads, HEAD_DIM)
    root = HEAD_DIM ** (-0.5)
    mask = allowed_keys(length, starts)[None]
    scores = jnp.where(mask, dot(queries, keys, "qhd,khd->hqk") * root, -1e30)
    highest = jnp.max(scores, -1, keepdims=True)
    powers = jnp.exp(scores - highest)
    probs = powers / jnp.sum(powers, -1, keepdims=True)
    weights = probs.astype(BF16)
    mixed = dot(weights, values, "hqk,khd->qhd").astype(BF16).reshape(length, columns)
    mixed_all = in_order([b[None] for b in blocks_over_expert(mixed)], "expert")
    mixed_all = jnp.swapaxes(mixed_all, 0, 1).reshape(length, padded)[:, :width]

    resid2 = x_all + dot(mixed_all, out_matrix, "te,ed->td")
    normed2, unit2, factor2 = normalize(resid2, gain2)
    normed2 = normed2.astype(BF16)
    logits = dot(normed2, router, "td,de->te")
    masked = jnp.where(named_all > 0, logits, -1e30)
    powers = named_all * jnp.exp(masked - jnp.max(masked, -1, keepdims=True))
    gates = powers / jnp.sum(powers, -1, keepdims=True)
    scale = lax.dynamic_slice_in_dim(gates, me, 1, 1)
    middle = shared_in.shape[1] // 2
    (y_s, gx_s, _, shared_gate_grad, shared_up_grad, shared_down_grad) = gated_units(
        normed2, dy_all, shared_in[:, :middle], shared_in[:, middle:], shared_out, 1.0
    )
    (y_e, gx_e, grad_scale, gate_grad, up_grad, down_grad) = gated_units(
        normed2, dy_all, expert_gate[0], expert_up[0], expert_down[0], scale
    )
    expert_bits = bits_of(experts)
    dp_bits = bits_of(copies)
    other_bits = dp_bits[1:2] + dp_bits[:1] + dp_bits[2:]
    gx = reduce_scatter((gx_s + gx_e).astype(BF16), "expert", expert_bits)
    y = reduce_scatter((y_s + y_e).astype(BF16), "expert", expert_bits)
    resid2_home = own_rows(resid2, "expert", tokens)
    outputs = (resid2_home + y).astype(BF16)

    grad_gates = own_rows(
        in_order([b[None] for b in blocks_over_expert(grad_scale)], "expert").T, "expert", tokens
    )
    gates_home = own_rows(gates, "expert", tokens)
    normed2_home = own_rows(normed2, "expert", tokens)
    grad_logits = (
        gates_home * (grad_gates - jnp.sum(gates_home * grad_gates, -1, keepdims=True))
    ).astype(BF16)
    router_grad = dot(normed2_home, grad_logits, "td,te->de")
    grad_normed2 = gx + dot(grad_logits, router, "te,de->td")
    unit2_home = own_rows(unit2, "expert", tokens)
    gain2_grad = jnp.sum(grad_normed2 * unit2_home, 0)
    grad_resid2 = cotangent[0].astype(F32) + normalize_back(
        grad_normed2, unit2_home, own_rows(factor2, "expert", tokens), gain2
    )
    grad_attended = in_order(blocks_over_expert(grad_resid2.astype(BF16)), "expert")

    out_grad = dot(mixed_all, grad_attended, "te,td->ed").astype(BF16)
    share = slab // experts
    out_grad = lax.dynamic_index_in_dim(
        out_grad.reshape(copies, experts, share, width), me, 1, keepdims=False
    )
    out_padded = jnp.pad(out_matrix, ((0, padded - width), (0, 0)))
    grad_mixed = dot(grad_attended, own_rows(out_padded, "expert", columns), "td,ed->te")
    grad_mixed = grad_mixed.astype(BF16).reshape(length, own_heads, HEAD_DIM)
    grad_probs = dot(grad_mixed, values, "qhd,khd->hqk")
    delta = jnp.sum(probs * grad_probs, -1, keepdims=True)
    grad_scores = (probs * (grad_probs - delta)).astype(BF16)
    grad_queries = dot(grad_scores, keys, "hqk,khd->qhd") * root
    grad_keys = dot(grad_scores, queries, "hqk,qhd->khd") * root
    grad_values = dot(weights, grad_mixed, "hqk,qhd->khd")
    grad_projected = jnp.concatenate(
        [
            rotate(grad_queries, cosines, sines, -1.0).reshape(length, columns),
            rotate(grad_keys, cosines, sines, -1.0).reshape(length, columns),
            grad_values.reshape(length, columns),
        ],
        1,
    ).astype(BF16)
    qkv_grad = dot(normed1, grad_projected, "td,te->de")
    grad_normed1 = dot(grad_projected, qkv_own, "te,de->td")
    gain1_grad = jnp.sum(grad_normed1 * unit1, 0)
    gn1 = reduce_scatter(grad_normed1.astype(BF16), "expert", expert_bits)
    grad_from_norm1 = normalize_back(
        gn1, own_rows(unit1, "expert", tokens), own_rows(factor1, "expert", tokens), gain1
    )
    input_grad = (grad_resid2 + grad_from_norm1).astype(BF16)

    extras = jnp.concatenate([gain1_grad[:, None], gain2_grad[:, None], router_grad], 1)
    last_grad = jnp.concatenate([qkv_grad, extras], 1).astype(BF16)
    shared_grad = jnp.concatenate([shared_gate_grad, shared_up_grad], 1)
    shared_grad = reduce_scatter(shared_grad, "dp", dp_bits)
    sdown_grad = reduce_scatter(shared_down_grad, "dp", dp_bits)
    gate_grad = reduce_scatter(gate_grad, "dp", dp_bits)
    up_grad = reduce_scatter(up_grad, "dp", other_bits)
    down_grad = reduce_scatter(down_grad, "dp", dp_bits)
    out_grad = reduce_scatter(out_grad.reshape(copies * share, width), "dp", dp_bits)
    last_grad = reduce_scatter(last_grad, "dp", other_bits)

    shared_pieces = rows_to_owners(shared_grad.astype(BF16)).astype(F32)
    shared_pieces = shared_pieces.reshape(experts, share, 2, copies, units)
    shared_pieces = shared_pieces.transpose(2, 1, 3, 0, 4).reshape(2, share, copies * experts * units)
    last_pieces = rows_to_owners(last_grad.astype(BF16)).astype(F32)
    qkv_pieces = last_pieces[:, :, : 3 * columns].reshape(experts, share, 3, columns)
    qkv_pieces = qkv_pieces.transpose(1, 2, 0, 3).reshape(share, 3, padded)[:, :, :width]
    extra_pieces = jnp.sum(last_pieces[:, :, 3 * columns :], 0)
    return (
        outputs[None],
        input_grad[None],
        extra_pieces[:, 0],
        qkv_pieces.reshape(share, 3 * width),
        out_grad,
        extra_pieces[:, 1],
        extra_pieces[:, 2:],
        shared_pieces[0],
        shared_pieces[1],
        sdown_grad,
        gate_grad[None],
        up_grad[None],
        down_grad[None],
    )


def solution(mesh):
    return jax.shard_map(
        shards,
        mesh=mesh,
        in_specs=(
            P("dp", "expert", None),
            P("dp"),
            P("dp", None),
            P("dp", None),
            P("dp"),
            P("dp", None),
            P("dp", None),
            P("dp", None),
            P("dp", None),
            P("expert", None, None),
            P("expert", None, None),
            P("expert", None, None),
            P("dp", "expert", None),
            P("dp", None),
            P("dp", "expert", None),
        ),
        out_specs=(
            P("dp", "expert", None),
            P("dp", "expert", None),
            P(("dp", "expert")),
            P(("dp", "expert"), None),
            P(("dp", "expert"), None),
            P(("dp", "expert")),
            P(("dp", "expert"), None),
            P(("dp", "expert"), None),
            P(("dp", "expert"), None),
            P(("dp", "expert"), None),
            P("expert", "dp", None),
            P("expert", "dp", None),
            P("expert", "dp", None),
        ),
        check_vma=False,
    )
```

```python
import functools

import jax
import jax.numpy as jnp
import numpy as np
from jax import lax
from jax.experimental import pallas as pl
from jax.experimental.pallas import tpu as pltpu
from jax.sharding import PartitionSpec as P

HEAD_DIM = 64
PIECE = 256
F32 = jnp.float32
BF16 = jnp.bfloat16
LANES = 128
SLOTS = 8
MIB = 1 << 20
VMEM = pl.BlockSpec(memory_space=pltpu.VMEM)
SMEM = pl.BlockSpec(memory_space=pltpu.SMEM)
ANY = pl.BlockSpec(memory_space=pl.ANY)


def swap(value, axis, distance):
    count = lax.axis_size(axis)
    return lax.ppermute(value, axis, [(i, i ^ distance) for i in range(count)])


def after(value, *others):
    return lax.optimization_barrier((value, *others))[0]


def bits_of(count):
    return [1 << k for k in range(count.bit_length() - 1)]


def far_blocks(axis, value):
    return {r: swap(value, axis, r) if r else value for r in range(0, lax.axis_size(axis), 2)}


def near_blocks(axis, found):
    every = dict(found)
    for r in found:
        every[r ^ 1] = swap(found[r], axis, 1)
    return [every[r] for r in range(lax.axis_size(axis))]


def in_order(blocks, axis):
    me = lax.axis_index(axis)
    rows = blocks[0].shape[0]
    whole = jnp.zeros((rows * len(blocks),) + blocks[0].shape[1:], blocks[0].dtype)
    for r, block in enumerate(blocks):
        whole = lax.dynamic_update_slice_in_dim(whole, block, (me ^ r) * rows, 0)
    return whole


def halves(order):
    rest = order[1:]
    found = []
    for r in range(2 << len(rest)):
        place = sum(((r & bit) != 0) << (len(rest) - 1 - i) for i, bit in enumerate(rest))
        found.append((r, bool(r & order[0]), place))
    return found


def order_over(count, first):
    return [first] + [bit for bit in bits_of(count) if bit != first]


class Halving:
    def __init__(self, keep, send, axis, order):
        self.axis = axis
        self.order = order[1:]
        self.count = keep.shape[0]
        self.terms = [keep, swap(send, axis, order[0])]

    def wait(self, *others):
        self.terms[-1] = after(self.terms[-1], *others)
        return self

    def exchange(self):
        half = self.count // 2
        sent = sum(term[half : self.count].astype(F32) for term in self.terms).astype(BF16)
        self.terms.append(swap(sent, self.axis, self.order.pop(0)))
        self.count = half
        return sent

    def rest(self):
        while self.order:
            self.exchange()
        return self.terms


def added(terms):
    return sum(term[0].astype(F32) for term in terms)


def dot(left, right):
    return lax.dot_general(left, right, (((1,), (0,)), ((), ())), preferred_element_type=F32)


def dot_t(left, right):
    return lax.dot_general(left, right, (((1,), (1,)), ((), ())), preferred_element_type=F32)


def t_dot(left, right):
    return lax.dot_general(left, right, (((0,), (0,)), ((), ())), preferred_element_type=F32)


def local(body, outs, scratch=(), scalars=1):
    def call(*args):
        return pl.pallas_call(
            body,
            out_shape=[jax.ShapeDtypeStruct(shape, kind) for shape, kind in outs],
            in_specs=[SMEM] * scalars + [VMEM] * (len(args) - scalars),
            out_specs=[VMEM] * len(outs),
            scratch_shapes=[pltpu.VMEM(shape, kind) for shape, kind in scratch],
            compiler_params=pltpu.CompilerParams(vmem_limit_bytes=60 * MIB),
            cost_estimate=pl.CostEstimate(flops=10**8, bytes_accessed=10**5, transcendentals=0),
        )(*args)

    return call


def moving(body, outs, scratch, copies, scalars=1):
    def call(*args):
        return pl.pallas_call(
            body,
            out_shape=[jax.ShapeDtypeStruct(shape, kind) for shape, kind in outs],
            in_specs=[SMEM] * scalars + [ANY] * (len(args) - scalars),
            out_specs=[ANY] * len(outs),
            scratch_shapes=[pltpu.VMEM(shape, kind) for shape, kind in scratch]
            + [pltpu.SemaphoreType.DMA((copies,))],
            compiler_params=pltpu.CompilerParams(vmem_limit_bytes=60 * MIB),
            cost_estimate=pl.CostEstimate(flops=10**8, bytes_accessed=10**5, transcendentals=0),
        )(*args)

    return call


def mixed_kernel(body, outs, scratch, copies, scalars=1):
    def call(*args):
        return pl.pallas_call(
            body,
            out_shape=[jax.ShapeDtypeStruct(shape, kind) for shape, kind in outs],
            in_specs=[SMEM] * scalars + [ANY] * (len(args) - scalars),
            out_specs=[VMEM] * len(outs),
            scratch_shapes=[pltpu.VMEM(shape, kind) for shape, kind in scratch]
            + [pltpu.SemaphoreType.DMA((copies,))],
            compiler_params=pltpu.CompilerParams(vmem_limit_bytes=60 * MIB),
            cost_estimate=pl.CostEstimate(flops=10**8, bytes_accessed=10**5, transcendentals=0),
        )(*args)

    return call


class Moves:
    def __init__(self, sems):
        self.sems = sems
        self.used = 0
        self.open = []

    def start(self, source, target):
        move = pltpu.make_async_copy(source, target, self.sems.at[self.used])
        self.used += 1
        move.start()
        self.open.append(move)
        return move

    def wait(self, *moves):
        for move in moves:
            move.wait()
            self.open = [other for other in self.open if other is not move]

    def finish(self):
        self.wait(*list(self.open))


def rows_at(place, count):
    return pl.ds(pl.multiple_of(place * count, count), count)


def normal(values):
    factor = lax.rsqrt(jnp.mean(values * values, -1, keepdims=True) + 1e-06)
    return values * factor, factor


def normal_back(grad_normed, unit, factor, gain):
    grad_unit = grad_normed * gain
    return factor * (grad_unit - unit * jnp.mean(grad_unit * unit, -1, keepdims=True))


def turned(pairs, cosines, sines):
    span = pairs.shape[1]
    lane = lax.broadcasted_iota(jnp.int32, pairs.shape, 1)
    first = lane % HEAD_DIM < HEAD_DIM // 2
    partner = jnp.where(
        first, pltpu.roll(pairs, span - HEAD_DIM // 2, 1), pltpu.roll(pairs, HEAD_DIM // 2, 1)
    )
    return pairs * cosines + partner * sines


def rotary_tables(count):
    halfway = HEAD_DIM // 2
    frequency = np.power(10000.0, -np.arange(halfway, dtype=np.float32) / halfway)
    angles = np.arange(count, dtype=np.float32)[:, None] * frequency.astype(np.float32)[None, :]
    cosines, sines = np.cos(angles), np.sin(angles)
    cosines = np.tile(cosines, (1, 4)).astype(np.float32)
    sines = np.concatenate([-sines, sines, -sines, sines], 1).astype(np.float32)
    return jnp.asarray(cosines), jnp.asarray(sines)


def widened(table, span):
    return jnp.concatenate([table] * (span // LANES), 1)


def reach(block, experts, tokens):
    return min(block + 2, experts) * tokens


def pack_first_body(experts, where, gain1, gain2, router, qkv, result, wide):
    slab, width = result.shape[0], qkv.shape[1] // 3
    columns = (result.shape[1] - LANES) // 3
    wide[...] = jnp.zeros_like(wide)
    wide[0:1, :slab] = gain1[...].astype(F32)
    wide[1:2, :slab] = gain2[...].astype(F32)
    wide[SLOTS : SLOTS + router.shape[0], :slab] = router[...].astype(F32)
    result[:, :LANES] = wide[...].T[:slab, :].astype(BF16)
    for e in range(experts):

        @pl.when(where[0] == e)
        def _():
            for i in range(3):
                start = min(e * columns, width)
                stop = min(start + columns, width)
                at = LANES + i * columns
                if stop > start:
                    result[:, at : at + stop - start] = qkv[:, i * width + start : i * width + stop]
                if stop - start < columns:
                    blank = jnp.zeros((slab, columns - stop + start), BF16)
                    result[:, at + stop - start : at + columns] = blank


def pack_units_body(experts, copies, where, gate, up, down, result):
    slab, width = gate.shape[0], down.shape[1]
    units = down.shape[0] // experts
    total = copies * units
    for e in range(experts):

        @pl.when(where[0] == e)
        def _():
            for k, matrix in enumerate((gate, up)):
                parts = [
                    matrix[:, (d * experts + e) * units : (d * experts + e + 1) * units]
                    for d in range(copies)
                ]
                result[:slab, k * total : (k + 1) * total] = jnp.concatenate(parts, 1)
            result[slab:, :width] = down[e * units : (e + 1) * units, :]
            if result.shape[1] > width:
                result[slab:, width:] = jnp.zeros((units, result.shape[1] - width), BF16)


def attend_body(experts, copies, blocks, *refs):
    where, starts, cosine_in, sine_in = refs[:4]
    x_refs, w_refs = refs[4 : 4 + experts], refs[4 + experts : 4 + experts + blocks]
    refs = refs[4 + experts + blocks :]
    n1_out, q_out, k_out, v_out, probs_out, mixed_out, weight_out, vectors_out = refs[:8]
    cosine_table, sine_table, x, n1, q, k, v, probs, mixed, weight, vectors, sems = refs[8:]
    moves = Moves(sems)
    me, place = where[0], where[1]
    tokens = x_refs[0].shape[0]
    columns = q.shape[1]
    own_heads = columns // HEAD_DIM
    slab = w_refs[0].shape[0]
    if blocks == 1:
        arriving = [moves.start(w_refs[0], weight)]
    else:
        arriving = [
            moves.start(w_refs[r], weight.at[rows_at(place ^ r, slab), :]) for r in range(blocks)
        ]
    tables = [moves.start(cosine_in, cosine_table), moves.start(sine_in, sine_table)]
    rows_in = [moves.start(x_refs[r], x.at[r]) for r in range(experts)]
    moves.wait(*arriving)
    vectors[...] = weight[:, :LANES].astype(F32).T
    moves.start(weight, weight_out)
    moves.start(vectors, vectors_out)
    gain = vectors[0:1, :]
    moves.wait(*tables)
    for r in range(experts):
        rows = rows_at(me ^ r, tokens)
        moves.wait(rows_in[r])
        unit, _ = normal(x[r].astype(F32))
        normed = (unit * gain).astype(BF16)
        n1[rows, :] = normed
        projected = dot(normed, weight[:, LANES:])
        cosines = widened(cosine_table[rows, :], 2 * columns)
        sines = widened(sine_table[rows, :], 2 * columns)
        pair = turned(projected[:, : 2 * columns], cosines, sines).astype(BF16)
        q[rows, :] = pair[:, :columns] * HEAD_DIM ** (-0.5)
        k[rows, :] = pair[:, columns:]
        v[rows, :] = projected[:, 2 * columns :].astype(BF16)
    for held, result in ((n1, n1_out), (q, q_out), (k, k_out), (v, v_out)):
        moves.start(held, result)
    pieces = starts.shape[1]
    leaving = {}
    for block in range(experts):
        seen = reach(block, experts, tokens)
        rows = slice(block * tokens, (block + 1) * tokens)
        query_pos = block * tokens + lax.broadcasted_iota(jnp.int32, (tokens, 1), 0)
        key_pos = lax.broadcasted_iota(jnp.int32, (1, seen), 1)
        query_piece = jnp.full((tokens, 1), -1, jnp.int32)
        key_piece = jnp.full((1, seen), -2, jnp.int32)
        for j in range(pieces):
            start = starts[0, j]
            query_piece = jnp.where(
                (query_pos >= start) & (query_pos < start + PIECE), j, query_piece
            )
            key_piece = jnp.where((key_pos >= start) & (key_pos < start + PIECE), j, key_piece)
        bias = jnp.where((key_pos <= query_pos) | (query_piece == key_piece), 0.0, -1e30)
        slot = block % 2
        if block >= 2:
            moves.wait(leaving[block - 2])
        for h in range(own_heads):
            head = slice(h * HEAD_DIM, (h + 1) * HEAD_DIM)
            scores = dot_t(q[rows, head], k[:seen, head]) + bias
            powers = jnp.exp(scores - jnp.max(scores, -1, keepdims=True))
            share = (powers * (1.0 / jnp.sum(powers, -1, keepdims=True))).astype(BF16)
            probs[slot, h, :, :seen] = share
            mixed[rows, head] = dot(share, v[:seen, head]).astype(BF16)
        leaving[block] = moves.start(
            probs.at[slot, :, :, :seen], probs_out.at[:, rows, :seen]
        )
    moves.start(mixed, mixed_out)
    moves.finish()


def settle_body(experts, *refs):
    where, vectors_in = refs[:2]
    x_refs = refs[2 : 2 + experts]
    dy_refs = refs[2 + experts : 2 + 2 * experts]
    m_refs = refs[2 + 2 * experts : 2 + 3 * experts]
    matrix_in = refs[2 + 3 * experts]
    refs = refs[3 + 3 * experts :]
    n2_out, n2_turned_out, dy_out, gates_out, own_resid_out, own_n2_out, own_gates_out = refs[:7]
    vectors, x, dy, mixed, out_matrix, n2, n2_turned, gates, own_resid, sems = refs[7:]
    moves = Moves(sems)
    me = where[0]
    tokens, width = x_refs[0].shape
    columns = m_refs[0].shape[1]
    mixed_in = [moves.start(m_refs[j], mixed.at[j]) for j in range(experts)]
    vectors_move = moves.start(vectors_in, vectors)
    x_in = [moves.start(x_refs[r], x.at[r]) for r in range(experts)]
    dy_in = [moves.start(dy_refs[r], dy.at[r]) for r in range(experts)]
    moves.wait(moves.start(matrix_in, out_matrix), *mixed_in, vectors_move)
    gain = vectors[1:2, :]
    router = vectors[SLOTS : 2 * SLOTS, :].astype(BF16)
    for r in range(experts):
        rows = rows_at(me ^ r, tokens)
        moves.wait(x_in[r], dy_in[r])
        moves.start(dy.at[r, :, :width], dy_out.at[rows, :])
        resid = x[r].astype(F32)
        for j in range(experts):
            resid += dot(mixed[j, rows, :], out_matrix[rows_at(me ^ j, columns), :])
        unit, _ = normal(resid)
        normed = (unit * gain).astype(BF16)
        logits = dot_t(normed, router)
        chosen = dy[r, :, width : width + SLOTS].astype(F32)
        masked = jnp.where(chosen > 0.0, logits, -1e30)
        powers = chosen * jnp.exp(masked - jnp.max(masked, -1, keepdims=True))
        n2[r] = normed
        n2_turned[r] = normed.astype(F32).T.astype(BF16)
        gates[r] = powers / jnp.sum(powers, -1, keepdims=True)
        moves.start(n2.at[r], n2_out.at[rows, :])
        moves.start(n2_turned.at[r], n2_turned_out.at[:, rows])
        moves.start(gates.at[r], gates_out.at[rows, :])
        if r == 0:
            own_resid[...] = resid
            moves.start(own_resid, own_resid_out)
            moves.start(n2.at[0], own_n2_out)
            moves.start(gates.at[0], own_gates_out)
    moves.finish()


def unit_tile(me, fresh, n2, dy, gates, wg, wu, wd, y, gx, gg, hidden_s, gate_s, up_s):
    chunk = 512 if n2.shape[0] <= 1024 else 256

    def step(c, carry):
        rows = pl.ds(pl.multiple_of(c * chunk, chunk), chunk)
        x, g = n2[rows, :], dy[rows, :]
        gate_pre = dot(x, wg[...])
        up_pre = dot(x, wu[...])
        raw = dot_t(g, wd[...])
        logistic = lax.logistic(gate_pre)
        swish = gate_pre * logistic
        slope = logistic + swish * (1.0 - logistic)
        hidden = swish * up_pre
        if gates is not None:
            lane = lax.broadcasted_iota(jnp.int32, (chunk, SLOTS), 1)
            scale = jnp.sum(jnp.where(lane == me, gates[rows, :], 0.0), -1, keepdims=True)
            gg[rows, :] += jnp.sum(hidden * raw, -1, keepdims=True)
            hidden = hidden * scale
            raw = raw * scale
        hidden = hidden.astype(BF16)
        grad_gate = (raw * up_pre * slope).astype(BF16)
        grad_up = (raw * swish).astype(BF16)
        hidden_s[rows, :] = hidden
        gate_s[rows, :] = grad_gate
        up_s[rows, :] = grad_up
        out = dot(hidden, wd[...])
        back = dot_t(grad_gate, wg[...]) + dot_t(grad_up, wu[...])
        if fresh:
            y[rows, :] = out
            gx[rows, :] = back
        else:
            y[rows, :] += out
            gx[rows, :] += back
        return carry

    lax.fori_loop(0, n2.shape[0] // chunk, step, 0)


def shared_body(copies, blocks, *refs):
    where, n2_in, n2_turned_in, dy_in, y_in, gx_in = refs[:6]
    b_refs = refs[6 : 6 + blocks]
    keep_out, send_out, y_out, gx_out = refs[6 + blocks : 10 + blocks]
    n2, n2_turned, dy, y, gx, y_more, gx_more, wg, wu, wd = refs[10 + blocks : 20 + blocks]
    hidden_s, gate_s, up_s, grad_gate, grad_up, grad_down, keep, send, sems = refs[20 + blocks :]
    moves = Moves(sems)
    place = where[1]
    width = n2.shape[1]
    total = wg.shape[1]
    units = total // copies
    slab = width // copies
    if blocks == 2:
        places = [
            (b_refs[0].at[:, :total], wg),
            (b_refs[0].at[:, total : 2 * total], wu),
            (b_refs[1], wd),
        ]
    else:
        places = []
        for r in range(copies):
            rows = slice(r * slab, (r + 1) * slab)
            places.append((b_refs[0].at[r, :slab, :total], wg.at[rows, :]))
            places.append((b_refs[0].at[r, :slab, total : 2 * total], wu.at[rows, :]))
            rows = slice(r * units, (r + 1) * units)
            places.append((b_refs[0].at[r, slab:, :width], wd.at[rows, :]))
    arriving = [moves.start(source, target) for source, target in places]
    arriving += [moves.start(n2_in, n2), moves.start(dy_in, dy)]
    moves.wait(*arriving)
    sums_in = [moves.start(y_in, y_more), moves.start(gx_in, gx_more)]
    turned_in = moves.start(n2_turned_in, n2_turned)
    unit_tile(None, True, n2, dy, None, wg, wu, wd, y, gx, None, hidden_s, gate_s, up_s)
    moves.wait(*sums_in)
    y[...] += y_more[...]
    gx[...] += gx_more[...]
    moves.start(y, y_out)
    moves.start(gx, gx_out)
    moves.wait(turned_in)
    grad_gate[...] = dot(n2_turned[...], gate_s[...])
    grad_up[...] = dot(n2_turned[...], up_s[...])
    grad_down[...] = t_dot(hidden_s[...], dy[...])
    for r, leaves, k in halves(order_over(copies, 2)):
        half = send if leaves else keep
        rows = rows_at(place ^ r, slab)
        half[k, :slab, :total] = grad_gate[rows, :].astype(BF16)
        half[k, :slab, total : 2 * total] = grad_up[rows, :].astype(BF16)
        half[k, slab:, :width] = grad_down[rows_at(place ^ r, units), :].astype(BF16)
        spare = half.shape[2] - width
        if spare:
            half[k, slab:, width:] = jnp.zeros((units, spare), BF16)
        spare = half.shape[2] - 2 * total
        if spare:
            half[k, :slab, 2 * total :] = jnp.zeros((slab, spare), BF16)
    moves.start(send, send_out)
    moves.start(keep, keep_out)
    moves.finish()


def expert_body(experts, copies, last, *refs):
    where, n2_in, n2_turned_in, dy_in, gates_in, wg_in, wu_in, wd_in = refs[:8]
    refs = refs[8:]
    if last:
        y_in, gx_in, gg_in, down_in = refs[:4]
        keep_out, send_out, down_keep_out, down_send_out = refs[4:8]
        y_keep_out, y_send_out, gx_keep_out, gx_send_out = refs[8:12]
        refs = refs[12:]
    else:
        keep_out, send_out, y_out, gx_out, gg_out, down_out = refs[:6]
        refs = refs[6:]
    n2, n2_turned, dy, gates, y, gx, gg, down, wg, wu, wd = refs[:11]
    hidden_s, gate_s, up_s, grad_gate, grad_up, keep, send = refs[11:18]
    if last:
        down_keep, down_send, y_keep, y_send, gx_keep, gx_send, gg_more = refs[18:25]
        gx_more, y_more = refs[25], refs[-2]
    moves = Moves(refs[-1])
    me, place = where[0], where[1]
    slab = keep.shape[2]
    tile = wg.shape[2]
    hidden = wd_in.shape[0]
    steps = hidden // 2 // tile
    first = hidden // 2 if last else 0
    units = [slice(first + s * tile, first + (s + 1) * tile) for s in range(steps)]

    def fetch(step):
        slot = step % 2
        return [
            moves.start(wg_in.at[:, units[step]], wg.at[slot]),
            moves.start(wu_in.at[:, units[step]], wu.at[slot]),
            moves.start(wd_in.at[units[step], :], wd.at[slot]),
        ]

    weights = {0: fetch(0)}
    arriving = [moves.start(n2_in, n2), moves.start(dy_in, dy), moves.start(gates_in, gates)]
    gg[...] = jnp.zeros_like(gg)
    moves.wait(*arriving)
    turned_in = [moves.start(n2_turned_in, n2_turned)]
    weights[1] = fetch(1)
    if last:
        sums_in = [moves.start(gx_in, gx_more), moves.start(gg_in, gg_more)]
        roomy = y_more is not gx_more
        if roomy:
            sums_in.append(moves.start(y_in, y_more))
        earlier = moves.start(down_in, down.at[: hidden // 2, :])
    leaving = {}
    for step in range(steps):
        slot = step % 2
        moves.wait(*weights[step])
        unit_tile(
            me, step == 0, n2, dy, gates, wg.at[slot], wu.at[slot], wd.at[slot],
            y, gx, gg, hidden_s, gate_s, up_s,
        )
        if 1 <= step and step + 1 < steps:
            weights[step + 1] = fetch(step + 1)
        elif step == 0 and steps > 2:
            weights[2] = fetch(2)
        if step == steps - 1:
            if last:
                tokens, width = y_keep.shape[1], n2.shape[1]
                moves.wait(*sums_in)
                gg[...] += gg_more[...]
                for r, leaves, k in halves(bits_of(experts)):
                    rows = rows_at(me ^ r, tokens)
                    half = gx_send if leaves else gx_keep
                    half[k, :, :width] = (gx[rows, :] + gx_more[rows, :]).astype(BF16)
                    lane = lax.broadcasted_iota(jnp.int32, (tokens, LANES), 1)
                    whole = gg[rows, :]
                    coarse = whole.astype(BF16).astype(F32)
                    half[k, :, width:] = (
                        jnp.where(lane == me, coarse, 0.0)
                        + jnp.where(lane == me + SLOTS, whole - coarse, 0.0)
                    ).astype(BF16)
                moves.start(gx_send, gx_send_out)
                moves.start(gx_keep, gx_keep_out)
                if not roomy:
                    moves.wait(moves.start(y_in, y_more))
                for r, leaves, k in halves(bits_of(experts)):
                    rows = rows_at(me ^ r, tokens)
                    half = y_send if leaves else y_keep
                    half[k] = (y[rows, :] + y_more[rows, :]).astype(BF16)
                moves.start(y_send, y_send_out)
                moves.start(y_keep, y_keep_out)
            else:
                moves.start(y, y_out)
                moves.start(gx, gx_out)
                moves.start(gg, gg_out)
        moves.wait(*turned_in)
        turned_in = []
        grad_gate[...] = dot(n2_turned[...], gate_s[...])
        grad_up[...] = dot(n2_turned[...], up_s[...])
        down[units[step] if last else slice(step * tile, (step + 1) * tile), :] = t_dot(
            hidden_s[...], dy[...]
        ).astype(BF16)
        if step >= 2:
            moves.wait(*leaving[step - 2])
        for r, leaves, k in halves(order_over(copies, 1)):
            half = send if leaves else keep
            rows = rows_at(place ^ r, slab)
            half[slot, k, :, :tile] = grad_gate[rows, :].astype(BF16)
            half[slot, k, :, tile:] = grad_up[rows, :].astype(BF16)
        at = slice(2 * step * tile, 2 * (step + 1) * tile)
        leaving[step] = [
            moves.start(send.at[slot], send_out.at[:, :, at]),
            moves.start(keep.at[slot], keep_out.at[:, :, at]),
        ]
    if last:
        moves.wait(earlier)
        per = hidden // copies
        for r, leaves, k in halves(order_over(copies, 2)):
            half = down_send if leaves else down_keep
            half[k] = down[rows_at(place ^ r, per), :]
        moves.start(down_send, down_send_out)
        moves.start(down_keep, down_keep_out)
    else:
        moves.start(down, down_out)
    moves.finish()


def home_body(terms, *refs):
    where, vectors = refs[:2]
    parts = refs[2 : 2 + terms]
    own_resid, own_n2, own_gates, cotangent, attended, grad_resid, sums = refs[2 + terms :]
    width = own_n2.shape[1]
    total = added(parts)
    grad_gates = total[:, width : width + SLOTS] + total[:, width + SLOTS : width + 2 * SLOTS]
    gates = own_gates[...]
    grad_logits = (
        gates * (grad_gates - jnp.sum(gates * grad_gates, -1, keepdims=True))
    ).astype(BF16)
    grad_normed = total[:, :width] + dot(
        grad_logits, vectors[SLOTS : 2 * SLOTS, :].astype(BF16)
    )
    unit, factor = normal(own_resid[...])
    sums[0:SLOTS, :] = jnp.broadcast_to(
        jnp.sum(grad_normed * unit, 0, keepdims=True), (SLOTS, width)
    )
    sums[SLOTS : 2 * SLOTS, :] = t_dot(grad_logits, own_n2[...])
    back = cotangent[...].astype(F32) + normal_back(grad_normed, unit, factor, vectors[1:2, :])
    grad_resid[...] = back
    attended[...] = back.astype(BF16)


def grad_share(matrix, start, me, count, experts):
    if count % 8 == 0:
        return matrix[pl.ds(pl.multiple_of(start + me * count, count), count), :]
    rows = matrix[pl.ds(pl.multiple_of(start, 8), count * experts), :]
    picked = rows[:count]
    for e in range(1, experts):
        picked = jnp.where(me == e, rows[e * count : (e + 1) * count], picked)
    return picked


def attend_back_body(experts, copies, *refs):
    where, cosine_in, sine_in, sums_in = refs[:4]
    a_refs = refs[4 : 4 + experts]
    m_refs = refs[4 + experts : 4 + 2 * experts]
    x_refs = refs[4 + 2 * experts : 4 + 3 * experts]
    refs = refs[4 + 3 * experts :]
    matrix_in, q_in, k_in, v_in, n1_in, weight_in, probs_in = refs[:7]
    keep_out, send_out, gn_keep_out, gn_send_out = refs[7:11]
    refs = refs[11:]
    cosine_table, sine_table, sums, attended, mixed, x, out_matrix, q, k, v, n1, weight, probs = refs[:13]
    grad_q, grad_k, grad_v, grad_projected, grad_out, grad_qkv, extra, side = refs[13:21]
    keep, send, gn_keep, gn_send, sems = refs[21:]
    moves = Moves(sems)
    me, place = where[0], where[1]
    tokens, width = x_refs[0].shape
    columns = q.shape[1]
    own_heads = columns // HEAD_DIM
    root = HEAD_DIM ** (-0.5)

    def fetch(block):
        seen = reach(block, experts, tokens)
        rows = slice(block * tokens, (block + 1) * tokens)
        return moves.start(
            probs_in.at[:, rows, :seen], probs.at[block % 2, :, :, :seen]
        )

    needed = [
        moves.start(a_refs[r], attended.at[rows_at(me ^ r, tokens), :]) for r in range(experts)
    ]
    needed += [moves.start(matrix_in, out_matrix)]
    needed += [moves.start(source, held) for source, held in ((v_in, v), (k_in, k), (q_in, q))]
    shares = {0: fetch(0), 1: fetch(1)}
    mixed_in = [moves.start(m_refs[j], mixed.at[j]) for j in range(experts)]
    later = [moves.start(weight_in, weight), moves.start(cosine_in, cosine_table)]
    later += [moves.start(sine_in, sine_table), moves.start(sums_in, sums)]
    x_in = [moves.start(x_refs[r], x.at[r]) for r in range(experts)]
    n1_move = moves.start(n1_in, n1)
    grad_k[...] = jnp.zeros_like(grad_k)
    grad_v[...] = jnp.zeros_like(grad_v)
    moves.wait(*needed)
    own_out = out_matrix[rows_at(me, columns), :]
    for block in range(experts):
        seen = reach(block, experts, tokens)
        rows = slice(block * tokens, (block + 1) * tokens)
        slot = block % 2
        grad_mixed = dot_t(attended[rows, :], own_out).astype(BF16)
        moves.wait(shares[block])
        for h in range(own_heads):
            head = slice(h * HEAD_DIM, (h + 1) * HEAD_DIM)
            gm = grad_mixed[:, head]
            share = probs[slot, h, :, :seen]
            wide = share.astype(F32)
            grad_probs = dot_t(gm, v[:seen, head])
            delta = jnp.sum(wide * grad_probs, -1, keepdims=True)
            grad_scores = (wide * (grad_probs - delta)).astype(BF16)
            grad_q[rows, head] = dot(grad_scores, k[:seen, head]) * root
            grad_k[:seen, head] += t_dot(grad_scores, q[rows, head])
            grad_v[:seen, head] += t_dot(share, gm)
        if block + 2 < experts:
            shares[block + 2] = fetch(block + 2)
    moves.wait(*later)
    gain_sum = jnp.zeros((1, width), F32)
    for r in list(range(1, experts, 2)) + list(range(0, experts, 2)):
        rows = rows_at(me ^ r, tokens)
        pair = jnp.concatenate([grad_q[rows, :], grad_k[rows, :]], 1)
        cosines = widened(cosine_table[rows, :], 2 * columns)
        sines = widened(sine_table[rows, :], 2 * columns)
        back = turned(pair, cosines, -sines).astype(BF16)
        grad_projected[rows, : 2 * columns] = back
        grad_projected[rows, 2 * columns :] = grad_v[rows, :].astype(BF16)
        grad_normed = dot_t(grad_projected[rows, :], weight[:, LANES:])
        moves.wait(x_in[r])
        unit, _ = normal(x[r].astype(F32))
        gain_sum += jnp.sum(grad_normed * unit, 0, keepdims=True)
        _, leaves, spot = halves(bits_of(experts))[r]
        half, result = (gn_send, gn_send_out) if leaves else (gn_keep, gn_keep_out)
        half[spot] = grad_normed.astype(BF16)
        moves.start(half.at[spot], result.at[spot])
    moves.wait(n1_move, *mixed_in)
    for r in range(experts):
        grad_out[rows_at(me ^ r, columns), :] = t_dot(mixed[r], attended[...])
    grad_qkv[...] = t_dot(n1[...], grad_projected[...])
    extra[...] = jnp.zeros_like(extra)
    extra[0:1, :] = gain_sum
    extra[1:2, :] = sums[0:1, :]
    extra[SLOTS : 2 * SLOTS, :] = sums[SLOTS : 2 * SLOTS, :]
    side[...] = extra[...].T
    slab = width // copies
    share_rows = slab // experts
    spare = keep.shape[1] - slab
    for r, leaves, place_of in halves(order_over(copies, 1)):
        half = send if leaves else keep
        rows = rows_at(place ^ r, slab)
        half[place_of, :slab, :LANES] = side[rows, :].astype(BF16)
        half[place_of, :slab, LANES : LANES + 3 * columns] = grad_qkv[rows, :].astype(BF16)
        block = grad_share(grad_out, (place ^ r) * slab, me, share_rows, experts)
        if spare > share_rows:
            block = jnp.concatenate([block, jnp.zeros((spare - share_rows, width), F32)], 0)
        half[place_of, slab:, :width] = block.astype(BF16)
        if half.shape[2] > LANES + 3 * columns:
            half[place_of, :slab, LANES + 3 * columns :] = jnp.zeros(
                (slab, half.shape[2] - LANES - 3 * columns), BF16
            )
    moves.start(send, send_out)
    moves.start(keep, keep_out)
    moves.finish()


def finish_body(terms, *refs):
    where, vectors, x = refs[:3]
    parts = refs[3 : 3 + terms]
    grad_resid, result = refs[3 + terms :]
    total = added(parts)
    unit, factor = normal(x[...].astype(F32))
    back = normal_back(total, unit, factor, vectors[0:1, :])
    result[...] = (grad_resid[...] + back).astype(BF16)


def collect_body(tile, *refs):
    count = (len(refs) - 6) // 2
    where, terms = refs[0], refs[1 : 1 + 2 * count]
    gate_out, up_out, held, gate, up, sems = refs[1 + 2 * count :]
    moves = Moves(sems)
    arriving = [moves.start(term.at[0], held.at[i]) for i, term in enumerate(terms)]
    steps = gate.shape[1] // tile
    moves.wait(*arriving)
    for step in range(steps):
        which, at = divmod(step, steps // 2)
        for k, result in enumerate((gate, up)):
            lanes = slice((2 * at + k) * tile, (2 * at + k + 1) * tile)
            total = held[which * count, :, lanes].astype(F32)
            for i in range(1, count):
                total += held[which * count + i, :, lanes].astype(F32)
            result[:, step * tile : (step + 1) * tile] = total
    moves.start(gate, gate_out)
    moves.start(up, up_out)
    moves.finish()


def shares_body(experts, top, bottom, *refs):
    where, terms = refs[0], refs[1 : -4 - experts]
    pieces, rest_out = refs[-4 - experts : -4], refs[-4]
    held, total, sems = refs[-3:]
    moves = Moves(sems)
    me = where[0]
    arriving = [moves.start(term.at[0], held.at[i]) for i, term in enumerate(terms)]
    moves.wait(*arriving)
    whole = held[0].astype(F32)
    for i in range(1, len(terms)):
        whole += held[i].astype(F32)
    total[...] = whole
    rest_out[...] = total[top : top + bottom, : rest_out.shape[1]]
    count = top // experts
    for r in range(experts):
        block = total[rows_at(me ^ r, count), : pieces[r].shape[1]]
        pieces[r][...] = block.astype(BF16)


def assemble_body(experts, copies, *refs):
    where = refs[0]
    units_in, heads_in = refs[1 : 1 + experts], refs[1 + experts : 1 + 2 * experts]
    gate, up, qkv, vectors = refs[1 + 2 * experts :]
    total = units_in[0].shape[1] // 2
    units = total // copies
    columns = (heads_in[0].shape[1] - LANES) // 3
    width = qkv.shape[1] // 3
    side = heads_in[0][:, :LANES].astype(F32)
    for r in range(1, experts):
        side += heads_in[r][:, :LANES].astype(F32)
    vectors[...] = side
    for e in range(experts):

        @pl.when(where[0] == e)
        def _():
            for k, result in enumerate((gate, up)):
                sources = [units_in[e ^ other][...].astype(F32) for other in range(experts)]
                parts = []
                for d in range(copies):
                    at = k * total + d * units
                    parts += [source[:, at : at + units] for source in sources]
                result[...] = jnp.concatenate(parts, 1)
            for i in range(3):
                at = LANES + i * columns
                parts = [
                    heads_in[e ^ other][:, at : at + columns].astype(F32)
                    for other in range(experts)
                ]
                qkv[:, i * width : (i + 1) * width] = jnp.concatenate(parts, 1)


def expert_half(operands, state, experts, copies, tile, last):
    n2, wg = operands[1], operands[5]
    length, width = n2.shape
    hidden = wg.shape[1]
    slab, per = width // copies, hidden // copies
    tokens = length // experts
    half = (copies // 2, slab, hidden)
    sums = (length, width)
    outs = [(half, BF16), (half, BF16)]
    down = (hidden if last else hidden // 2, width)
    slot = (2, copies // 2, slab, 2 * tile)
    scratch = [(sums, BF16), ((width, length), BF16), (sums, BF16), ((length, SLOTS), F32)]
    scratch += [(sums, F32)] * 2 + [((length, LANES), F32), (down, BF16)]
    scratch += [((2, width, tile), BF16)] * 2 + [((2, tile, width), BF16)]
    scratch += [((length, tile), BF16)] * 3 + [((width, tile), F32)] * 2 + [(slot, BF16)] * 2
    if last:
        final = [((copies // 2, per, width), BF16)] * 2
        for lanes in (width, width, width + LANES, width + LANES):
            final.append(((experts // 2, tokens, lanes), BF16))
        outs += final
        scratch += final + [((length, LANES), F32)] + [(sums, F32)] * (2 if tile == 512 else 1)
    else:
        outs += [(sums, F32), (sums, F32), ((length, LANES), F32), (down, BF16)]
    steps = hidden // 2 // tile
    body = functools.partial(expert_body, experts, copies, last)
    return moving(body, outs, scratch, 16 + 5 * steps)(*operands, *state)


def rows_to_owners(value):
    count = lax.axis_size("expert")
    me = lax.axis_index("expert")
    parts = value.reshape((count, value.shape[0] // count) + value.shape[1:])
    found = []
    for r in range(count):
        part = lax.dynamic_index_in_dim(parts, me ^ r, 0, keepdims=False)
        found.append((swap(part, "expert", r) if r else part)[None])
    return in_order(found, "expert")


def shards(
    inputs,
    norm1_gain,
    qkv_weight,
    out_weight,
    norm2_gain,
    router_weight,
    shared_gate,
    shared_up,
    shared_down,
    expert_gate,
    expert_up,
    expert_down,
    expert_ids,
    piece_starts,
    cotangent,
):
    tokens, width = inputs.shape[1:]
    heads = width // HEAD_DIM
    experts = lax.axis_size("expert")
    copies = lax.axis_size("dp")
    me = lax.axis_index("expert")
    place = lax.axis_index("dp")
    where = jnp.stack([me, place]).astype(jnp.int32)
    length = tokens * experts
    slab = width // copies
    own_heads = -(-heads // experts)
    columns = own_heads * HEAD_DIM
    padded = experts * columns
    units = shared_down.shape[0] // experts
    total = copies * units
    wide = max(2 * total, width)
    apart = slab % 16 == 0 and units % 16 == 0 and padded == width
    small = length <= 1024
    tile = 512 if small else 256

    first = local(
        functools.partial(pack_first_body, experts),
        [((slab, LANES + 3 * columns), BF16)],
        [((LANES, LANES), F32)],
    )(where, norm1_gain[None], norm2_gain[None], router_weight.T, qkv_weight)[0]
    x = far_blocks("expert", inputs[0])
    first = far_blocks("dp", first)
    named = jnp.any(
        expert_ids[0][:, :, None] == jnp.arange(LANES, dtype=jnp.int32)[None, None, :], 1
    ).astype(BF16)
    out_whole = lax.all_gather(out_weight, "dp", axis=0, tiled=True)
    out_whole = jnp.pad(out_whole, ((0, padded - width), (0, 0)))
    dy_own = jnp.concatenate([cotangent[0], named], 1)
    dy_far = far_blocks("expert", after(dy_own, x[2]))
    if apart:
        packed = local(
            functools.partial(pack_units_body, experts, copies), [((slab + units, wide), BF16)]
        )(where, shared_gate, shared_up, shared_down)[0]
        shared_blocks = [lax.all_gather(packed, "dp", axis=0, tiled=False)]
        first[6] = after(first[6], packed, dy_own)
        first = near_blocks("dp", first)
    else:

        def unit_columns(weight):
            split = weight.reshape(slab, copies, experts, units)
            split = lax.dynamic_index_in_dim(split, me, 2, keepdims=False)
            return split.reshape(slab, total)

        top = jnp.concatenate([unit_columns(shared_gate), unit_columns(shared_up)], 1)
        bottom = lax.dynamic_slice_in_dim(shared_down, me * units, units, 0)
        first = [in_order(near_blocks("dp", first), "dp")]
        shared_blocks = [lax.all_gather(part, "dp", axis=0, tiled=True) for part in (top, bottom)]
    x = near_blocks("expert", x)

    cosines, sines = rotary_tables(length)
    projected = [((length, width), BF16)] + [((length, columns), BF16)] * 3
    held = [
        ((length, columns), BF16),
        ((width, LANES + 3 * columns), BF16),
        ((LANES, width), F32),
    ]
    n1, q, k, v, probs, mixed, weight, vectors = moving(
        functools.partial(attend_body, experts, copies, len(first)),
        projected + [((own_heads, length, length), BF16)] + held,
        [((length, LANES), F32)] * 2
        + [((experts, tokens, width), BF16)]
        + projected
        + [((2, own_heads, tokens, length), BF16)]
        + held,
        len(first) + 2 * experts + 9,
        scalars=2,
    )(where, piece_starts, cosines, sines, *x, *first)
    mixed_blocks = near_blocks("expert", far_blocks("expert", mixed))
    dy_wide = near_blocks("expert", dy_far)
    n2, n2_turned, dy, gates, own_resid, own_n2, own_gates = moving(
        functools.partial(settle_body, experts),
        [
            ((length, width), BF16),
            ((width, length), BF16),
            ((length, width), BF16),
            ((length, SLOTS), F32),
            ((tokens, width), F32),
            ((tokens, width), BF16),
            ((tokens, SLOTS), F32),
        ],
        [
            ((LANES, width), F32),
            ((experts, tokens, width), BF16),
            ((experts, tokens, width + LANES), BF16),
            ((experts, length, columns), BF16),
            ((padded, width), BF16),
            ((experts, tokens, width), BF16),
            ((experts, width, tokens), BF16),
            ((experts, tokens, SLOTS), F32),
            ((tokens, width), F32),
        ],
        7 * experts + 5,
    )(where, vectors, *x, *dy_wide, *mixed_blocks, out_whole)

    operands = [where, n2, n2_turned, dy, gates, expert_gate[0], expert_up[0], expert_down[0]]
    a_keep, a_send, y, gx, gg, down = expert_half(operands, (), experts, copies, tile, False)
    y_first, z_first = order_over(copies, 1), order_over(copies, 2)
    a_sum = Halving(a_keep, a_send, "dp", y_first)
    half = ((copies // 2, slab + units, wide), BF16)
    both = [((length, width), F32)] * 2
    s_keep, s_send, y, gx = moving(
        functools.partial(shared_body, copies, len(shared_blocks)),
        [half, half] + both,
        [((length, width), BF16), ((width, length), BF16), ((length, width), BF16)]
        + both * 2
        + [((width, total), BF16)] * 2
        + [((total, width), BF16)]
        + [((length, total), BF16)] * 3
        + [((width, total), F32)] * 2
        + [((total, width), F32), half, half],
        3 * copies + 9,
    )(where, n2, n2_turned, dy, y, gx, *shared_blocks)
    s_sum = Halving(s_keep, s_send, "dp", z_first)
    b_keep, b_send, down_keep, down_send, y_keep, y_send, gx_keep, gx_send = expert_half(
        operands, (y, gx, gg, down), experts, copies, tile, True
    )
    across = bits_of(experts)
    gx_sum = Halving(gx_keep, gx_send, "expert", across)
    b_sum = Halving(b_keep, b_send, "dp", y_first)
    down_sum = Halving(down_keep, down_send, "dp", z_first)
    a_sent = a_sum.wait(gx_send).exchange()
    s_sent = s_sum.wait(gx_send).exchange()
    gx_sum.wait(a_sent, s_sent)
    gx_terms = gx_sum.rest()
    y_sum = Halving(y_keep, after(y_send, gx_terms[-1]), "expert", across)

    attended, grad_resid, sums = local(
        functools.partial(home_body, len(gx_terms)),
        [((tokens, width), BF16), ((tokens, width), F32), ((2 * SLOTS, width), F32)],
    )(where, vectors, *gx_terms, own_resid, own_n2, own_gates, cotangent[0])
    attended_blocks = near_blocks("expert", far_blocks("expert", attended))
    share = slab // experts
    last = ((copies // 2, slab + -(-share // 16) * 16, max(width, LANES + 3 * columns)), BF16)
    quarter = ((experts // 2, tokens, width), BF16)
    l_keep, l_send, gn_keep, gn_send = moving(
        functools.partial(attend_back_body, experts, copies),
        [last, last, quarter, quarter],
        [((length, LANES), F32)] * 2
        + [((2 * SLOTS, width), F32), ((length, width), BF16)]
        + [((experts, length, columns), BF16), ((experts, tokens, width), BF16)]
        + [((padded, width), BF16)]
        + [((length, columns), BF16)] * 3
        + [((length, width), BF16), ((width, LANES + 3 * columns), BF16)]
        + [((2, own_heads, tokens, length), BF16)]
        + [((length, columns), F32)] * 3
        + [((length, 3 * columns), BF16)]
        + [((padded, width), F32), ((width, 3 * columns), F32), ((LANES, width), F32)]
        + [((width, LANES), F32), last, last, quarter, quarter],
        5 * experts + 13,
    )(
        where, cosines, sines, sums, *attended_blocks, *mixed_blocks, *x,
        out_whole, q, k, v, n1, weight, probs,
    )
    last_sum = Halving(l_keep, l_send, "dp", y_first)
    gn_sum = Halving(gn_keep, gn_send, "expert", across)

    sent = [part.wait(l_send).exchange() for part in (b_sum, a_sum, s_sum, down_sum)]
    gn_sum.wait(*sent).exchange()
    last_sent = last_sum.wait(*sent).exchange()
    y_sum.wait(last_sent).exchange()
    sent = [part.wait(last_sent).exchange() for part in (b_sum, down_sum)]
    last_sent = last_sum.wait(*sent).exchange()
    gn_terms = gn_sum.wait(last_sent).rest()
    input_grad = local(
        functools.partial(finish_body, len(gn_terms)), [((tokens, width), BF16)]
    )(where, vectors, inputs[0], *gn_terms, grad_resid)[0]
    outputs = (own_resid + added(y_sum.wait(last_sent).rest())).astype(BF16)
    s_terms = s_sum.wait(last_sent).rest()
    hidden = expert_gate.shape[2]
    a_terms, b_terms = a_sum.rest(), b_sum.rest()
    gate_grad, up_grad = moving(
        functools.partial(collect_body, tile),
        [((slab, hidden), F32)] * 2,
        [((len(a_terms) + len(b_terms), slab, hidden), BF16)] + [((slab, hidden), F32)] * 2,
        len(a_terms) + len(b_terms) + 2,
    )(where, *a_terms, *b_terms)
    down_grad = added(down_sum.rest())
    if apart:

        def shares(terms, columns, bottom):
            rows, lanes = terms[0].shape[1:]
            *pieces, rest = mixed_kernel(
                functools.partial(shares_body, experts, slab, bottom),
                [((share, columns), BF16)] * experts + [((bottom, width), F32)],
                [((len(terms), rows, lanes), BF16), ((rows, lanes), F32)],
                len(terms),
            )(where, *terms)
            return [swap(p, "expert", r) if r else p for r, p in enumerate(pieces)], rest

        unit_pieces, sdown_grad = shares(s_terms, 2 * total, units)
        head_pieces, out_grad = shares(last_sum.rest(), LANES + 3 * columns, share)
        sgate_grad, sup_grad, qkv_grad, vector_sums = local(
            functools.partial(assemble_body, experts, copies),
            [
                ((share, experts * total), F32),
                ((share, experts * total), F32),
                ((share, 3 * width), F32),
                ((share, LANES), F32),
            ],
        )(where, *unit_pieces, *head_pieces)
    else:
        shared_sum, last_total = added(s_terms), added(last_sum.rest())
        sdown_grad, out_grad = shared_sum[slab:, :width], last_total[slab : slab + share, :width]
        pieces = rows_to_owners(shared_sum[:slab, : 2 * total].astype(BF16)).astype(F32)
        pieces = pieces.reshape(experts, share, 2, copies, units).transpose(2, 1, 3, 0, 4)
        sgate_grad, sup_grad = pieces.reshape(2, share, total * experts)
        pieces = rows_to_owners(last_total[:slab, : LANES + 3 * columns].astype(BF16)).astype(F32)
        qkv_grad = pieces[:, :, LANES:].reshape(experts, share, 3, columns)
        qkv_grad = qkv_grad.transpose(1, 2, 0, 3).reshape(share, 3, padded)[:, :, :width]
        qkv_grad = qkv_grad.reshape(share, 3 * width)
        vector_sums = jnp.sum(pieces[:, :, :LANES], 0)
    return (
        outputs[None],
        input_grad[None],
        vector_sums[:, 0],
        qkv_grad,
        out_grad,
        vector_sums[:, 1],
        vector_sums[:, SLOTS : SLOTS + experts],
        sgate_grad,
        sup_grad,
        sdown_grad,
        gate_grad[None],
        up_grad[None],
        down_grad[None],
    )


def solution(mesh):
    return jax.shard_map(
        shards,
        mesh=mesh,
        in_specs=(
            P("dp", "expert", None),
            P("dp"),
            P("dp", None),
            P("dp", None),
            P("dp"),
            P("dp", None),
            P("dp", None),
            P("dp", None),
            P("dp", None),
            P("expert", None, None),
            P("expert", None, None),
            P("expert", None, None),
            P("dp", "expert", None),
            P("dp", None),
            P("dp", "expert", None),
        ),
        out_specs=(
            P("dp", "expert", None),
            P("dp", "expert", None),
            P(("dp", "expert")),
            P(("dp", "expert"), None),
            P(("dp", "expert"), None),
            P(("dp", "expert")),
            P(("dp", "expert"), None),
            P(("dp", "expert"), None),
            P(("dp", "expert"), None),
            P(("dp", "expert"), None),
            P("expert", "dp", None),
            P("expert", "dp", None),
            P("expert", "dp", None),
        ),
        check_vma=False,
    )
```

```python
import functools

import jax
import jax.numpy as jnp
import numpy as np
from jax import lax
from jax.experimental import pallas as pl
from jax.experimental.pallas import tpu as pltpu
from jax.sharding import PartitionSpec as P

HEAD_DIM = 64
PIECE = 256
F32 = jnp.float32
BF16 = jnp.bfloat16
LANES = 128
SLOTS = 8
LIMIT = 63 << 20
VMEM = pl.BlockSpec(memory_space=pltpu.VMEM)
SMEM = pl.BlockSpec(memory_space=pltpu.SMEM)
ANY = pl.BlockSpec(memory_space=pl.ANY)


def swap(value, axis, distance):
    count = lax.axis_size(axis)
    return lax.ppermute(value, axis, [(i, i ^ distance) for i in range(count)])


def after(value, *others):
    return lax.optimization_barrier((value, *others))[0]


def bits_of(count):
    return [1 << k for k in range(count.bit_length() - 1)]


def far_blocks(axis, value):
    return {r: swap(value, axis, r) if r else value for r in range(0, lax.axis_size(axis), 2)}


def near_blocks(axis, found):
    every = dict(found)
    for r in found:
        every[r ^ 1] = swap(found[r], axis, 1)
    return [every[r] for r in range(lax.axis_size(axis))]


def in_order(blocks, axis):
    me = lax.axis_index(axis)
    rows = blocks[0].shape[0]
    whole = jnp.zeros((rows * len(blocks),) + blocks[0].shape[1:], blocks[0].dtype)
    for r, block in enumerate(blocks):
        whole = lax.dynamic_update_slice_in_dim(whole, block, (me ^ r) * rows, 0)
    return whole


def halves(order):
    rest = order[1:]
    found = []
    for r in range(2 << len(rest)):
        place = sum(((r & bit) != 0) << (len(rest) - 1 - i) for i, bit in enumerate(rest))
        found.append((r, bool(r & order[0]), place))
    return found


def crossed(r):
    return r // 4 * 4 + r % 2 * 2 + r // 2 % 2


def partner(me, place, r):
    if crossed(r) == r:
        return place ^ r
    return place ^ jnp.where(me % 2 == 1, crossed(r), r)


def trade(value, axis, bit):
    if axis != "dp":
        return swap(value, axis, bit)
    copies, experts = lax.axis_size("dp"), lax.axis_size("expert")
    pairs = []
    for d in range(copies):
        for e in range(experts):
            other = d ^ (crossed(bit) if e % 2 else bit)
            pairs.append((d * experts + e, other * experts + e))
    return lax.ppermute(value, ("dp", "expert"), pairs)


class Halving:
    def __init__(self, keep, send, axis, order):
        self.axis = axis
        self.order = order[1:]
        self.count = keep.shape[0]
        self.terms = [keep, trade(send, axis, order[0])]

    def wait(self, *others):
        self.terms[-1] = after(self.terms[-1], *others)
        return self

    def exchange(self):
        half = self.count // 2
        sent = sum(term[half : self.count].astype(F32) for term in self.terms).astype(BF16)
        self.terms.append(trade(sent, self.axis, self.order.pop(0)))
        self.count = half
        return sent

    def arrived(self):
        return self.terms[-1]

    def rest(self):
        while self.order:
            self.exchange()
        return self.terms


def added(terms):
    return sum(term[0].astype(F32) for term in terms)


def dot(left, right):
    return lax.dot_general(left, right, (((1,), (0,)), ((), ())), preferred_element_type=F32)


def dot_t(left, right):
    return lax.dot_general(left, right, (((1,), (1,)), ((), ())), preferred_element_type=F32)


def t_dot(left, right):
    return lax.dot_general(left, right, (((0,), (0,)), ((), ())), preferred_element_type=F32)


def local(body, outs, scratch=(), scalars=1):
    def call(*args):
        return pl.pallas_call(
            body,
            out_shape=[jax.ShapeDtypeStruct(shape, kind) for shape, kind in outs],
            in_specs=[SMEM] * scalars + [VMEM] * (len(args) - scalars),
            out_specs=[VMEM] * len(outs),
            scratch_shapes=[pltpu.VMEM(shape, kind) for shape, kind in scratch],
            compiler_params=pltpu.CompilerParams(vmem_limit_bytes=LIMIT),
            cost_estimate=pl.CostEstimate(flops=10**8, bytes_accessed=10**5, transcendentals=0),
        )(*args)

    return call


def moving(body, outs, scratch, copies, scalars=1):
    def call(*args):
        return pl.pallas_call(
            body,
            out_shape=[jax.ShapeDtypeStruct(shape, kind) for shape, kind in outs],
            in_specs=[SMEM] * scalars + [ANY] * (len(args) - scalars),
            out_specs=[ANY] * len(outs),
            scratch_shapes=[pltpu.VMEM(shape, kind) for shape, kind in scratch]
            + [pltpu.SemaphoreType.DMA((copies,))],
            compiler_params=pltpu.CompilerParams(vmem_limit_bytes=LIMIT),
            cost_estimate=pl.CostEstimate(flops=10**8, bytes_accessed=10**5, transcendentals=0),
        )(*args)

    return call


def mixed_kernel(body, outs, scratch, copies, scalars=1):
    def call(*args):
        return pl.pallas_call(
            body,
            out_shape=[jax.ShapeDtypeStruct(shape, kind) for shape, kind in outs],
            in_specs=[SMEM] * scalars + [ANY] * (len(args) - scalars),
            out_specs=[VMEM] * len(outs),
            scratch_shapes=[pltpu.VMEM(shape, kind) for shape, kind in scratch]
            + [pltpu.SemaphoreType.DMA((copies,))],
            compiler_params=pltpu.CompilerParams(vmem_limit_bytes=LIMIT),
            cost_estimate=pl.CostEstimate(flops=10**8, bytes_accessed=10**5, transcendentals=0),
        )(*args)

    return call


class Moves:
    def __init__(self, sems):
        self.sems = sems
        self.used = 0
        self.open = []

    def start(self, source, target):
        move = pltpu.make_async_copy(source, target, self.sems.at[self.used])
        self.used += 1
        move.start()
        self.open.append(move)
        return move

    def wait(self, *moves):
        for move in moves:
            move.wait()
            self.open = [other for other in self.open if other is not move]

    def finish(self):
        self.wait(*list(self.open))


def rows_at(place, count):
    return pl.ds(pl.multiple_of(place * count, count), count)


def normal(values):
    factor = lax.rsqrt(jnp.mean(values * values, -1, keepdims=True) + 1e-06)
    return values * factor, factor


def normal_back(grad_normed, unit, factor, gain):
    grad_unit = grad_normed * gain
    return factor * (grad_unit - unit * jnp.mean(grad_unit * unit, -1, keepdims=True))


def turned(pairs, cosines, sines):
    span = pairs.shape[1]
    lane = lax.broadcasted_iota(jnp.int32, pairs.shape, 1)
    first = lane % HEAD_DIM < HEAD_DIM // 2
    partner = jnp.where(
        first, pltpu.roll(pairs, span - HEAD_DIM // 2, 1), pltpu.roll(pairs, HEAD_DIM // 2, 1)
    )
    return pairs * cosines + partner * sines


def rotary_tables(count):
    halfway = HEAD_DIM // 2
    frequency = np.power(10000.0, -np.arange(halfway, dtype=np.float32) / halfway)
    angles = np.arange(count, dtype=np.float32)[:, None] * frequency.astype(np.float32)[None, :]
    cosines, sines = np.cos(angles), np.sin(angles)
    cosines = np.tile(cosines, (1, 4)).astype(np.float32)
    sines = np.concatenate([-sines, sines, -sines, sines], 1).astype(np.float32)
    return jnp.asarray(cosines), jnp.asarray(sines)


def widened(table, span):
    return jnp.concatenate([table] * (span // LANES), 1)


def reach(block, experts, tokens):
    return min(block + 2, experts) * tokens


def pack_first_body(experts, where, gain1, gain2, router, qkv, result, wide):
    slab, width = result.shape[0], qkv.shape[1] // 3
    columns = (result.shape[1] - LANES) // 3
    wide[...] = jnp.zeros_like(wide)
    wide[0:1, :slab] = gain1[...].astype(F32)
    wide[1:2, :slab] = gain2[...].astype(F32)
    wide[SLOTS : SLOTS + router.shape[0], :slab] = router[...].astype(F32)
    result[:, :LANES] = wide[...].T[:slab, :].astype(BF16)
    for e in range(experts):

        @pl.when(where[0] == e)
        def _():
            for i in range(3):
                start = min(e * columns, width)
                stop = min(start + columns, width)
                at = LANES + i * columns
                if stop > start:
                    result[:, at : at + stop - start] = qkv[:, i * width + start : i * width + stop]
                if stop - start < columns:
                    blank = jnp.zeros((slab, columns - stop + start), BF16)
                    result[:, at + stop - start : at + columns] = blank


def pack_units_body(experts, copies, where, gate, up, down, result):
    slab, width = gate.shape[0], down.shape[1]
    units = down.shape[0] // experts
    total = copies * units
    for e in range(experts):

        @pl.when(where[0] == e)
        def _():
            for k, matrix in enumerate((gate, up)):
                parts = [
                    matrix[:, (d * experts + e) * units : (d * experts + e + 1) * units]
                    for d in range(copies)
                ]
                result[:slab, k * total : (k + 1) * total] = jnp.concatenate(parts, 1)
            result[slab:, :width] = down[e * units : (e + 1) * units, :]
            if result.shape[1] > width:
                result[slab:, width:] = jnp.zeros((units, result.shape[1] - width), BF16)


def attend_body(experts, copies, blocks, *refs):
    where, starts, cosine_in, sine_in = refs[:4]
    x_refs, w_refs = refs[4 : 4 + experts], refs[4 + experts : 4 + experts + blocks]
    refs = refs[4 + experts + blocks :]
    n1_out, q_out, k_out, v_out, probs_out, mixed_out, weight_out, vectors_out = refs[:8]
    cosine_table, sine_table, x, n1, q, k, v, probs, mixed, weight, vectors, sems = refs[8:]
    moves = Moves(sems)
    me, place = where[0], where[1]
    tokens = x_refs[0].shape[0]
    columns = q.shape[1]
    own_heads = columns // HEAD_DIM
    slab = w_refs[0].shape[0]
    if blocks == 1:
        arriving = [moves.start(w_refs[0], weight)]
    else:
        arriving = [
            moves.start(w_refs[r], weight.at[rows_at(place ^ r, slab), :]) for r in range(blocks)
        ]
    tables = [moves.start(cosine_in, cosine_table), moves.start(sine_in, sine_table)]
    rows_in = [moves.start(x_refs[r], x.at[r]) for r in range(experts)]
    moves.wait(*arriving)
    vectors[...] = weight[:, :LANES].astype(F32).T
    moves.start(weight, weight_out)
    moves.start(vectors, vectors_out)
    gain = vectors[0:1, :]
    moves.wait(*tables)
    for r in range(experts):
        rows = rows_at(me ^ r, tokens)
        moves.wait(rows_in[r])
        unit, _ = normal(x[r].astype(F32))
        normed = (unit * gain).astype(BF16)
        n1[rows, :] = normed
        projected = dot(normed, weight[:, LANES:])
        cosines = widened(cosine_table[rows, :], 2 * columns)
        sines = widened(sine_table[rows, :], 2 * columns)
        pair = turned(projected[:, : 2 * columns], cosines, sines).astype(BF16)
        q[rows, :] = pair[:, :columns] * HEAD_DIM ** (-0.5)
        k[rows, :] = pair[:, columns:]
        v[rows, :] = projected[:, 2 * columns :].astype(BF16)
    for held, result in ((n1, n1_out), (q, q_out), (k, k_out), (v, v_out)):
        moves.start(held, result)
    pieces = starts.shape[1]
    leaving = {}
    for block in range(experts):
        seen = reach(block, experts, tokens)
        rows = slice(block * tokens, (block + 1) * tokens)
        query_pos = block * tokens + lax.broadcasted_iota(jnp.int32, (tokens, 1), 0)
        key_pos = lax.broadcasted_iota(jnp.int32, (1, seen), 1)
        query_piece = jnp.full((tokens, 1), -1, jnp.int32)
        key_piece = jnp.full((1, seen), -2, jnp.int32)
        for j in range(pieces):
            start = starts[0, j]
            query_piece = jnp.where(
                (query_pos >= start) & (query_pos < start + PIECE), j, query_piece
            )
            key_piece = jnp.where((key_pos >= start) & (key_pos < start + PIECE), j, key_piece)
        bias = jnp.where((key_pos <= query_pos) | (query_piece == key_piece), 0.0, -1e30)
        slot = block % 2
        if block >= 2:
            moves.wait(leaving[block - 2])
        for h in range(own_heads):
            head = slice(h * HEAD_DIM, (h + 1) * HEAD_DIM)
            scores = dot_t(q[rows, head], k[:seen, head]) + bias
            powers = jnp.exp(scores - jnp.max(scores, -1, keepdims=True))
            share = (powers * (1.0 / jnp.sum(powers, -1, keepdims=True))).astype(BF16)
            probs[slot, h, :, :seen] = share
            mixed[rows, head] = dot(share, v[:seen, head]).astype(BF16)
        leaving[block] = moves.start(
            probs.at[slot, :, :, :seen], probs_out.at[:, rows, :seen]
        )
    moves.start(mixed, mixed_out)
    moves.finish()


def settle_body(experts, blocks, *refs):
    where, vectors_in = refs[:2]
    x_refs = refs[2 : 2 + experts]
    dy_refs = refs[2 + experts : 2 + 2 * experts]
    m_refs = refs[2 + 2 * experts : 2 + 3 * experts]
    o_refs, refs = refs[2 + 3 * experts :][:blocks], refs[2 + 3 * experts + blocks :]
    n2_out, n2_turned_out, dy_out, gates_out, own_resid_out, own_n2_out, own_gates_out, matrix_out = refs[:8]
    vectors, x, dy, mixed, out_matrix, n2, n2_turned, gates, own_resid, sems = refs[8:]
    moves = Moves(sems)
    me, place = where[0], where[1]
    slab = o_refs[0].shape[0]
    tokens, width = x_refs[0].shape
    columns = m_refs[0].shape[1]
    mixed_in = [moves.start(m_refs[j], mixed.at[j]) for j in range(experts)]
    vectors_move = moves.start(vectors_in, vectors)
    x_in = [moves.start(x_refs[r], x.at[r]) for r in range(experts)]
    dy_in = [moves.start(dy_refs[r], dy.at[r]) for r in range(experts)]
    if blocks == 1:
        matrix_in = [moves.start(o_refs[0], out_matrix)]
    else:
        matrix_in = [
            moves.start(o_refs[r], out_matrix.at[rows_at(place ^ r, slab), :])
            for r in range(blocks)
        ]
    moves.wait(*matrix_in, *mixed_in, vectors_move)
    moves.start(out_matrix, matrix_out)
    gain = vectors[1:2, :]
    router = vectors[SLOTS : 2 * SLOTS, :].astype(BF16)
    for r in range(experts):
        rows = rows_at(me ^ r, tokens)
        moves.wait(x_in[r], dy_in[r])
        moves.start(dy.at[r, :, :width], dy_out.at[rows, :])
        resid = x[r].astype(F32)
        for j in range(experts):
            resid += dot(mixed[j, rows, :], out_matrix[rows_at(me ^ j, columns), :])
        unit, _ = normal(resid)
        normed = (unit * gain).astype(BF16)
        logits = dot_t(normed, router)
        chosen = dy[r, :, width : width + SLOTS].astype(F32)
        masked = jnp.where(chosen > 0.0, logits, -1e30)
        powers = chosen * jnp.exp(masked - jnp.max(masked, -1, keepdims=True))
        n2[r] = normed
        n2_turned[r] = normed.astype(F32).T.astype(BF16)
        gates[r] = powers / jnp.sum(powers, -1, keepdims=True)
        moves.start(n2.at[r], n2_out.at[rows, :])
        moves.start(n2_turned.at[r], n2_turned_out.at[:, rows])
        moves.start(gates.at[r], gates_out.at[rows, :])
        if r == 0:
            own_resid[...] = resid
            moves.start(own_resid, own_resid_out)
            moves.start(n2.at[0], own_n2_out)
            moves.start(gates.at[0], own_gates_out)
    moves.finish()


def unit_tile(me, fresh, n2, dy, gates, wg, wu, wd, y, gx, gg, hidden_s, gate_s, up_s):
    chunk = 512 if n2.shape[0] <= 1024 else 256

    def step(c, carry):
        rows = pl.ds(pl.multiple_of(c * chunk, chunk), chunk)
        x, g = n2[rows, :], dy[rows, :]
        gate_pre = dot(x, wg[...])
        up_pre = dot(x, wu[...])
        raw = dot_t(g, wd[...])
        logistic = lax.logistic(gate_pre)
        swish = gate_pre * logistic
        slope = logistic + swish * (1.0 - logistic)
        hidden = swish * up_pre
        if gates is not None:
            lane = lax.broadcasted_iota(jnp.int32, (chunk, SLOTS), 1)
            scale = jnp.sum(jnp.where(lane == me, gates[rows, :], 0.0), -1, keepdims=True)
            gg[rows, :] += jnp.sum(hidden * raw, -1, keepdims=True)
            hidden = hidden * scale
            raw = raw * scale
        hidden = hidden.astype(BF16)
        grad_gate = (raw * up_pre * slope).astype(BF16)
        grad_up = (raw * swish).astype(BF16)
        hidden_s[rows, :] = hidden
        gate_s[rows, :] = grad_gate
        up_s[rows, :] = grad_up
        out = dot(hidden, wd[...])
        back = dot_t(grad_gate, wg[...]) + dot_t(grad_up, wu[...])
        if fresh:
            y[rows, :] = out
            gx[rows, :] = back
        else:
            y[rows, :] += out
            gx[rows, :] += back
        return carry

    lax.fori_loop(0, n2.shape[0] // chunk, step, 0)


def shared_body(experts, copies, blocks, *refs):
    where, n2_in, n2_turned_in, dy_in, y_in, gx_in, gg_in = refs[:7]
    b_refs, refs = refs[7 : 7 + blocks], refs[7 + blocks :]
    keep_out, send_out, y_keep_out, y_send_out, gx_keep_out, gx_send_out = refs[:6]
    n2, n2_turned, dy, y, gx, y_more, gx_more, gg, wg, wu, wd = refs[6:17]
    hidden_s, gate_s, up_s, grad_gate, grad_up, grad_down = refs[17:23]
    keep, send, y_keep, y_send, gx_keep, gx_send, sems = refs[23:]
    moves = Moves(sems)
    me, place = where[0], where[1]
    width = n2.shape[1]
    total = wg.shape[1]
    units = total // copies
    slab = width // copies
    tokens = y_keep.shape[1]
    if blocks == 2:
        places = [
            (b_refs[0].at[:, :total], wg),
            (b_refs[0].at[:, total : 2 * total], wu),
            (b_refs[1], wd),
        ]
    else:
        places = []
        for r in range(copies):
            rows = slice(r * slab, (r + 1) * slab)
            places.append((b_refs[0].at[r, :slab, :total], wg.at[rows, :]))
            places.append((b_refs[0].at[r, :slab, total : 2 * total], wu.at[rows, :]))
            rows = slice(r * units, (r + 1) * units)
            places.append((b_refs[0].at[r, slab:, :width], wd.at[rows, :]))
    arriving = [moves.start(source, target) for source, target in places]
    arriving += [moves.start(n2_in, n2), moves.start(dy_in, dy)]
    moves.wait(*arriving)
    sums_in = [moves.start(gx_in, gx_more), moves.start(gg_in, gg), moves.start(y_in, y_more)]
    turned_in = moves.start(n2_turned_in, n2_turned)
    unit_tile(None, True, n2, dy, None, wg, wu, wd, y, gx, None, hidden_s, gate_s, up_s)
    moves.wait(*sums_in)
    for r, leaves, k in halves(bits_of(experts)):
        rows = rows_at(me ^ r, tokens)
        half = gx_send if leaves else gx_keep
        half[k, :, :width] = (gx[rows, :] + gx_more[rows, :]).astype(BF16)
        lane = lax.broadcasted_iota(jnp.int32, (tokens, LANES), 1)
        whole = gg[rows, :]
        coarse = whole.astype(BF16).astype(F32)
        half[k, :, width:] = (
            jnp.where(lane == me, coarse, 0.0)
            + jnp.where(lane == me + SLOTS, whole - coarse, 0.0)
        ).astype(BF16)
        half = y_send if leaves else y_keep
        half[k] = (y[rows, :] + y_more[rows, :]).astype(BF16)
    moves.start(gx_send, gx_send_out)
    moves.start(gx_keep, gx_keep_out)
    moves.start(y_send, y_send_out)
    moves.start(y_keep, y_keep_out)
    moves.wait(turned_in)
    grad_gate[...] = dot(n2_turned[...], gate_s[...])
    grad_up[...] = dot(n2_turned[...], up_s[...])
    grad_down[...] = t_dot(hidden_s[...], dy[...])
    for r, leaves, k in halves(bits_of(copies)):
        half = send if leaves else keep
        rows = rows_at(partner(me, place, r), slab)
        half[k, :slab, :total] = grad_gate[rows, :].astype(BF16)
        half[k, :slab, total : 2 * total] = grad_up[rows, :].astype(BF16)
        rows = rows_at(partner(me, place, r), units)
        half[k, slab:, :width] = grad_down[rows, :].astype(BF16)
        spare = half.shape[2] - width
        if spare:
            half[k, slab:, width:] = jnp.zeros((units, spare), BF16)
        spare = half.shape[2] - 2 * total
        if spare:
            half[k, :slab, 2 * total :] = jnp.zeros((slab, spare), BF16)
    moves.start(send, send_out)
    moves.start(keep, keep_out)
    moves.finish()


def expert_body(copies, last, *refs):
    where, n2_in, n2_turned_in, dy_in, gates_in, wg_in, wu_in, wd_in = refs[:8]
    refs = refs[8:]
    if last:
        y_in, gx_in, gg_in, down_in = refs[:4]
        refs = refs[4:]
    keep_out, send_out, y_out, gx_out, gg_out, down_out = refs[:6]
    refs = refs[6:]
    if last:
        down_send_out, refs = refs[0], refs[1:]
    n2, n2_turned, dy, gates, y, gx, gg, down, wg, wu, wd = refs[:11]
    hidden_s, gate_s, up_s, grad_gate, grad_up, keep, send = refs[11:18]
    if last:
        down_keep, down_send, gg_more = refs[18:21]
        gx_more, y_more = refs[21], refs[-2]
        roomy = y_more is not gx_more
    moves = Moves(refs[-1])
    me, place = where[0], where[1]
    slab = keep.shape[2]
    tile = wg.shape[2]
    hidden = wd_in.shape[0]
    steps = hidden // 2 // tile
    first = hidden // 2 if last else 0
    units = [slice(first + s * tile, first + (s + 1) * tile) for s in range(steps)]

    def fetch(step):
        slot = step % 2
        return [
            moves.start(wg_in.at[:, units[step]], wg.at[slot]),
            moves.start(wu_in.at[:, units[step]], wu.at[slot]),
            moves.start(wd_in.at[units[step], :], wd.at[slot]),
        ]

    weights = {0: fetch(0)}
    arriving = [moves.start(n2_in, n2), moves.start(dy_in, dy), moves.start(gates_in, gates)]
    gg[...] = jnp.zeros_like(gg)
    moves.wait(*arriving)
    turned_in = [moves.start(n2_turned_in, n2_turned)]
    weights[1] = fetch(1)
    if last:
        sums_in = [moves.start(gx_in, gx_more), moves.start(gg_in, gg_more)]
        if roomy:
            sums_in.append(moves.start(y_in, y_more))
        earlier = moves.start(down_in, down.at[: hidden // 2, :])
    leaving = {}
    for step in range(steps):
        slot = step % 2
        moves.wait(*weights[step])
        unit_tile(
            me, step == 0, n2, dy, gates, wg.at[slot], wu.at[slot], wd.at[slot],
            y, gx, gg, hidden_s, gate_s, up_s,
        )
        if 1 <= step and step + 1 < steps:
            weights[step + 1] = fetch(step + 1)
        elif step == 0 and steps > 2:
            weights[2] = fetch(2)
        if step == steps - 1:
            if last:
                moves.wait(*sums_in)
                gg[...] += gg_more[...]
                gx[...] += gx_more[...]
                if not roomy:
                    moves.wait(moves.start(y_in, y_more))
                y[...] += y_more[...]
            moves.start(y, y_out)
            moves.start(gx, gx_out)
            moves.start(gg, gg_out)
        moves.wait(*turned_in)
        turned_in = []
        grad_gate[...] = dot(n2_turned[...], gate_s[...])
        grad_up[...] = dot(n2_turned[...], up_s[...])
        down[units[step] if last else slice(step * tile, (step + 1) * tile), :] = t_dot(
            hidden_s[...], dy[...]
        ).astype(BF16)
        if step >= 2:
            moves.wait(*leaving[step - 2])
        for r, leaves, k in halves(bits_of(copies)):
            half = send if leaves else keep
            rows = rows_at(partner(me, place, r), slab)
            half[slot, k, :, :tile] = grad_gate[rows, :].astype(BF16)
            half[slot, k, :, tile:] = grad_up[rows, :].astype(BF16)
        at = slice(2 * step * tile, 2 * (step + 1) * tile)
        leaving[step] = [
            moves.start(send.at[slot], send_out.at[:, :, at]),
            moves.start(keep.at[slot], keep_out.at[:, :, at]),
        ]
    if last:
        moves.wait(earlier)
        per = hidden // copies
        for r, leaves, k in halves(bits_of(copies)):
            half = down_send if leaves else down_keep
            half[k] = down[rows_at(partner(me, place, r), per), :]
        moves.start(down_send, down_send_out)
        moves.start(down_keep, down_out)
    else:
        moves.start(down, down_out)
    moves.finish()


def home_body(terms, *refs):
    where, vectors = refs[:2]
    parts = refs[2 : 2 + terms]
    own_resid, own_n2, own_gates, cotangent, attended, grad_resid, sums = refs[2 + terms :]
    width = own_n2.shape[1]
    total = added(parts)
    grad_gates = total[:, width : width + SLOTS] + total[:, width + SLOTS : width + 2 * SLOTS]
    gates = own_gates[...]
    grad_logits = (
        gates * (grad_gates - jnp.sum(gates * grad_gates, -1, keepdims=True))
    ).astype(BF16)
    grad_normed = total[:, :width] + dot(
        grad_logits, vectors[SLOTS : 2 * SLOTS, :].astype(BF16)
    )
    unit, factor = normal(own_resid[...])
    sums[0:SLOTS, :] = jnp.broadcast_to(
        jnp.sum(grad_normed * unit, 0, keepdims=True), (SLOTS, width)
    )
    sums[SLOTS : 2 * SLOTS, :] = t_dot(grad_logits, own_n2[...])
    back = cotangent[...].astype(F32) + normal_back(grad_normed, unit, factor, vectors[1:2, :])
    grad_resid[...] = back
    attended[...] = back.astype(BF16)


def grad_share(matrix, start, me, count, experts):
    if count % 8 == 0:
        return matrix[pl.ds(pl.multiple_of(start + me * count, count), count), :]
    rows = matrix[pl.ds(pl.multiple_of(start, 8), count * experts), :]
    picked = rows[:count]
    for e in range(1, experts):
        picked = jnp.where(me == e, rows[e * count : (e + 1) * count], picked)
    return picked


def attend_back_body(experts, copies, *refs):
    where, cosine_in, sine_in, sums_in = refs[:4]
    a_refs = refs[4 : 4 + experts]
    m_refs = refs[4 + experts : 4 + 2 * experts]
    x_refs = refs[4 + 2 * experts : 4 + 3 * experts]
    refs = refs[4 + 3 * experts :]
    matrix_in, q_in, k_in, v_in, n1_in, weight_in, probs_in = refs[:7]
    keep_out, send_out, gn_keep_out, gn_send_out = refs[7:11]
    refs = refs[11:]
    cosine_table, sine_table, sums, attended, mixed, x, out_matrix, q, k, v, n1, weight, probs = refs[:13]
    grad_q, grad_k, grad_v, grad_projected, grad_out, grad_qkv, extra, side = refs[13:21]
    keep, send, gn_keep, gn_send, sems = refs[21:]
    moves = Moves(sems)
    me, place = where[0], where[1]
    tokens, width = x_refs[0].shape
    columns = q.shape[1]
    own_heads = columns // HEAD_DIM
    root = HEAD_DIM ** (-0.5)

    def fetch(block):
        seen = reach(block, experts, tokens)
        rows = slice(block * tokens, (block + 1) * tokens)
        return moves.start(
            probs_in.at[:, rows, :seen], probs.at[block % 2, :, :, :seen]
        )

    needed = [
        moves.start(a_refs[r], attended.at[rows_at(me ^ r, tokens), :]) for r in range(experts)
    ]
    needed += [moves.start(matrix_in, out_matrix)]
    needed += [moves.start(source, held) for source, held in ((v_in, v), (k_in, k), (q_in, q))]
    shares = {0: fetch(0), 1: fetch(1)}
    mixed_in = [moves.start(m_refs[j], mixed.at[j]) for j in range(experts)]
    later = [moves.start(weight_in, weight), moves.start(cosine_in, cosine_table)]
    later += [moves.start(sine_in, sine_table), moves.start(sums_in, sums)]
    x_in = [moves.start(x_refs[r], x.at[r]) for r in range(experts)]
    n1_move = moves.start(n1_in, n1)
    grad_k[...] = jnp.zeros_like(grad_k)
    grad_v[...] = jnp.zeros_like(grad_v)
    moves.wait(*needed)
    own_out = out_matrix[rows_at(me, columns), :]
    for block in range(experts):
        seen = reach(block, experts, tokens)
        rows = slice(block * tokens, (block + 1) * tokens)
        slot = block % 2
        grad_mixed = dot_t(attended[rows, :], own_out).astype(BF16)
        moves.wait(shares[block])
        for h in range(own_heads):
            head = slice(h * HEAD_DIM, (h + 1) * HEAD_DIM)
            gm = grad_mixed[:, head]
            share = probs[slot, h, :, :seen]
            wide = share.astype(F32)
            grad_probs = dot_t(gm, v[:seen, head])
            delta = jnp.sum(wide * grad_probs, -1, keepdims=True)
            grad_scores = (wide * (grad_probs - delta)).astype(BF16)
            grad_q[rows, head] = dot(grad_scores, k[:seen, head]) * root
            grad_k[:seen, head] += t_dot(grad_scores, q[rows, head])
            grad_v[:seen, head] += t_dot(share, gm)
        if block + 2 < experts:
            shares[block + 2] = fetch(block + 2)
    moves.wait(*later)
    gain_sum = jnp.zeros((1, width), F32)
    for r in list(range(1, experts, 2)) + list(range(0, experts, 2)):
        rows = rows_at(me ^ r, tokens)
        pair = jnp.concatenate([grad_q[rows, :], grad_k[rows, :]], 1)
        cosines = widened(cosine_table[rows, :], 2 * columns)
        sines = widened(sine_table[rows, :], 2 * columns)
        back = turned(pair, cosines, -sines).astype(BF16)
        grad_projected[rows, : 2 * columns] = back
        grad_projected[rows, 2 * columns :] = grad_v[rows, :].astype(BF16)
        grad_normed = dot_t(grad_projected[rows, :], weight[:, LANES:])
        moves.wait(x_in[r])
        unit, _ = normal(x[r].astype(F32))
        gain_sum += jnp.sum(grad_normed * unit, 0, keepdims=True)
        _, leaves, spot = halves(bits_of(experts))[r]
        half, result = (gn_send, gn_send_out) if leaves else (gn_keep, gn_keep_out)
        half[spot] = grad_normed.astype(BF16)
        moves.start(half.at[spot], result.at[spot])
    moves.wait(n1_move, *mixed_in)
    for r in range(experts):
        grad_out[rows_at(me ^ r, columns), :] = t_dot(mixed[r], attended[...])
    grad_qkv[...] = t_dot(n1[...], grad_projected[...])
    extra[...] = jnp.zeros_like(extra)
    extra[0:1, :] = gain_sum
    extra[1:2, :] = sums[0:1, :]
    extra[SLOTS : 2 * SLOTS, :] = sums[SLOTS : 2 * SLOTS, :]
    side[...] = extra[...].T
    slab = width // copies
    share_rows = slab // experts
    spare = keep.shape[1] - slab
    for r, leaves, place_of in halves(bits_of(copies)):
        half = send if leaves else keep
        owner = partner(me, place, r)
        rows = rows_at(owner, slab)
        half[place_of, :slab, :LANES] = side[rows, :].astype(BF16)
        half[place_of, :slab, LANES : LANES + 3 * columns] = grad_qkv[rows, :].astype(BF16)
        block = grad_share(grad_out, owner * slab, me, share_rows, experts)
        if spare > share_rows:
            block = jnp.concatenate([block, jnp.zeros((spare - share_rows, width), F32)], 0)
        half[place_of, slab:, :width] = block.astype(BF16)
        if half.shape[2] > LANES + 3 * columns:
            half[place_of, :slab, LANES + 3 * columns :] = jnp.zeros(
                (slab, half.shape[2] - LANES - 3 * columns), BF16
            )
    moves.start(send, send_out)
    moves.start(keep, keep_out)
    moves.finish()


def finish_body(terms, *refs):
    where, vectors, x = refs[:3]
    parts = refs[3 : 3 + terms]
    grad_resid, result = refs[3 + terms :]
    total = added(parts)
    unit, factor = normal(x[...].astype(F32))
    back = normal_back(total, unit, factor, vectors[0:1, :])
    result[...] = (grad_resid[...] + back).astype(BF16)


def collect_body(tile, *refs):
    count = (len(refs) - 6) // 2
    where, terms = refs[0], refs[1 : 1 + 2 * count]
    gate_out, up_out, held, gate, up, sems = refs[1 + 2 * count :]
    moves = Moves(sems)
    arriving = [moves.start(term.at[0], held.at[i]) for i, term in enumerate(terms)]
    steps = gate.shape[1] // tile
    moves.wait(*arriving)
    for step in range(steps):
        which, at = divmod(step, steps // 2)
        for k, result in enumerate((gate, up)):
            lanes = slice((2 * at + k) * tile, (2 * at + k + 1) * tile)
            total = held[which * count, :, lanes].astype(F32)
            for i in range(1, count):
                total += held[which * count + i, :, lanes].astype(F32)
            result[:, step * tile : (step + 1) * tile] = total
    moves.start(gate, gate_out)
    moves.start(up, up_out)
    moves.finish()


def shares_body(experts, top, bottom, *refs):
    where, terms = refs[0], refs[1 : -4 - experts]
    pieces, rest_out = refs[-4 - experts : -4], refs[-4]
    held, total, sems = refs[-3:]
    moves = Moves(sems)
    me = where[0]
    arriving = [moves.start(term.at[0], held.at[i]) for i, term in enumerate(terms)]
    moves.wait(*arriving)
    whole = held[0].astype(F32)
    for i in range(1, len(terms)):
        whole += held[i].astype(F32)
    total[...] = whole
    rest_out[...] = total[top : top + bottom, : rest_out.shape[1]]
    count = top // experts
    for r in range(experts):
        block = total[rows_at(me ^ r, count), : pieces[r].shape[1]]
        pieces[r][...] = block.astype(BF16)


def assemble_body(experts, copies, *refs):
    where = refs[0]
    units_in, heads_in = refs[1 : 1 + experts], refs[1 + experts : 1 + 2 * experts]
    gate, up, qkv, gain1, gain2, router = refs[1 + 2 * experts :]
    total = units_in[0].shape[1] // 2
    units = total // copies
    columns = (heads_in[0].shape[1] - LANES) // 3
    width = qkv.shape[1] // 3
    side = heads_in[0][:, :LANES].astype(F32)
    for r in range(1, experts):
        side += heads_in[r][:, :LANES].astype(F32)
    rows = side.T
    gain1[...] = rows[0:1, :]
    gain2[...] = rows[1:2, :]
    router[...] = rows[SLOTS : SLOTS + experts, :]
    for e in range(experts):

        @pl.when(where[0] == e)
        def _():
            for k, result in enumerate((gate, up)):
                sources = [units_in[e ^ other][...].astype(F32) for other in range(experts)]
                parts = []
                for d in range(copies):
                    at = k * total + d * units
                    parts += [source[:, at : at + units] for source in sources]
                result[...] = jnp.concatenate(parts, 1)
            for i in range(3):
                at = LANES + i * columns
                parts = [
                    heads_in[e ^ other][:, at : at + columns].astype(F32)
                    for other in range(experts)
                ]
                qkv[:, i * width : (i + 1) * width] = jnp.concatenate(parts, 1)


def expert_half(operands, state, copies, tile, last):
    n2, wg = operands[1], operands[5]
    length, width = n2.shape
    hidden = wg.shape[1]
    slab, per = width // copies, hidden // copies
    half = (copies // 2, slab, hidden)
    sums = (length, width)
    outs = [(half, BF16), (half, BF16), (sums, F32), (sums, F32), ((length, LANES), F32)]
    down = (hidden if last else hidden // 2, width)
    slot = (2, copies // 2, slab, 2 * tile)
    scratch = [(sums, BF16), ((width, length), BF16), (sums, BF16), ((length, SLOTS), F32)]
    scratch += [(sums, F32)] * 2 + [((length, LANES), F32), (down, BF16)]
    scratch += [((2, width, tile), BF16)] * 2 + [((2, tile, width), BF16)]
    scratch += [((length, tile), BF16)] * 3 + [((width, tile), F32)] * 2 + [(slot, BF16)] * 2
    if last:
        final = [((copies // 2, per, width), BF16)] * 2
        outs += final
        scratch += final + [((length, LANES), F32)] + [(sums, F32)] * (2 if tile == 512 else 1)
    else:
        outs.append((down, BF16))
    steps = hidden // 2 // tile
    body = functools.partial(expert_body, copies, last)
    return moving(body, outs, scratch, 16 + 5 * steps)(*operands, *state)


def rows_to_owners(value):
    count = lax.axis_size("expert")
    me = lax.axis_index("expert")
    parts = value.reshape((count, value.shape[0] // count) + value.shape[1:])
    found = []
    for r in range(count):
        part = lax.dynamic_index_in_dim(parts, me ^ r, 0, keepdims=False)
        found.append((swap(part, "expert", r) if r else part)[None])
    return in_order(found, "expert")


def shards(
    inputs,
    norm1_gain,
    qkv_weight,
    out_weight,
    norm2_gain,
    router_weight,
    shared_gate,
    shared_up,
    shared_down,
    expert_gate,
    expert_up,
    expert_down,
    expert_ids,
    piece_starts,
    cotangent,
):
    tokens, width = inputs.shape[1:]
    heads = width // HEAD_DIM
    experts = lax.axis_size("expert")
    copies = lax.axis_size("dp")
    me = lax.axis_index("expert")
    place = lax.axis_index("dp")
    where = jnp.stack([me, place]).astype(jnp.int32)
    length = tokens * experts
    slab = width // copies
    own_heads = -(-heads // experts)
    columns = own_heads * HEAD_DIM
    padded = experts * columns
    units = shared_down.shape[0] // experts
    total = copies * units
    wide = max(2 * total, width)
    apart = slab % 16 == 0 and units % 16 == 0 and padded == width
    small = length <= 1024
    tile = 512 if small else 256

    first = local(
        functools.partial(pack_first_body, experts),
        [((slab, LANES + 3 * columns), BF16)],
        [((LANES, LANES), F32)],
    )(where, norm1_gain[None], norm2_gain[None], router_weight.T, qkv_weight)[0]
    x = far_blocks("expert", inputs[0])
    first = far_blocks("dp", first)
    named = jnp.any(
        expert_ids[0][:, :, None] == jnp.arange(LANES, dtype=jnp.int32)[None, None, :], 1
    ).astype(BF16)
    out_whole = lax.all_gather(after(out_weight, first[6]), "dp", axis=0, tiled=True)
    out_blocks = [jnp.pad(out_whole, ((0, padded - width), (0, 0)))]
    dy_own = jnp.concatenate([cotangent[0], named], 1)
    dy_far = far_blocks("expert", after(dy_own, x[2]))
    if apart:
        packed = local(
            functools.partial(pack_units_body, experts, copies), [((slab + units, wide), BF16)]
        )(where, shared_gate, shared_up, shared_down)[0]
        first[6] = after(first[6], packed, dy_own)
        shared_blocks = [lax.all_gather(packed, "dp", axis=0, tiled=False)]
        first = near_blocks("dp", first)
    else:

        def unit_columns(weight):
            split = weight.reshape(slab, copies, experts, units)
            split = lax.dynamic_index_in_dim(split, me, 2, keepdims=False)
            return split.reshape(slab, total)

        top = jnp.concatenate([unit_columns(shared_gate), unit_columns(shared_up)], 1)
        bottom = lax.dynamic_slice_in_dim(shared_down, me * units, units, 0)
        first = [in_order(near_blocks("dp", first), "dp")]
        shared_blocks = [lax.all_gather(part, "dp", axis=0, tiled=True) for part in (top, bottom)]
    x = near_blocks("expert", x)

    cosines, sines = rotary_tables(length)
    projected = [((length, width), BF16)] + [((length, columns), BF16)] * 3
    held = [
        ((length, columns), BF16),
        ((width, LANES + 3 * columns), BF16),
        ((LANES, width), F32),
    ]
    n1, q, k, v, probs, mixed, weight, vectors = moving(
        functools.partial(attend_body, experts, copies, len(first)),
        projected + [((own_heads, length, length), BF16)] + held,
        [((length, LANES), F32)] * 2
        + [((experts, tokens, width), BF16)]
        + projected
        + [((2, own_heads, tokens, length), BF16)]
        + held,
        len(first) + 2 * experts + 9,
        scalars=2,
    )(where, piece_starts, cosines, sines, *x, *first)
    mixed_blocks = near_blocks("expert", far_blocks("expert", mixed))
    dy_wide = near_blocks("expert", dy_far)
    n2, n2_turned, dy, gates, own_resid, own_n2, own_gates, out_whole = moving(
        functools.partial(settle_body, experts, len(out_blocks)),
        [
            ((length, width), BF16),
            ((width, length), BF16),
            ((length, width), BF16),
            ((length, SLOTS), F32),
            ((tokens, width), F32),
            ((tokens, width), BF16),
            ((tokens, SLOTS), F32),
            ((padded, width), BF16),
        ],
        [
            ((LANES, width), F32),
            ((experts, tokens, width), BF16),
            ((experts, tokens, width + LANES), BF16),
            ((experts, length, columns), BF16),
            ((padded, width), BF16),
            ((experts, tokens, width), BF16),
            ((experts, width, tokens), BF16),
            ((experts, tokens, SLOTS), F32),
            ((tokens, width), F32),
        ],
        len(out_blocks) + 7 * experts + 5,
    )(where, vectors, *x, *dy_wide, *mixed_blocks, *out_blocks)

    operands = [where, n2, n2_turned, dy, gates, expert_gate[0], expert_up[0], expert_down[0]]
    a_keep, a_send, y, gx, gg, down = expert_half(operands, (), copies, tile, False)
    far, across = bits_of(copies), bits_of(experts)
    a_sum = Halving(a_keep, a_send, "dp", far)
    b_keep, b_send, y, gx, gg, down_keep, down_send = expert_half(
        operands, (y, gx, gg, down), copies, tile, True
    )
    b_sum = Halving(b_keep, b_send, "dp", far)
    sent = a_sum.wait(b_send).exchange()
    half = ((copies // 2, slab + units, wide), BF16)
    both = [((length, width), F32)] * 2
    final = [
        ((experts // 2, tokens, lanes), BF16)
        for lanes in (width, width, width + LANES, width + LANES)
    ]
    s_keep, s_send, y_keep, y_send, gx_keep, gx_send = moving(
        functools.partial(shared_body, experts, copies, len(shared_blocks)),
        [half, half] + final,
        [((length, width), BF16), ((width, length), BF16), ((length, width), BF16)]
        + both * 2
        + [((length, LANES), F32)]
        + [((width, total), BF16)] * 2
        + [((total, width), BF16)]
        + [((length, total), BF16)] * 3
        + [((width, total), F32)] * 2
        + [((total, width), F32), half, half]
        + final,
        3 * copies + 12,
    )(after(where, sent), n2, n2_turned, dy, y, gx, gg, *shared_blocks)
    gx_sum = Halving(gx_keep, gx_send, "expert", across)
    gx_sent = gx_sum.wait(a_sum.wait(gx_send).exchange()).exchange()
    down_sum = Halving(down_keep, after(down_send, gx_send), "dp", far)
    sent = [b_sum.wait(gx_sent).exchange()]
    gx_terms = gx_sum.rest()
    y_sum = Halving(y_keep, after(y_send, gx_terms[-1]), "expert", across)

    attended, grad_resid, sums = local(
        functools.partial(home_body, len(gx_terms)),
        [((tokens, width), BF16), ((tokens, width), F32), ((2 * SLOTS, width), F32)],
    )(after(where, *sent), vectors, *gx_terms, own_resid, own_n2, own_gates, cotangent[0])
    attended_blocks = near_blocks("expert", far_blocks("expert", attended))
    s_sum = Halving(s_keep, after(s_send, attended), "dp", far)
    sent = [part.wait(attended_blocks[2]).exchange() for part in (b_sum, down_sum)]
    share = slab // experts
    last = ((copies // 2, slab + -(-share // 16) * 16, max(width, LANES + 3 * columns)), BF16)
    quarter = ((experts // 2, tokens, width), BF16)
    l_keep, l_send, gn_keep, gn_send = moving(
        functools.partial(attend_back_body, experts, copies),
        [last, last, quarter, quarter],
        [((length, LANES), F32)] * 2
        + [((2 * SLOTS, width), F32), ((length, width), BF16)]
        + [((experts, length, columns), BF16), ((experts, tokens, width), BF16)]
        + [((padded, width), BF16)]
        + [((length, columns), BF16)] * 3
        + [((length, width), BF16), ((width, LANES + 3 * columns), BF16)]
        + [((2, own_heads, tokens, length), BF16)]
        + [((length, columns), F32)] * 3
        + [((length, 3 * columns), BF16)]
        + [((padded, width), F32), ((width, 3 * columns), F32), ((LANES, width), F32)]
        + [((width, LANES), F32), last, last, quarter, quarter],
        5 * experts + 13,
    )(
        after(where, *sent), cosines, sines, sums, *attended_blocks, *mixed_blocks, *x,
        out_whole, q, k, v, n1, weight, probs,
    )
    last_sum = Halving(l_keep, l_send, "dp", far)
    gn_sum = Halving(gn_keep, gn_send, "expert", across)

    sent = down_sum.wait(l_send, a_sum.arrived(), b_sum.arrived()).exchange()
    s_sent = s_sum.wait(l_send).exchange()
    gn_sent = gn_sum.wait(sent, s_sent).exchange()
    last_sent = last_sum.wait(gn_sent).exchange()
    y_sent = y_sum.wait(last_sent).exchange()
    s_sum.wait(last_sent).exchange()
    last_sent = last_sum.wait(y_sent).exchange()
    gn_terms = gn_sum.wait(last_sent).rest()
    input_grad = local(
        functools.partial(finish_body, len(gn_terms)), [((tokens, width), BF16)]
    )(where, vectors, inputs[0], *gn_terms, grad_resid)[0]
    outputs = (own_resid + added(y_sum.wait(last_sent).rest())).astype(BF16)
    for part in (a_sum, b_sum, s_sum, down_sum):
        part.wait(last_sent)
    s_terms = s_sum.rest()
    hidden = expert_gate.shape[2]
    a_terms, b_terms = a_sum.rest(), b_sum.rest()
    gate_grad, up_grad = moving(
        functools.partial(collect_body, tile),
        [((slab, hidden), F32)] * 2,
        [((len(a_terms) + len(b_terms), slab, hidden), BF16)] + [((slab, hidden), F32)] * 2,
        len(a_terms) + len(b_terms) + 2,
    )(where, *a_terms, *b_terms)
    down_grad = added(down_sum.rest())
    if apart:

        def shares(terms, columns, bottom):
            rows, lanes = terms[0].shape[1:]
            *pieces, rest = mixed_kernel(
                functools.partial(shares_body, experts, slab, bottom),
                [((share, columns), BF16)] * experts + [((bottom, width), F32)],
                [((len(terms), rows, lanes), BF16), ((rows, lanes), F32)],
                len(terms),
            )(where, *terms)
            return [swap(p, "expert", r) if r else p for r, p in enumerate(pieces)], rest

        unit_pieces, sdown_grad = shares(s_terms, 2 * total, units)
        last_sum.wait(gate_grad, down_grad, input_grad, outputs, sdown_grad)
        head_pieces, out_grad = shares(last_sum.rest(), LANES + 3 * columns, share)
        sgate_grad, sup_grad, qkv_grad, gain1_grad, gain2_grad, router_grad = local(
            functools.partial(assemble_body, experts, copies),
            [
                ((share, experts * total), F32),
                ((share, experts * total), F32),
                ((share, 3 * width), F32),
                ((1, share), F32),
                ((1, share), F32),
                ((experts, share), F32),
            ],
        )(where, *unit_pieces, *head_pieces)
        gain1_grad, gain2_grad, router_grad = gain1_grad[0], gain2_grad[0], router_grad.T
    else:
        shared_sum, last_total = added(s_terms), added(last_sum.rest())
        sdown_grad, out_grad = shared_sum[slab:, :width], last_total[slab : slab + share, :width]
        pieces = rows_to_owners(shared_sum[:slab, : 2 * total].astype(BF16)).astype(F32)
        pieces = pieces.reshape(experts, share, 2, copies, units).transpose(2, 1, 3, 0, 4)
        sgate_grad, sup_grad = pieces.reshape(2, share, total * experts)
        pieces = rows_to_owners(last_total[:slab, : LANES + 3 * columns].astype(BF16)).astype(F32)
        qkv_grad = pieces[:, :, LANES:].reshape(experts, share, 3, columns)
        qkv_grad = qkv_grad.transpose(1, 2, 0, 3).reshape(share, 3, padded)[:, :, :width]
        qkv_grad = qkv_grad.reshape(share, 3 * width)
        vector_sums = jnp.sum(pieces[:, :, :LANES], 0)
        gain1_grad, gain2_grad = vector_sums[:, 0], vector_sums[:, 1]
        router_grad = vector_sums[:, SLOTS : SLOTS + experts]
    return (
        outputs[None],
        input_grad[None],
        gain1_grad,
        qkv_grad,
        out_grad,
        gain2_grad,
        router_grad,
        sgate_grad,
        sup_grad,
        sdown_grad,
        gate_grad[None],
        up_grad[None],
        down_grad[None],
    )


def solution(mesh):
    return jax.shard_map(
        shards,
        mesh=mesh,
        in_specs=(
            P("dp", "expert", None),
            P("dp"),
            P("dp", None),
            P("dp", None),
            P("dp"),
            P("dp", None),
            P("dp", None),
            P("dp", None),
            P("dp", None),
            P("expert", None, None),
            P("expert", None, None),
            P("expert", None, None),
            P("dp", "expert", None),
            P("dp", None),
            P("dp", "expert", None),
        ),
        out_specs=(
            P("dp", "expert", None),
            P("dp", "expert", None),
            P(("dp", "expert")),
            P(("dp", "expert"), None),
            P(("dp", "expert"), None),
            P(("dp", "expert")),
            P(("dp", "expert"), None),
            P(("dp", "expert"), None),
            P(("dp", "expert"), None),
            P(("dp", "expert"), None),
            P("expert", "dp", None),
            P("expert", "dp", None),
            P("expert", "dp", None),
        ),
        check_vma=False,
    )
```

```python
import functools

import jax
import jax.numpy as jnp
import numpy as np
from jax import lax
from jax.experimental import pallas as pl
from jax.experimental.pallas import tpu as pltpu
from jax.sharding import PartitionSpec as P

HEAD_DIM = 64
PIECE = 256
F32 = jnp.float32
BF16 = jnp.bfloat16
LANES = 128
SLOTS = 8
VECTORS = 64
LIMIT = 63 << 20
VMEM = pl.BlockSpec(memory_space=pltpu.VMEM)
SMEM = pl.BlockSpec(memory_space=pltpu.SMEM)
ANY = pl.BlockSpec(memory_space=pl.ANY)


def swap(value, axis, distance):
    count = lax.axis_size(axis)
    return lax.ppermute(value, axis, [(i, i ^ distance) for i in range(count)])


def after(value, *others):
    return lax.optimization_barrier((value, *others))[0]


def bits_of(count):
    return [1 << k for k in range(count.bit_length() - 1)]


def far_blocks(axis, value):
    return {r: swap(value, axis, r) if r else value for r in range(0, lax.axis_size(axis), 2)}


def near_blocks(axis, found):
    every = dict(found)
    for r in found:
        every[r ^ 1] = swap(found[r], axis, 1)
    return [every[r] for r in range(lax.axis_size(axis))]


def in_order(blocks, axis):
    me = lax.axis_index(axis)
    rows = blocks[0].shape[0]
    whole = jnp.zeros((rows * len(blocks),) + blocks[0].shape[1:], blocks[0].dtype)
    for r, block in enumerate(blocks):
        whole = lax.dynamic_update_slice_in_dim(whole, block, (me ^ r) * rows, 0)
    return whole


def halves(order):
    rest = order[1:]
    found = []
    for r in range(2 << len(rest)):
        place = sum(((r & bit) != 0) << (len(rest) - 1 - i) for i, bit in enumerate(rest))
        found.append((r, bool(r & order[0]), place))
    return found


def crossed(r):
    return r // 4 * 4 + r % 2 * 2 + r // 2 % 2


def partner(me, place, r, turn=0):
    if crossed(r) == r:
        return place ^ r
    return place ^ jnp.where((me + turn) % 2 == 1, crossed(r), r)


def trade(value, axis, bit, turn):
    if axis != "dp":
        return swap(value, axis, bit)
    copies, experts = lax.axis_size("dp"), lax.axis_size("expert")
    pairs = []
    for d in range(copies):
        for e in range(experts):
            other = d ^ (crossed(bit) if (e + turn) % 2 else bit)
            pairs.append((d * experts + e, other * experts + e))
    return lax.ppermute(value, ("dp", "expert"), pairs)


class Halving:
    def __init__(self, keep, send, axis, order, turn=0):
        self.axis = axis
        self.turn = turn
        self.order = order[1:]
        self.count = keep.shape[0]
        self.terms = [keep, trade(send, axis, order[0], turn)]

    def wait(self, *others):
        self.terms[-1] = after(self.terms[-1], *others)
        return self

    def exchange(self):
        half = self.count // 2
        sent = sum(term[half : self.count].astype(F32) for term in self.terms).astype(BF16)
        self.terms.append(trade(sent, self.axis, self.order.pop(0), self.turn))
        self.count = half
        return sent

    def arrived(self):
        return self.terms[-1]

    def rest(self):
        while self.order:
            self.exchange()
        return self.terms


def added(terms):
    return sum(term[0].astype(F32) for term in terms)


def dot(left, right):
    return lax.dot_general(left, right, (((1,), (0,)), ((), ())), preferred_element_type=F32)


def dot_t(left, right):
    return lax.dot_general(left, right, (((1,), (1,)), ((), ())), preferred_element_type=F32)


def t_dot(left, right):
    return lax.dot_general(left, right, (((0,), (0,)), ((), ())), preferred_element_type=F32)


def local(body, outs, scratch=(), scalars=1):
    def call(*args):
        return pl.pallas_call(
            body,
            out_shape=[jax.ShapeDtypeStruct(shape, kind) for shape, kind in outs],
            in_specs=[SMEM] * scalars + [VMEM] * (len(args) - scalars),
            out_specs=[VMEM] * len(outs),
            scratch_shapes=[pltpu.VMEM(shape, kind) for shape, kind in scratch],
            compiler_params=pltpu.CompilerParams(vmem_limit_bytes=LIMIT),
            cost_estimate=pl.CostEstimate(flops=10**8, bytes_accessed=10**5, transcendentals=0),
        )(*args)

    return call


def moving(body, outs, scratch, copies, scalars=1):
    def call(*args):
        return pl.pallas_call(
            body,
            out_shape=[jax.ShapeDtypeStruct(shape, kind) for shape, kind in outs],
            in_specs=[SMEM] * scalars + [ANY] * (len(args) - scalars),
            out_specs=[ANY] * len(outs),
            scratch_shapes=[pltpu.VMEM(shape, kind) for shape, kind in scratch]
            + [pltpu.SemaphoreType.DMA((copies,))],
            compiler_params=pltpu.CompilerParams(vmem_limit_bytes=LIMIT),
            cost_estimate=pl.CostEstimate(flops=10**8, bytes_accessed=10**5, transcendentals=0),
        )(*args)

    return call


def mixed_kernel(body, outs, scratch, copies, scalars=1):
    def call(*args):
        return pl.pallas_call(
            body,
            out_shape=[jax.ShapeDtypeStruct(shape, kind) for shape, kind in outs],
            in_specs=[SMEM] * scalars + [ANY] * (len(args) - scalars),
            out_specs=[VMEM] * len(outs),
            scratch_shapes=[pltpu.VMEM(shape, kind) for shape, kind in scratch]
            + [pltpu.SemaphoreType.DMA((copies,))],
            compiler_params=pltpu.CompilerParams(vmem_limit_bytes=LIMIT),
            cost_estimate=pl.CostEstimate(flops=10**8, bytes_accessed=10**5, transcendentals=0),
        )(*args)

    return call


class Moves:
    def __init__(self, sems):
        self.sems = sems
        self.used = 0
        self.open = []

    def start(self, source, target):
        move = pltpu.make_async_copy(source, target, self.sems.at[self.used])
        self.used += 1
        move.start()
        self.open.append(move)
        return move

    def wait(self, *moves):
        for move in moves:
            move.wait()
            self.open = [other for other in self.open if other is not move]

    def finish(self):
        self.wait(*list(self.open))


def rows_at(place, count):
    return pl.ds(pl.multiple_of(place * count, count), count)


def normal(values):
    factor = lax.rsqrt(jnp.mean(values * values, -1, keepdims=True) + 1e-06)
    return values * factor, factor


def normal_back(grad_normed, unit, factor, gain):
    grad_unit = grad_normed * gain
    return factor * (grad_unit - unit * jnp.mean(grad_unit * unit, -1, keepdims=True))


def turned(pairs, cosines, sines):
    span = pairs.shape[1]
    lane = lax.broadcasted_iota(jnp.int32, pairs.shape, 1)
    first = lane % HEAD_DIM < HEAD_DIM // 2
    partner = jnp.where(
        first, pltpu.roll(pairs, span - HEAD_DIM // 2, 1), pltpu.roll(pairs, HEAD_DIM // 2, 1)
    )
    return pairs * cosines + partner * sines


def rotary_tables(count):
    halfway = HEAD_DIM // 2
    frequency = np.power(10000.0, -np.arange(halfway, dtype=np.float32) / halfway)
    angles = np.arange(count, dtype=np.float32)[:, None] * frequency.astype(np.float32)[None, :]
    cosines, sines = np.cos(angles), np.sin(angles)
    cosines = np.tile(cosines, (1, 4)).astype(np.float32)
    sines = np.concatenate([-sines, sines, -sines, sines], 1).astype(np.float32)
    return jnp.asarray(cosines), jnp.asarray(sines)


def widened(table, span):
    return jnp.concatenate([table] * (span // LANES), 1)


def reach(block, experts, tokens):
    return min(block + 2, experts) * tokens


def pack_first_body(experts, where, gain1, gain2, router, qkv, result, wide):
    slab, width = result.shape[0], qkv.shape[1] // 3
    columns = (result.shape[1] - VECTORS) // 3
    wide[...] = jnp.zeros_like(wide)
    wide[0:1, :slab] = gain1[...].astype(F32)
    wide[1:2, :slab] = gain2[...].astype(F32)
    wide[SLOTS : SLOTS + router.shape[0], :slab] = router[...].astype(F32)
    result[:, 3 * columns :] = wide[...].T[:slab, :VECTORS].astype(BF16)
    for e in range(experts):

        @pl.when(where[0] == e)
        def _():
            for i in range(3):
                start = min(e * columns, width)
                stop = min(start + columns, width)
                at = i * columns
                if stop > start:
                    result[:, at : at + stop - start] = qkv[:, i * width + start : i * width + stop]
                if stop - start < columns:
                    blank = jnp.zeros((slab, columns - stop + start), BF16)
                    result[:, at + stop - start : at + columns] = blank


def pack_units_body(experts, copies, where, gate, up, down, result):
    slab, width = gate.shape[0], down.shape[1]
    units = down.shape[0] // experts
    total = copies * units
    for e in range(experts):

        @pl.when(where[0] == e)
        def _():
            for k, matrix in enumerate((gate, up)):
                parts = [
                    matrix[:, (d * experts + e) * units : (d * experts + e + 1) * units]
                    for d in range(copies)
                ]
                result[:slab, k * total : (k + 1) * total] = jnp.concatenate(parts, 1)
            result[slab:, :width] = down[e * units : (e + 1) * units, :]
            if result.shape[1] > width:
                result[slab:, width:] = jnp.zeros((units, result.shape[1] - width), BF16)


def attend_body(experts, copies, blocks, *refs):
    where, starts, cosine_in, sine_in = refs[:4]
    x_refs, w_refs = refs[4 : 4 + experts], refs[4 + experts : 4 + experts + blocks]
    refs = refs[4 + experts + blocks :]
    n1_out, q_out, k_out, v_out, probs_out, mixed_out, weight_out, vectors_out = refs[:8]
    cosine_table, sine_table, x, n1, q, k, v, probs, mixed, weight, vectors, sems = refs[8:]
    moves = Moves(sems)
    me, place = where[0], where[1]
    tokens = x_refs[0].shape[0]
    columns = q.shape[1]
    own_heads = columns // HEAD_DIM
    slab = w_refs[0].shape[0]
    if blocks == 1:
        arriving = [moves.start(w_refs[0], weight)]
    else:
        arriving = [
            moves.start(w_refs[r], weight.at[rows_at(place ^ r, slab), :]) for r in range(blocks)
        ]
    tables = [moves.start(cosine_in, cosine_table), moves.start(sine_in, sine_table)]
    rows_in = [moves.start(x_refs[r], x.at[r]) for r in range(experts)]
    moves.wait(*arriving)
    vectors[...] = weight[:, 3 * columns :].astype(F32).T
    moves.start(weight, weight_out)
    moves.start(vectors, vectors_out)
    gain = vectors[0:1, :]
    moves.wait(*tables)
    for r in range(experts):
        rows = rows_at(me ^ r, tokens)
        moves.wait(rows_in[r])
        unit, _ = normal(x[r].astype(F32))
        normed = (unit * gain).astype(BF16)
        n1[rows, :] = normed
        projected = dot(normed, weight[:, : 3 * columns])
        cosines = widened(cosine_table[rows, :], 2 * columns)
        sines = widened(sine_table[rows, :], 2 * columns)
        pair = turned(projected[:, : 2 * columns], cosines, sines).astype(BF16)
        q[rows, :] = pair[:, :columns] * HEAD_DIM ** (-0.5)
        k[rows, :] = pair[:, columns:]
        v[rows, :] = projected[:, 2 * columns :].astype(BF16)
    for held, result in ((n1, n1_out), (q, q_out), (k, k_out), (v, v_out)):
        moves.start(held, result)
    pieces = starts.shape[1]
    leaving = {}
    for block in range(experts):
        seen = reach(block, experts, tokens)
        rows = slice(block * tokens, (block + 1) * tokens)
        query_pos = block * tokens + lax.broadcasted_iota(jnp.int32, (tokens, 1), 0)
        key_pos = lax.broadcasted_iota(jnp.int32, (1, seen), 1)
        query_piece = jnp.full((tokens, 1), -1, jnp.int32)
        key_piece = jnp.full((1, seen), -2, jnp.int32)
        for j in range(pieces):
            start = starts[0, j]
            query_piece = jnp.where(
                (query_pos >= start) & (query_pos < start + PIECE), j, query_piece
            )
            key_piece = jnp.where((key_pos >= start) & (key_pos < start + PIECE), j, key_piece)
        bias = jnp.where((key_pos <= query_pos) | (query_piece == key_piece), 0.0, -1e30)
        slot = block % 2
        if block >= 2:
            moves.wait(leaving[block - 2])
        for h in range(own_heads):
            head = slice(h * HEAD_DIM, (h + 1) * HEAD_DIM)
            scores = dot_t(q[rows, head], k[:seen, head]) + bias
            powers = jnp.exp(scores - jnp.max(scores, -1, keepdims=True))
            share = (powers * (1.0 / jnp.sum(powers, -1, keepdims=True))).astype(BF16)
            probs[slot, h, :, :seen] = share
            mixed[rows, head] = dot(share, v[:seen, head]).astype(BF16)
        leaving[block] = moves.start(
            probs.at[slot, :, :, :seen], probs_out.at[:, rows, :seen]
        )
    moves.start(mixed, mixed_out)
    moves.finish()


def settle_body(experts, blocks, *refs):
    where, vectors_in = refs[:2]
    x_refs = refs[2 : 2 + experts]
    dy_refs = refs[2 + experts : 2 + 2 * experts]
    m_refs = refs[2 + 2 * experts : 2 + 3 * experts]
    o_refs, refs = refs[2 + 3 * experts :][:blocks], refs[2 + 3 * experts + blocks :]
    n2_out, n2_turned_out, dy_out, gates_out, own_resid_out, own_n2_out, own_gates_out, matrix_out = refs[:8]
    vectors, x, dy, mixed, out_matrix, n2, n2_turned, gates, own_resid, sems = refs[8:]
    moves = Moves(sems)
    me, place = where[0], where[1]
    slab = o_refs[0].shape[0]
    tokens, width = x_refs[0].shape
    columns = m_refs[0].shape[1]
    mixed_in = [moves.start(m_refs[j], mixed.at[j]) for j in range(experts)]
    vectors_move = moves.start(vectors_in, vectors)
    x_in = [moves.start(x_refs[r], x.at[r]) for r in range(experts)]
    dy_in = [moves.start(dy_refs[r], dy.at[r]) for r in range(experts)]
    if blocks == 1:
        matrix_in = [moves.start(o_refs[0], out_matrix)]
    else:
        matrix_in = [
            moves.start(o_refs[r], out_matrix.at[rows_at(place ^ r, slab), :])
            for r in range(blocks)
        ]
    moves.wait(*matrix_in, *mixed_in, vectors_move)
    moves.start(out_matrix, matrix_out)
    gain = vectors[1:2, :]
    router = vectors[SLOTS : 2 * SLOTS, :].astype(BF16)
    for r in range(experts):
        rows = rows_at(me ^ r, tokens)
        moves.wait(x_in[r], dy_in[r])
        moves.start(dy.at[r, :, :width], dy_out.at[rows, :])
        resid = x[r].astype(F32)
        for j in range(experts):
            resid += dot(mixed[j, rows, :], out_matrix[rows_at(me ^ j, columns), :])
        unit, _ = normal(resid)
        normed = (unit * gain).astype(BF16)
        logits = dot_t(normed, router)
        chosen = dy[r, :, width : width + SLOTS].astype(F32)
        masked = jnp.where(chosen > 0.0, logits, -1e30)
        powers = chosen * jnp.exp(masked - jnp.max(masked, -1, keepdims=True))
        n2[r] = normed
        n2_turned[r] = normed.astype(F32).T.astype(BF16)
        gates[r] = powers / jnp.sum(powers, -1, keepdims=True)
        moves.start(n2.at[r], n2_out.at[rows, :])
        moves.start(n2_turned.at[r], n2_turned_out.at[:, rows])
        moves.start(gates.at[r], gates_out.at[rows, :])
        if r == 0:
            own_resid[...] = resid
            moves.start(own_resid, own_resid_out)
            moves.start(n2.at[0], own_n2_out)
            moves.start(gates.at[0], own_gates_out)
    moves.finish()


def unit_tile(me, fresh, n2, dy, gates, wg, wu, wd, y, gx, gg, hidden_s, gate_s, up_s):
    chunk = 512 if n2.shape[0] <= 1024 else 256

    def step(c, carry):
        rows = pl.ds(pl.multiple_of(c * chunk, chunk), chunk)
        x, g = n2[rows, :], dy[rows, :]
        gate_pre = dot(x, wg[...])
        up_pre = dot(x, wu[...])
        raw = dot_t(g, wd[...])
        logistic = lax.logistic(gate_pre)
        swish = gate_pre * logistic
        slope = logistic + swish * (1.0 - logistic)
        hidden = swish * up_pre
        if gates is not None:
            lane = lax.broadcasted_iota(jnp.int32, (chunk, SLOTS), 1)
            scale = jnp.sum(jnp.where(lane == me, gates[rows, :], 0.0), -1, keepdims=True)
            gg[rows, :] += jnp.sum(hidden * raw, -1, keepdims=True)
            hidden = hidden * scale
            raw = raw * scale
        hidden = hidden.astype(BF16)
        grad_gate = (raw * up_pre * slope).astype(BF16)
        grad_up = (raw * swish).astype(BF16)
        hidden_s[rows, :] = hidden
        gate_s[rows, :] = grad_gate
        up_s[rows, :] = grad_up
        out = dot(hidden, wd[...])
        back = dot_t(grad_gate, wg[...]) + dot_t(grad_up, wu[...])
        if fresh:
            y[rows, :] = out
            gx[rows, :] = back
        else:
            y[rows, :] += out
            gx[rows, :] += back
        return carry

    lax.fori_loop(0, n2.shape[0] // chunk, step, 0)


def shared_body(experts, copies, blocks, *refs):
    where, n2_in, n2_turned_in, dy_in, y_in, gx_in, gg_in = refs[:7]
    b_refs, refs = refs[7 : 7 + blocks], refs[7 + blocks :]
    keep_out, send_out, y_keep_out, y_send_out, gx_keep_out, gx_send_out = refs[:6]
    n2, n2_turned, dy, y, gx, y_more, gx_more, gg, wg, wu, wd = refs[6:17]
    hidden_s, gate_s, up_s, grad_gate, grad_up, grad_down = refs[17:23]
    keep, send, y_keep, y_send, gx_keep, gx_send, sems = refs[23:]
    moves = Moves(sems)
    me, place = where[0], where[1]
    width = n2.shape[1]
    total = wg.shape[1]
    units = total // copies
    slab = width // copies
    tokens = y_keep.shape[1]
    if blocks == 2:
        places = [
            (b_refs[0].at[:, :total], wg),
            (b_refs[0].at[:, total : 2 * total], wu),
            (b_refs[1], wd),
        ]
    else:
        places = []
        for r in range(copies):
            rows = slice(r * slab, (r + 1) * slab)
            places.append((b_refs[0].at[r, :slab, :total], wg.at[rows, :]))
            places.append((b_refs[0].at[r, :slab, total : 2 * total], wu.at[rows, :]))
            rows = slice(r * units, (r + 1) * units)
            places.append((b_refs[0].at[r, slab:, :width], wd.at[rows, :]))
    arriving = [moves.start(source, target) for source, target in places]
    arriving += [moves.start(n2_in, n2), moves.start(dy_in, dy)]
    moves.wait(*arriving)
    sums_in = [moves.start(gx_in, gx_more), moves.start(gg_in, gg), moves.start(y_in, y_more)]
    turned_in = moves.start(n2_turned_in, n2_turned)
    unit_tile(None, True, n2, dy, None, wg, wu, wd, y, gx, None, hidden_s, gate_s, up_s)
    moves.wait(*sums_in)
    for r, leaves, k in halves(bits_of(experts)):
        rows = rows_at(me ^ r, tokens)
        half = gx_send if leaves else gx_keep
        half[k, :, :width] = (gx[rows, :] + gx_more[rows, :]).astype(BF16)
        lane = lax.broadcasted_iota(jnp.int32, (tokens, LANES), 1)
        whole = gg[rows, :]
        coarse = whole.astype(BF16).astype(F32)
        half[k, :, width:] = (
            jnp.where(lane == me, coarse, 0.0)
            + jnp.where(lane == me + SLOTS, whole - coarse, 0.0)
        ).astype(BF16)
        half = y_send if leaves else y_keep
        half[k] = (y[rows, :] + y_more[rows, :]).astype(BF16)
    moves.start(gx_send, gx_send_out)
    moves.start(gx_keep, gx_keep_out)
    moves.start(y_send, y_send_out)
    moves.start(y_keep, y_keep_out)
    moves.wait(turned_in)
    grad_gate[...] = dot(n2_turned[...], gate_s[...])
    grad_up[...] = dot(n2_turned[...], up_s[...])
    grad_down[...] = t_dot(hidden_s[...], dy[...])
    for r, leaves, k in halves(bits_of(copies)):
        half = send if leaves else keep
        rows = rows_at(partner(me, place, r, 1), slab)
        half[k, :slab, :total] = grad_gate[rows, :].astype(BF16)
        half[k, :slab, total : 2 * total] = grad_up[rows, :].astype(BF16)
        rows = rows_at(partner(me, place, r, 1), units)
        half[k, slab:, :width] = grad_down[rows, :].astype(BF16)
        spare = half.shape[2] - width
        if spare:
            half[k, slab:, width:] = jnp.zeros((units, spare), BF16)
        spare = half.shape[2] - 2 * total
        if spare:
            half[k, :slab, 2 * total :] = jnp.zeros((slab, spare), BF16)
    moves.start(send, send_out)
    moves.start(keep, keep_out)
    moves.finish()


def expert_body(copies, last, *refs):
    where, n2_in, n2_turned_in, dy_in, gates_in, wg_in, wu_in, wd_in = refs[:8]
    refs = refs[8:]
    if last:
        y_in, gx_in, gg_in, down_in = refs[:4]
        refs = refs[4:]
    keep_out, send_out, y_out, gx_out, gg_out, down_out = refs[:6]
    refs = refs[6:]
    if last:
        down_send_out, refs = refs[0], refs[1:]
    n2, n2_turned, dy, gates, y, gx, gg, down, wg, wu, wd = refs[:11]
    hidden_s, gate_s, up_s, grad_gate, grad_up, keep, send = refs[11:18]
    if last:
        down_keep, down_send, gg_more = refs[18:21]
        gx_more, y_more = refs[21], refs[-2]
        roomy = y_more is not gx_more
    moves = Moves(refs[-1])
    me, place = where[0], where[1]
    slab = keep.shape[2]
    tile = wg.shape[2]
    hidden = wd_in.shape[0]
    steps = hidden // 2 // tile
    first = hidden // 2 if last else 0
    units = [slice(first + s * tile, first + (s + 1) * tile) for s in range(steps)]

    def fetch(step):
        slot = step % 2
        return [
            moves.start(wg_in.at[:, units[step]], wg.at[slot]),
            moves.start(wu_in.at[:, units[step]], wu.at[slot]),
            moves.start(wd_in.at[units[step], :], wd.at[slot]),
        ]

    weights = {0: fetch(0)}
    arriving = [moves.start(n2_in, n2), moves.start(dy_in, dy), moves.start(gates_in, gates)]
    gg[...] = jnp.zeros_like(gg)
    moves.wait(*arriving)
    turned_in = [moves.start(n2_turned_in, n2_turned)]
    weights[1] = fetch(1)
    if last:
        sums_in = [moves.start(gx_in, gx_more), moves.start(gg_in, gg_more)]
        if roomy:
            sums_in.append(moves.start(y_in, y_more))
        earlier = moves.start(down_in, down.at[: hidden // 2, :])
    leaving = {}
    for step in range(steps):
        slot = step % 2
        moves.wait(*weights[step])
        unit_tile(
            me, step == 0, n2, dy, gates, wg.at[slot], wu.at[slot], wd.at[slot],
            y, gx, gg, hidden_s, gate_s, up_s,
        )
        if 1 <= step and step + 1 < steps:
            weights[step + 1] = fetch(step + 1)
        elif step == 0 and steps > 2:
            weights[2] = fetch(2)
        if step == steps - 1:
            if last:
                moves.wait(*sums_in)
                gg[...] += gg_more[...]
                gx[...] += gx_more[...]
                if not roomy:
                    moves.wait(moves.start(y_in, y_more))
                y[...] += y_more[...]
            moves.start(y, y_out)
            moves.start(gx, gx_out)
            moves.start(gg, gg_out)
        moves.wait(*turned_in)
        turned_in = []
        grad_gate[...] = dot(n2_turned[...], gate_s[...])
        grad_up[...] = dot(n2_turned[...], up_s[...])
        down[units[step] if last else slice(step * tile, (step + 1) * tile), :] = t_dot(
            hidden_s[...], dy[...]
        ).astype(BF16)
        if step >= 2:
            moves.wait(*leaving[step - 2])
        for r, leaves, k in halves(bits_of(copies)):
            half = send if leaves else keep
            rows = rows_at(partner(me, place, r), slab)
            half[slot, k, :, :tile] = grad_gate[rows, :].astype(BF16)
            half[slot, k, :, tile:] = grad_up[rows, :].astype(BF16)
        at = slice(2 * step * tile, 2 * (step + 1) * tile)
        leaving[step] = [
            moves.start(send.at[slot], send_out.at[:, :, at]),
            moves.start(keep.at[slot], keep_out.at[:, :, at]),
        ]
    if last:
        moves.wait(earlier)
        per = hidden // copies
        for r, leaves, k in halves(bits_of(copies)):
            half = down_send if leaves else down_keep
            half[k] = down[rows_at(partner(me, place, r, 1), per), :]
        moves.start(down_send, down_send_out)
        moves.start(down_keep, down_out)
    else:
        moves.start(down, down_out)
    moves.finish()


def home_body(terms, *refs):
    where, vectors = refs[:2]
    parts = refs[2 : 2 + terms]
    own_resid, own_n2, own_gates, cotangent, attended, grad_resid, sums = refs[2 + terms :]
    width = own_n2.shape[1]
    total = added(parts)
    grad_gates = total[:, width : width + SLOTS] + total[:, width + SLOTS : width + 2 * SLOTS]
    gates = own_gates[...]
    grad_logits = (
        gates * (grad_gates - jnp.sum(gates * grad_gates, -1, keepdims=True))
    ).astype(BF16)
    grad_normed = total[:, :width] + dot(
        grad_logits, vectors[SLOTS : 2 * SLOTS, :].astype(BF16)
    )
    unit, factor = normal(own_resid[...])
    sums[0:SLOTS, :] = jnp.broadcast_to(
        jnp.sum(grad_normed * unit, 0, keepdims=True), (SLOTS, width)
    )
    sums[SLOTS : 2 * SLOTS, :] = t_dot(grad_logits, own_n2[...])
    back = cotangent[...].astype(F32) + normal_back(grad_normed, unit, factor, vectors[1:2, :])
    grad_resid[...] = back
    attended[...] = back.astype(BF16)


def grad_share(matrix, start, me, count, experts):
    if count % 8 == 0:
        return matrix[pl.ds(pl.multiple_of(start + me * count, count), count), :]
    rows = matrix[pl.ds(pl.multiple_of(start, 8), count * experts), :]
    picked = rows[:count]
    for e in range(1, experts):
        picked = jnp.where(me == e, rows[e * count : (e + 1) * count], picked)
    return picked


def attend_back_body(experts, copies, *refs):
    where, cosine_in, sine_in, sums_in = refs[:4]
    a_refs = refs[4 : 4 + experts]
    m_refs = refs[4 + experts : 4 + 2 * experts]
    x_refs = refs[4 + 2 * experts : 4 + 3 * experts]
    refs = refs[4 + 3 * experts :]
    matrix_in, q_in, k_in, v_in, n1_in, weight_in, probs_in = refs[:7]
    keep_out, send_out, gn_keep_out, gn_send_out = refs[7:11]
    refs = refs[11:]
    cosine_table, sine_table, sums, attended, mixed, x, out_matrix, q, k, v, n1, weight, probs = refs[:13]
    grad_q, grad_k, grad_v, grad_projected, grad_out, grad_qkv, extra, side = refs[13:21]
    keep, send, gn_keep, gn_send, sems = refs[21:]
    moves = Moves(sems)
    me, place = where[0], where[1]
    tokens, width = x_refs[0].shape
    columns = q.shape[1]
    own_heads = columns // HEAD_DIM
    root = HEAD_DIM ** (-0.5)

    def fetch(block):
        seen = reach(block, experts, tokens)
        rows = slice(block * tokens, (block + 1) * tokens)
        return moves.start(
            probs_in.at[:, rows, :seen], probs.at[block % 2, :, :, :seen]
        )

    needed = [
        moves.start(a_refs[r], attended.at[rows_at(me ^ r, tokens), :]) for r in range(experts)
    ]
    needed += [moves.start(matrix_in, out_matrix)]
    needed += [moves.start(source, held) for source, held in ((v_in, v), (k_in, k), (q_in, q))]
    shares = {0: fetch(0), 1: fetch(1)}
    mixed_in = [moves.start(m_refs[j], mixed.at[j]) for j in range(experts)]
    later = [moves.start(weight_in, weight), moves.start(cosine_in, cosine_table)]
    later += [moves.start(sine_in, sine_table), moves.start(sums_in, sums)]
    x_in = [moves.start(x_refs[r], x.at[r]) for r in range(experts)]
    n1_move = moves.start(n1_in, n1)
    grad_k[...] = jnp.zeros_like(grad_k)
    grad_v[...] = jnp.zeros_like(grad_v)
    moves.wait(*needed)
    own_out = out_matrix[rows_at(me, columns), :]
    for block in range(experts):
        seen = reach(block, experts, tokens)
        rows = slice(block * tokens, (block + 1) * tokens)
        slot = block % 2
        grad_mixed = dot_t(attended[rows, :], own_out).astype(BF16)
        moves.wait(shares[block])
        for h in range(own_heads):
            head = slice(h * HEAD_DIM, (h + 1) * HEAD_DIM)
            gm = grad_mixed[:, head]
            share = probs[slot, h, :, :seen]
            wide = share.astype(F32)
            grad_probs = dot_t(gm, v[:seen, head])
            delta = jnp.sum(wide * grad_probs, -1, keepdims=True)
            grad_scores = (wide * (grad_probs - delta)).astype(BF16)
            grad_q[rows, head] = dot(grad_scores, k[:seen, head]) * root
            grad_k[:seen, head] += t_dot(grad_scores, q[rows, head])
            grad_v[:seen, head] += t_dot(share, gm)
        if block + 2 < experts:
            shares[block + 2] = fetch(block + 2)
    moves.wait(*later)
    gain_sum = jnp.zeros((1, width), F32)
    for r in list(range(1, experts, 2)) + list(range(0, experts, 2)):
        rows = rows_at(me ^ r, tokens)
        pair = jnp.concatenate([grad_q[rows, :], grad_k[rows, :]], 1)
        cosines = widened(cosine_table[rows, :], 2 * columns)
        sines = widened(sine_table[rows, :], 2 * columns)
        back = turned(pair, cosines, -sines).astype(BF16)
        grad_projected[rows, : 2 * columns] = back
        grad_projected[rows, 2 * columns :] = grad_v[rows, :].astype(BF16)
        grad_normed = dot_t(grad_projected[rows, :], weight[:, : 3 * columns])
        moves.wait(x_in[r])
        unit, _ = normal(x[r].astype(F32))
        gain_sum += jnp.sum(grad_normed * unit, 0, keepdims=True)
        _, leaves, spot = halves(bits_of(experts))[r]
        half, result = (gn_send, gn_send_out) if leaves else (gn_keep, gn_keep_out)
        half[spot] = grad_normed.astype(BF16)
        moves.start(half.at[spot], result.at[spot])
    moves.wait(n1_move, *mixed_in)
    for r in range(experts):
        grad_out[rows_at(me ^ r, columns), :] = t_dot(mixed[r], attended[...])
    grad_qkv[...] = t_dot(n1[...], grad_projected[...])
    extra[...] = jnp.zeros_like(extra)
    extra[0:1, :] = gain_sum
    extra[1:2, :] = sums[0:1, :]
    extra[SLOTS : 2 * SLOTS, :] = sums[SLOTS : 2 * SLOTS, :]
    side[...] = extra[...].T
    slab = width // copies
    share_rows = slab // experts
    spare = keep.shape[1] - slab
    for r, leaves, place_of in halves(bits_of(copies)):
        half = send if leaves else keep
        owner = partner(me, place, r)
        rows = rows_at(owner, slab)
        half[place_of, :slab, :LANES] = side[rows, :].astype(BF16)
        half[place_of, :slab, LANES : LANES + 3 * columns] = grad_qkv[rows, :].astype(BF16)
        block = grad_share(grad_out, owner * slab, me, share_rows, experts)
        if spare > share_rows:
            block = jnp.concatenate([block, jnp.zeros((spare - share_rows, width), F32)], 0)
        half[place_of, slab:, :width] = block.astype(BF16)
        if half.shape[2] > LANES + 3 * columns:
            half[place_of, :slab, LANES + 3 * columns :] = jnp.zeros(
                (slab, half.shape[2] - LANES - 3 * columns), BF16
            )
    moves.start(send, send_out)
    moves.start(keep, keep_out)
    moves.finish()


def finish_body(terms, *refs):
    where, vectors, x = refs[:3]
    parts = refs[3 : 3 + terms]
    grad_resid, result = refs[3 + terms :]
    total = added(parts)
    unit, factor = normal(x[...].astype(F32))
    back = normal_back(total, unit, factor, vectors[0:1, :])
    result[...] = (grad_resid[...] + back).astype(BF16)


def collect_body(tile, *refs):
    count = (len(refs) - 6) // 2
    where, terms = refs[0], refs[1 : 1 + 2 * count]
    gate_out, up_out, held, gate, up, sems = refs[1 + 2 * count :]
    moves = Moves(sems)
    arriving = [moves.start(term.at[0], held.at[i]) for i, term in enumerate(terms)]
    steps = gate.shape[1] // tile
    moves.wait(*arriving)
    for step in range(steps):
        which, at = divmod(step, steps // 2)
        for k, result in enumerate((gate, up)):
            lanes = slice((2 * at + k) * tile, (2 * at + k + 1) * tile)
            total = held[which * count, :, lanes].astype(F32)
            for i in range(1, count):
                total += held[which * count + i, :, lanes].astype(F32)
            result[:, step * tile : (step + 1) * tile] = total
    moves.start(gate, gate_out)
    moves.start(up, up_out)
    moves.finish()


def shares_body(experts, top, bottom, *refs):
    where, terms = refs[0], refs[1 : -4 - experts]
    pieces, rest_out = refs[-4 - experts : -4], refs[-4]
    held, total, sems = refs[-3:]
    moves = Moves(sems)
    me = where[0]
    arriving = [moves.start(term.at[0], held.at[i]) for i, term in enumerate(terms)]
    moves.wait(*arriving)
    whole = held[0].astype(F32)
    for i in range(1, len(terms)):
        whole += held[i].astype(F32)
    total[...] = whole
    rest_out[...] = total[top : top + bottom, : rest_out.shape[1]]
    count = top // experts
    for r in range(experts):
        block = total[rows_at(me ^ r, count), : pieces[r].shape[1]]
        pieces[r][...] = block.astype(BF16)


def assemble_body(experts, copies, *refs):
    where = refs[0]
    units_in, heads_in = refs[1 : 1 + experts], refs[1 + experts : 1 + 2 * experts]
    gate, up, qkv, gain1, gain2, router = refs[1 + 2 * experts :]
    total = units_in[0].shape[1] // 2
    units = total // copies
    columns = (heads_in[0].shape[1] - LANES) // 3
    width = qkv.shape[1] // 3
    side = heads_in[0][:, :LANES].astype(F32)
    for r in range(1, experts):
        side += heads_in[r][:, :LANES].astype(F32)
    rows = side.T
    gain1[...] = rows[0:1, :]
    gain2[...] = rows[1:2, :]
    router[...] = rows[SLOTS : SLOTS + experts, :]
    for e in range(experts):

        @pl.when(where[0] == e)
        def _():
            for k, result in enumerate((gate, up)):
                sources = [units_in[e ^ other][...].astype(F32) for other in range(experts)]
                parts = []
                for d in range(copies):
                    at = k * total + d * units
                    parts += [source[:, at : at + units] for source in sources]
                result[...] = jnp.concatenate(parts, 1)
            for i in range(3):
                at = LANES + i * columns
                parts = [
                    heads_in[e ^ other][:, at : at + columns].astype(F32)
                    for other in range(experts)
                ]
                qkv[:, i * width : (i + 1) * width] = jnp.concatenate(parts, 1)


def expert_half(operands, state, copies, tile, last):
    n2, wg = operands[1], operands[5]
    length, width = n2.shape
    hidden = wg.shape[1]
    slab, per = width // copies, hidden // copies
    half = (copies // 2, slab, hidden)
    sums = (length, width)
    outs = [(half, BF16), (half, BF16), (sums, F32), (sums, F32), ((length, LANES), F32)]
    down = (hidden if last else hidden // 2, width)
    slot = (2, copies // 2, slab, 2 * tile)
    scratch = [(sums, BF16), ((width, length), BF16), (sums, BF16), ((length, SLOTS), F32)]
    scratch += [(sums, F32)] * 2 + [((length, LANES), F32), (down, BF16)]
    scratch += [((2, width, tile), BF16)] * 2 + [((2, tile, width), BF16)]
    scratch += [((length, tile), BF16)] * 3 + [((width, tile), F32)] * 2 + [(slot, BF16)] * 2
    if last:
        final = [((copies // 2, per, width), BF16)] * 2
        outs += final
        scratch += final + [((length, LANES), F32)] + [(sums, F32)] * (2 if tile == 512 else 1)
    else:
        outs.append((down, BF16))
    steps = hidden // 2 // tile
    body = functools.partial(expert_body, copies, last)
    return moving(body, outs, scratch, 16 + 5 * steps)(*operands, *state)


def rows_to_owners(value):
    count = lax.axis_size("expert")
    me = lax.axis_index("expert")
    parts = value.reshape((count, value.shape[0] // count) + value.shape[1:])
    found = []
    for r in range(count):
        part = lax.dynamic_index_in_dim(parts, me ^ r, 0, keepdims=False)
        found.append((swap(part, "expert", r) if r else part)[None])
    return in_order(found, "expert")


def shards(
    inputs,
    norm1_gain,
    qkv_weight,
    out_weight,
    norm2_gain,
    router_weight,
    shared_gate,
    shared_up,
    shared_down,
    expert_gate,
    expert_up,
    expert_down,
    expert_ids,
    piece_starts,
    cotangent,
):
    tokens, width = inputs.shape[1:]
    heads = width // HEAD_DIM
    experts = lax.axis_size("expert")
    copies = lax.axis_size("dp")
    me = lax.axis_index("expert")
    place = lax.axis_index("dp")
    where = jnp.stack([me, place]).astype(jnp.int32)
    length = tokens * experts
    slab = width // copies
    own_heads = -(-heads // experts)
    columns = own_heads * HEAD_DIM
    padded = experts * columns
    units = shared_down.shape[0] // experts
    total = copies * units
    wide = max(2 * total, width)
    apart = slab % 16 == 0 and units % 16 == 0 and padded == width
    small = length <= 1024
    tile = 512 if small else 256

    first = local(
        functools.partial(pack_first_body, experts),
        [((slab, 3 * columns + VECTORS), BF16)],
        [((LANES, LANES), F32)],
    )(where, norm1_gain[None], norm2_gain[None], router_weight.T, qkv_weight)[0]
    x = far_blocks("expert", inputs[0])
    first = far_blocks("dp", first)
    named = jnp.any(
        expert_ids[0][:, :, None] == jnp.arange(LANES, dtype=jnp.int32)[None, None, :], 1
    ).astype(BF16)
    dy_own = jnp.concatenate([cotangent[0], named], 1)
    dy_far = far_blocks("expert", after(dy_own, x[2]))
    if apart:
        packed = local(
            functools.partial(pack_units_body, experts, copies), [((slab + units, wide), BF16)]
        )(where, shared_gate, shared_up, shared_down)[0]
        gate = [first[r] for r in first if r]
        first[6] = after(first[6], packed, dy_own)
        first = near_blocks("dp", first)
        gate += [first[1], x[2], packed]
        out_whole = lax.all_gather(after(out_weight, *gate), "dp", axis=0, tiled=True)
        out_blocks = [jnp.pad(out_whole, ((0, padded - width), (0, 0)))]
        shared_blocks = [lax.all_gather(packed, "dp", axis=0, tiled=False)]
    else:
        out_whole = lax.all_gather(out_weight, "dp", axis=0, tiled=True)
        out_blocks = [jnp.pad(out_whole, ((0, padded - width), (0, 0)))]

        def unit_columns(weight):
            split = weight.reshape(slab, copies, experts, units)
            split = lax.dynamic_index_in_dim(split, me, 2, keepdims=False)
            return split.reshape(slab, total)

        top = jnp.concatenate([unit_columns(shared_gate), unit_columns(shared_up)], 1)
        bottom = lax.dynamic_slice_in_dim(shared_down, me * units, units, 0)
        first = [in_order(near_blocks("dp", first), "dp")]
        shared_blocks = [lax.all_gather(part, "dp", axis=0, tiled=True) for part in (top, bottom)]
    x = near_blocks("expert", x)

    cosines, sines = rotary_tables(length)
    projected = [((length, width), BF16)] + [((length, columns), BF16)] * 3
    held = [
        ((length, columns), BF16),
        ((width, 3 * columns + VECTORS), BF16),
        ((VECTORS, width), F32),
    ]
    n1, q, k, v, probs, mixed, weight, vectors = moving(
        functools.partial(attend_body, experts, copies, len(first)),
        projected + [((own_heads, length, length), BF16)] + held,
        [((length, LANES), F32)] * 2
        + [((experts, tokens, width), BF16)]
        + projected
        + [((2, own_heads, tokens, length), BF16)]
        + held,
        len(first) + 2 * experts + 9,
        scalars=2,
    )(where, piece_starts, cosines, sines, *x, *first)
    mixed_blocks = near_blocks("expert", far_blocks("expert", mixed))
    dy_wide = near_blocks("expert", dy_far)
    n2, n2_turned, dy, gates, own_resid, own_n2, own_gates, out_whole = moving(
        functools.partial(settle_body, experts, len(out_blocks)),
        [
            ((length, width), BF16),
            ((width, length), BF16),
            ((length, width), BF16),
            ((length, SLOTS), F32),
            ((tokens, width), F32),
            ((tokens, width), BF16),
            ((tokens, SLOTS), F32),
            ((padded, width), BF16),
        ],
        [
            ((VECTORS, width), F32),
            ((experts, tokens, width), BF16),
            ((experts, tokens, width + LANES), BF16),
            ((experts, length, columns), BF16),
            ((padded, width), BF16),
            ((experts, tokens, width), BF16),
            ((experts, width, tokens), BF16),
            ((experts, tokens, SLOTS), F32),
            ((tokens, width), F32),
        ],
        len(out_blocks) + 7 * experts + 5,
    )(where, vectors, *x, *dy_wide, *mixed_blocks, *out_blocks)

    operands = [where, n2, n2_turned, dy, gates, expert_gate[0], expert_up[0], expert_down[0]]
    a_keep, a_send, y, gx, gg, down = expert_half(operands, (), copies, tile, False)
    far, across = bits_of(copies), bits_of(experts)
    a_sum = Halving(a_keep, a_send, "dp", far)
    b_keep, b_send, y, gx, gg, down_keep, down_send = expert_half(
        operands, (y, gx, gg, down), copies, tile, True
    )
    b_sum = Halving(b_keep, b_send, "dp", far)
    sent = a_sum.wait(b_send).exchange()
    half = ((copies // 2, slab + units, wide), BF16)
    both = [((length, width), F32)] * 2
    final = [
        ((experts // 2, tokens, lanes), BF16)
        for lanes in (width, width, width + LANES, width + LANES)
    ]
    s_keep, s_send, y_keep, y_send, gx_keep, gx_send = moving(
        functools.partial(shared_body, experts, copies, len(shared_blocks)),
        [half, half] + final,
        [((length, width), BF16), ((width, length), BF16), ((length, width), BF16)]
        + both * 2
        + [((length, LANES), F32)]
        + [((width, total), BF16)] * 2
        + [((total, width), BF16)]
        + [((length, total), BF16)] * 3
        + [((width, total), F32)] * 2
        + [((total, width), F32), half, half]
        + final,
        3 * copies + 12,
    )(after(where, sent), n2, n2_turned, dy, y, gx, gg, *shared_blocks)
    gx_sum = Halving(gx_keep, gx_send, "expert", across)
    gx_sent = gx_sum.wait(a_sum.wait(gx_send).exchange()).exchange()
    down_sum = Halving(down_keep, after(down_send, gx_send), "dp", far, 1)
    sent = [b_sum.wait(gx_sent).exchange()]
    gx_terms = gx_sum.rest()
    y_sum = Halving(y_keep, after(y_send, gx_terms[-1]), "expert", across)

    attended, grad_resid, sums = local(
        functools.partial(home_body, len(gx_terms)),
        [((tokens, width), BF16), ((tokens, width), F32), ((2 * SLOTS, width), F32)],
    )(after(where, *sent), vectors, *gx_terms, own_resid, own_n2, own_gates, cotangent[0])
    attended_blocks = near_blocks("expert", far_blocks("expert", attended))
    s_sum = Halving(s_keep, after(s_send, attended), "dp", far, 1)
    sent = [part.wait(attended_blocks[2]).exchange() for part in (b_sum, down_sum)]
    share = slab // experts
    last = ((copies // 2, slab + -(-share // 16) * 16, max(width, LANES + 3 * columns)), BF16)
    quarter = ((experts // 2, tokens, width), BF16)
    l_keep, l_send, gn_keep, gn_send = moving(
        functools.partial(attend_back_body, experts, copies),
        [last, last, quarter, quarter],
        [((length, LANES), F32)] * 2
        + [((2 * SLOTS, width), F32), ((length, width), BF16)]
        + [((experts, length, columns), BF16), ((experts, tokens, width), BF16)]
        + [((padded, width), BF16)]
        + [((length, columns), BF16)] * 3
        + [((length, width), BF16), ((width, 3 * columns + VECTORS), BF16)]
        + [((2, own_heads, tokens, length), BF16)]
        + [((length, columns), F32)] * 3
        + [((length, 3 * columns), BF16)]
        + [((padded, width), F32), ((width, 3 * columns), F32), ((LANES, width), F32)]
        + [((width, LANES), F32), last, last, quarter, quarter],
        5 * experts + 13,
    )(
        after(where, *sent), cosines, sines, sums, *attended_blocks, *mixed_blocks, *x,
        out_whole, q, k, v, n1, weight, probs,
    )
    last_sum = Halving(l_keep, l_send, "dp", far)
    gn_sum = Halving(gn_keep, gn_send, "expert", across)

    sent = down_sum.wait(l_send, a_sum.arrived(), b_sum.arrived()).exchange()
    s_sent = s_sum.wait(l_send).exchange()
    gn_sent = gn_sum.wait(sent, s_sent).exchange()
    last_sent = last_sum.wait(gn_sent).exchange()
    y_sent = y_sum.wait(last_sent).exchange()
    s_sum.wait(last_sent).exchange()
    last_sent = last_sum.wait(y_sent).exchange()
    gn_terms = gn_sum.wait(last_sent).rest()
    input_grad = local(
        functools.partial(finish_body, len(gn_terms)), [((tokens, width), BF16)]
    )(where, vectors, inputs[0], *gn_terms, grad_resid)[0]
    outputs = (own_resid + added(y_sum.wait(last_sent).rest())).astype(BF16)
    for part in (a_sum, b_sum, s_sum, down_sum):
        part.wait(last_sent)
    s_terms = s_sum.rest()
    hidden = expert_gate.shape[2]
    a_terms, b_terms = a_sum.rest(), b_sum.rest()
    gate_grad, up_grad = moving(
        functools.partial(collect_body, tile),
        [((slab, hidden), F32)] * 2,
        [((len(a_terms) + len(b_terms), slab, hidden), BF16)] + [((slab, hidden), F32)] * 2,
        len(a_terms) + len(b_terms) + 2,
    )(where, *a_terms, *b_terms)
    down_grad = added(down_sum.rest())
    if apart:

        def shares(terms, columns, bottom):
            rows, lanes = terms[0].shape[1:]
            *pieces, rest = mixed_kernel(
                functools.partial(shares_body, experts, slab, bottom),
                [((share, columns), BF16)] * experts + [((bottom, width), F32)],
                [((len(terms), rows, lanes), BF16), ((rows, lanes), F32)],
                len(terms),
            )(where, *terms)
            return [swap(p, "expert", r) if r else p for r, p in enumerate(pieces)], rest

        unit_pieces, sdown_grad = shares(s_terms, 2 * total, units)
        last_sum.wait(gate_grad, down_grad, input_grad, outputs, sdown_grad)
        head_pieces, out_grad = shares(last_sum.rest(), LANES + 3 * columns, share)
        sgate_grad, sup_grad, qkv_grad, gain1_grad, gain2_grad, router_grad = local(
            functools.partial(assemble_body, experts, copies),
            [
                ((share, experts * total), F32),
                ((share, experts * total), F32),
                ((share, 3 * width), F32),
                ((1, share), F32),
                ((1, share), F32),
                ((experts, share), F32),
            ],
        )(where, *unit_pieces, *head_pieces)
        gain1_grad, gain2_grad, router_grad = gain1_grad[0], gain2_grad[0], router_grad.T
    else:
        shared_sum, last_total = added(s_terms), added(last_sum.rest())
        sdown_grad, out_grad = shared_sum[slab:, :width], last_total[slab : slab + share, :width]
        pieces = rows_to_owners(shared_sum[:slab, : 2 * total].astype(BF16)).astype(F32)
        pieces = pieces.reshape(experts, share, 2, copies, units).transpose(2, 1, 3, 0, 4)
        sgate_grad, sup_grad = pieces.reshape(2, share, total * experts)
        pieces = rows_to_owners(last_total[:slab, : LANES + 3 * columns].astype(BF16)).astype(F32)
        qkv_grad = pieces[:, :, LANES:].reshape(experts, share, 3, columns)
        qkv_grad = qkv_grad.transpose(1, 2, 0, 3).reshape(share, 3, padded)[:, :, :width]
        qkv_grad = qkv_grad.reshape(share, 3 * width)
        vector_sums = jnp.sum(pieces[:, :, :LANES], 0)
        gain1_grad, gain2_grad = vector_sums[:, 0], vector_sums[:, 1]
        router_grad = vector_sums[:, SLOTS : SLOTS + experts]
    return (
        outputs[None],
        input_grad[None],
        gain1_grad,
        qkv_grad,
        out_grad,
        gain2_grad,
        router_grad,
        sgate_grad,
        sup_grad,
        sdown_grad,
        gate_grad[None],
        up_grad[None],
        down_grad[None],
    )


def solution(mesh):
    return jax.shard_map(
        shards,
        mesh=mesh,
        in_specs=(
            P("dp", "expert", None),
            P("dp"),
            P("dp", None),
            P("dp", None),
            P("dp"),
            P("dp", None),
            P("dp", None),
            P("dp", None),
            P("dp", None),
            P("expert", None, None),
            P("expert", None, None),
            P("expert", None, None),
            P("dp", "expert", None),
            P("dp", None),
            P("dp", "expert", None),
        ),
        out_specs=(
            P("dp", "expert", None),
            P("dp", "expert", None),
            P(("dp", "expert")),
            P(("dp", "expert"), None),
            P(("dp", "expert"), None),
            P(("dp", "expert")),
            P(("dp", "expert"), None),
            P(("dp", "expert"), None),
            P(("dp", "expert"), None),
            P(("dp", "expert"), None),
            P("expert", "dp", None),
            P("expert", "dp", None),
            P("expert", "dp", None),
        ),
        check_vma=False,
    )
```

```python
import functools

import jax
import jax.numpy as jnp
import numpy as np
from jax import lax
from jax.experimental import pallas as pl
from jax.experimental.pallas import tpu as pltpu
from jax.sharding import PartitionSpec as P

HEAD_DIM = 64
PIECE = 256
F32 = jnp.float32
BF16 = jnp.bfloat16
LANES = 128
SLOTS = 8
VECTORS = 64
LIMIT = 63 << 20
VMEM = pl.BlockSpec(memory_space=pltpu.VMEM)
SMEM = pl.BlockSpec(memory_space=pltpu.SMEM)
ANY = pl.BlockSpec(memory_space=pl.ANY)


def swap(value, axis, distance):
    count = lax.axis_size(axis)
    return lax.ppermute(value, axis, [(i, i ^ distance) for i in range(count)])


def after(value, *others):
    return lax.optimization_barrier((value, *others))[0]


def bits_of(count):
    return [1 << k for k in range(count.bit_length() - 1)]


def far_blocks(axis, value):
    return {r: swap(value, axis, r) if r else value for r in range(0, lax.axis_size(axis), 2)}


def near_blocks(axis, found):
    every = dict(found)
    for r in found:
        every[r ^ 1] = swap(found[r], axis, 1)
    return [every[r] for r in range(lax.axis_size(axis))]


def in_order(blocks, axis):
    me = lax.axis_index(axis)
    rows = blocks[0].shape[0]
    whole = jnp.zeros((rows * len(blocks),) + blocks[0].shape[1:], blocks[0].dtype)
    for r, block in enumerate(blocks):
        whole = lax.dynamic_update_slice_in_dim(whole, block, (me ^ r) * rows, 0)
    return whole


def halves(order):
    rest = order[1:]
    found = []
    for r in range(2 << len(rest)):
        place = sum(((r & bit) != 0) << (len(rest) - 1 - i) for i, bit in enumerate(rest))
        found.append((r, bool(r & order[0]), place))
    return found


def crossed(r):
    return r // 4 * 4 + r % 2 * 2 + r // 2 % 2


def partner(me, place, r, turn=0):
    if crossed(r) == r:
        return place ^ r
    return place ^ jnp.where((me + turn) % 2 == 1, crossed(r), r)


def trade(value, axis, bit, turn):
    if axis != "dp":
        return swap(value, axis, bit)
    copies, experts = lax.axis_size("dp"), lax.axis_size("expert")
    pairs = []
    for d in range(copies):
        for e in range(experts):
            other = d ^ (crossed(bit) if (e + turn) % 2 else bit)
            pairs.append((d * experts + e, other * experts + e))
    return lax.ppermute(value, ("dp", "expert"), pairs)


class Halving:
    def __init__(self, keep, send, axis, order, turn=0):
        self.axis = axis
        self.turn = turn
        self.order = order[1:]
        self.count = keep.shape[0]
        self.terms = [keep, trade(send, axis, order[0], turn)]

    def wait(self, *others):
        self.terms[-1] = after(self.terms[-1], *others)
        return self

    def exchange(self):
        half = self.count // 2
        sent = sum(term[half : self.count].astype(F32) for term in self.terms).astype(BF16)
        self.terms.append(trade(sent, self.axis, self.order.pop(0), self.turn))
        self.count = half
        return sent

    def arrived(self):
        return self.terms[-1]

    def rest(self):
        while self.order:
            self.exchange()
        return self.terms


def added(terms):
    return sum(term[0].astype(F32) for term in terms)


def dot(left, right):
    return lax.dot_general(left, right, (((1,), (0,)), ((), ())), preferred_element_type=F32)


def dot_t(left, right):
    return lax.dot_general(left, right, (((1,), (1,)), ((), ())), preferred_element_type=F32)


def t_dot(left, right):
    return lax.dot_general(left, right, (((0,), (0,)), ((), ())), preferred_element_type=F32)


def local(body, outs, scratch=(), scalars=1):
    def call(*args):
        return pl.pallas_call(
            body,
            out_shape=[jax.ShapeDtypeStruct(shape, kind) for shape, kind in outs],
            in_specs=[SMEM] * scalars + [VMEM] * (len(args) - scalars),
            out_specs=[VMEM] * len(outs),
            scratch_shapes=[pltpu.VMEM(shape, kind) for shape, kind in scratch],
            compiler_params=pltpu.CompilerParams(vmem_limit_bytes=LIMIT),
            cost_estimate=pl.CostEstimate(flops=10**8, bytes_accessed=10**5, transcendentals=0),
        )(*args)

    return call


def moving(body, outs, scratch, copies, scalars=1):
    def call(*args):
        return pl.pallas_call(
            body,
            out_shape=[jax.ShapeDtypeStruct(shape, kind) for shape, kind in outs],
            in_specs=[SMEM] * scalars + [ANY] * (len(args) - scalars),
            out_specs=[ANY] * len(outs),
            scratch_shapes=[pltpu.VMEM(shape, kind) for shape, kind in scratch]
            + [pltpu.SemaphoreType.DMA((copies,))],
            compiler_params=pltpu.CompilerParams(vmem_limit_bytes=LIMIT),
            cost_estimate=pl.CostEstimate(flops=10**8, bytes_accessed=10**5, transcendentals=0),
        )(*args)

    return call


def mixed_kernel(body, outs, scratch, copies, scalars=1):
    def call(*args):
        return pl.pallas_call(
            body,
            out_shape=[jax.ShapeDtypeStruct(shape, kind) for shape, kind in outs],
            in_specs=[SMEM] * scalars + [ANY] * (len(args) - scalars),
            out_specs=[VMEM] * len(outs),
            scratch_shapes=[pltpu.VMEM(shape, kind) for shape, kind in scratch]
            + [pltpu.SemaphoreType.DMA((copies,))],
            compiler_params=pltpu.CompilerParams(vmem_limit_bytes=LIMIT),
            cost_estimate=pl.CostEstimate(flops=10**8, bytes_accessed=10**5, transcendentals=0),
        )(*args)

    return call


class Moves:
    def __init__(self, sems):
        self.sems = sems
        self.used = 0
        self.open = []

    def start(self, source, target):
        move = pltpu.make_async_copy(source, target, self.sems.at[self.used])
        self.used += 1
        move.start()
        self.open.append(move)
        return move

    def wait(self, *moves):
        for move in moves:
            move.wait()
            self.open = [other for other in self.open if other is not move]

    def finish(self):
        self.wait(*list(self.open))


def rows_at(place, count):
    return pl.ds(pl.multiple_of(place * count, count), count)


def normal(values):
    factor = lax.rsqrt(jnp.mean(values * values, -1, keepdims=True) + 1e-06)
    return values * factor, factor


def normal_back(grad_normed, unit, factor, gain):
    grad_unit = grad_normed * gain
    return factor * (grad_unit - unit * jnp.mean(grad_unit * unit, -1, keepdims=True))


def turned(pairs, cosines, sines):
    span = pairs.shape[1]
    lane = lax.broadcasted_iota(jnp.int32, pairs.shape, 1)
    first = lane % HEAD_DIM < HEAD_DIM // 2
    partner = jnp.where(
        first, pltpu.roll(pairs, span - HEAD_DIM // 2, 1), pltpu.roll(pairs, HEAD_DIM // 2, 1)
    )
    return pairs * cosines + partner * sines


def rotary_tables(count):
    halfway = HEAD_DIM // 2
    frequency = np.power(10000.0, -np.arange(halfway, dtype=np.float32) / halfway)
    angles = np.arange(count, dtype=np.float32)[:, None] * frequency.astype(np.float32)[None, :]
    cosines, sines = np.cos(angles), np.sin(angles)
    cosines = np.tile(cosines, (1, 4)).astype(np.float32)
    sines = np.concatenate([-sines, sines, -sines, sines], 1).astype(np.float32)
    return jnp.asarray(cosines), jnp.asarray(sines)


def widened(table, span):
    return jnp.concatenate([table] * (span // LANES), 1)


def reach(block, experts, tokens):
    return min(block + 2, experts) * tokens


def pack_first_body(experts, where, gain1, gain2, router, qkv, result, wide):
    slab, width = result.shape[0], qkv.shape[1] // 3
    columns = (result.shape[1] - VECTORS) // 3
    wide[...] = jnp.zeros_like(wide)
    wide[0:1, :slab] = gain1[...].astype(F32)
    wide[1:2, :slab] = gain2[...].astype(F32)
    wide[SLOTS : SLOTS + router.shape[0], :slab] = router[...].astype(F32)
    result[:, 3 * columns :] = wide[...].T[:slab, :VECTORS].astype(BF16)
    for e in range(experts):

        @pl.when(where[0] == e)
        def _():
            for i in range(3):
                start = min(e * columns, width)
                stop = min(start + columns, width)
                at = i * columns
                if stop > start:
                    result[:, at : at + stop - start] = qkv[:, i * width + start : i * width + stop]
                if stop - start < columns:
                    blank = jnp.zeros((slab, columns - stop + start), BF16)
                    result[:, at + stop - start : at + columns] = blank


def pack_units_body(experts, copies, where, gate, up, down, result):
    slab, width = gate.shape[0], down.shape[1]
    units = down.shape[0] // experts
    total = copies * units
    for e in range(experts):

        @pl.when(where[0] == e)
        def _():
            for k, matrix in enumerate((gate, up)):
                parts = [
                    matrix[:, (d * experts + e) * units : (d * experts + e + 1) * units]
                    for d in range(copies)
                ]
                result[:slab, k * total : (k + 1) * total] = jnp.concatenate(parts, 1)
            result[slab:, :width] = down[e * units : (e + 1) * units, :]
            if result.shape[1] > width:
                result[slab:, width:] = jnp.zeros((units, result.shape[1] - width), BF16)


def attend_body(experts, copies, blocks, *refs):
    where, starts, cosine_in, sine_in = refs[:4]
    x_refs, w_refs = refs[4 : 4 + experts], refs[4 + experts : 4 + experts + blocks]
    refs = refs[4 + experts + blocks :]
    n1_out, q_out, k_out, v_out, probs_out, mixed_out, weight_out, vectors_out = refs[:8]
    cosine_table, sine_table, x, n1, q, k, v, probs, mixed, weight, vectors, sems = refs[8:]
    moves = Moves(sems)
    me, place = where[0], where[1]
    tokens = x_refs[0].shape[0]
    columns = q.shape[1]
    own_heads = columns // HEAD_DIM
    slab = w_refs[0].shape[0]
    if blocks == 1:
        arriving = [moves.start(w_refs[0], weight)]
    else:
        arriving = [
            moves.start(w_refs[r], weight.at[rows_at(place ^ r, slab), :]) for r in range(blocks)
        ]
    tables = [moves.start(cosine_in, cosine_table), moves.start(sine_in, sine_table)]
    rows_in = [moves.start(x_refs[r], x.at[r]) for r in range(experts)]
    moves.wait(*arriving)
    vectors[...] = weight[:, 3 * columns :].astype(F32).T
    moves.start(weight, weight_out)
    moves.start(vectors, vectors_out)
    gain = vectors[0:1, :]
    moves.wait(*tables)
    for r in range(experts):
        rows = rows_at(me ^ r, tokens)
        moves.wait(rows_in[r])
        unit, _ = normal(x[r].astype(F32))
        normed = (unit * gain).astype(BF16)
        n1[rows, :] = normed
        projected = dot(normed, weight[:, : 3 * columns])
        cosines = widened(cosine_table[rows, :], 2 * columns)
        sines = widened(sine_table[rows, :], 2 * columns)
        pair = turned(projected[:, : 2 * columns], cosines, sines).astype(BF16)
        q[rows, :] = pair[:, :columns] * HEAD_DIM ** (-0.5)
        k[rows, :] = pair[:, columns:]
        v[rows, :] = projected[:, 2 * columns :].astype(BF16)
    for held, result in ((n1, n1_out), (q, q_out), (k, k_out), (v, v_out)):
        moves.start(held, result)
    pieces = starts.shape[1]
    leaving = {}
    for block in range(experts):
        seen = reach(block, experts, tokens)
        rows = slice(block * tokens, (block + 1) * tokens)
        query_pos = block * tokens + lax.broadcasted_iota(jnp.int32, (tokens, 1), 0)
        key_pos = lax.broadcasted_iota(jnp.int32, (1, seen), 1)
        query_piece = jnp.full((tokens, 1), -1, jnp.int32)
        key_piece = jnp.full((1, seen), -2, jnp.int32)
        for j in range(pieces):
            start = starts[0, j]
            query_piece = jnp.where(
                (query_pos >= start) & (query_pos < start + PIECE), j, query_piece
            )
            key_piece = jnp.where((key_pos >= start) & (key_pos < start + PIECE), j, key_piece)
        bias = jnp.where((key_pos <= query_pos) | (query_piece == key_piece), 0.0, -1e30)
        slot = block % 2
        if block >= 2:
            moves.wait(leaving[block - 2])
        for h in range(own_heads):
            head = slice(h * HEAD_DIM, (h + 1) * HEAD_DIM)
            scores = dot_t(q[rows, head], k[:seen, head]) + bias
            powers = jnp.exp(scores - jnp.max(scores, -1, keepdims=True))
            share = (powers * (1.0 / jnp.sum(powers, -1, keepdims=True))).astype(BF16)
            probs[slot, h, :, :seen] = share
            mixed[rows, head] = dot(share, v[:seen, head]).astype(BF16)
        leaving[block] = moves.start(
            probs.at[slot, :, :, :seen], probs_out.at[:, rows, :seen]
        )
    moves.start(mixed, mixed_out)
    moves.finish()


def settle_body(experts, blocks, *refs):
    where, vectors_in = refs[:2]
    x_refs = refs[2 : 2 + experts]
    dy_refs = refs[2 + experts : 2 + 2 * experts]
    m_refs = refs[2 + 2 * experts : 2 + 3 * experts]
    o_refs, refs = refs[2 + 3 * experts :][:blocks], refs[2 + 3 * experts + blocks :]
    n2_out, n2_turned_out, dy_out, gates_out, own_resid_out, own_n2_out, own_gates_out, matrix_out = refs[:8]
    vectors, x, dy, mixed, out_matrix, n2, n2_turned, gates, own_resid, sems = refs[8:]
    moves = Moves(sems)
    me, place = where[0], where[1]
    slab = o_refs[0].shape[0]
    tokens, width = x_refs[0].shape
    columns = m_refs[0].shape[1]
    mixed_in = [moves.start(m_refs[j], mixed.at[j]) for j in range(experts)]
    vectors_move = moves.start(vectors_in, vectors)
    x_in = [moves.start(x_refs[r], x.at[r]) for r in range(experts)]
    dy_in = [moves.start(dy_refs[r], dy.at[r]) for r in range(experts)]
    if blocks == 1:
        matrix_in = [moves.start(o_refs[0], out_matrix)]
    else:
        matrix_in = [
            moves.start(o_refs[r], out_matrix.at[rows_at(place ^ r, slab), :])
            for r in range(blocks)
        ]
    moves.wait(*matrix_in, *mixed_in, vectors_move)
    moves.start(out_matrix, matrix_out)
    gain = vectors[1:2, :]
    router = vectors[SLOTS : 2 * SLOTS, :].astype(BF16)
    for r in range(experts):
        rows = rows_at(me ^ r, tokens)
        moves.wait(x_in[r], dy_in[r])
        moves.start(dy.at[r, :, :width], dy_out.at[rows, :])
        resid = x[r].astype(F32)
        for j in range(experts):
            resid += dot(mixed[j, rows, :], out_matrix[rows_at(me ^ j, columns), :])
        unit, _ = normal(resid)
        normed = (unit * gain).astype(BF16)
        logits = dot_t(normed, router)
        chosen = dy[r, :, width : width + SLOTS].astype(F32)
        masked = jnp.where(chosen > 0.0, logits, -1e30)
        powers = chosen * jnp.exp(masked - jnp.max(masked, -1, keepdims=True))
        n2[r] = normed
        n2_turned[r] = normed.astype(F32).T.astype(BF16)
        gates[r] = powers / jnp.sum(powers, -1, keepdims=True)
        moves.start(n2.at[r], n2_out.at[rows, :])
        moves.start(n2_turned.at[r], n2_turned_out.at[:, rows])
        moves.start(gates.at[r], gates_out.at[rows, :])
        if r == 0:
            own_resid[...] = resid
            moves.start(own_resid, own_resid_out)
            moves.start(n2.at[0], own_n2_out)
            moves.start(gates.at[0], own_gates_out)
    moves.finish()


def unit_tile(me, fresh, n2, dy, gates, wg, wu, wd, y, gx, gg, hidden_s, gate_s, up_s):
    chunk = 512 if n2.shape[0] <= 1024 else 256

    def step(c, carry):
        rows = pl.ds(pl.multiple_of(c * chunk, chunk), chunk)
        x, g = n2[rows, :], dy[rows, :]
        gate_pre = dot(x, wg[...])
        up_pre = dot(x, wu[...])
        raw = dot_t(g, wd[...])
        logistic = lax.logistic(gate_pre)
        swish = gate_pre * logistic
        slope = logistic + swish * (1.0 - logistic)
        hidden = swish * up_pre
        if gates is not None:
            lane = lax.broadcasted_iota(jnp.int32, (chunk, SLOTS), 1)
            scale = jnp.sum(jnp.where(lane == me, gates[rows, :], 0.0), -1, keepdims=True)
            gg[rows, :] += jnp.sum(hidden * raw, -1, keepdims=True)
            hidden = hidden * scale
            raw = raw * scale
        hidden = hidden.astype(BF16)
        grad_gate = (raw * up_pre * slope).astype(BF16)
        grad_up = (raw * swish).astype(BF16)
        hidden_s[rows, :] = hidden
        gate_s[rows, :] = grad_gate
        up_s[rows, :] = grad_up
        out = dot(hidden, wd[...])
        back = dot_t(grad_gate, wg[...]) + dot_t(grad_up, wu[...])
        if fresh:
            y[rows, :] = out
            gx[rows, :] = back
        else:
            y[rows, :] += out
            gx[rows, :] += back
        return carry

    lax.fori_loop(0, n2.shape[0] // chunk, step, 0)


def shared_body(experts, copies, blocks, *refs):
    where, n2_in, n2_turned_in, dy_in, y_in, gx_in, gg_in = refs[:7]
    b_refs, refs = refs[7 : 7 + blocks], refs[7 + blocks :]
    keep_out, send_out, y_keep_out, y_send_out, gx_keep_out, gx_send_out = refs[:6]
    n2, n2_turned, dy, y, gx, y_more, gx_more, gg, wg, wu, wd = refs[6:17]
    hidden_s, gate_s, up_s, grad_gate, grad_up, grad_down = refs[17:23]
    keep, send, y_keep, y_send, gx_keep, gx_send, sems = refs[23:]
    moves = Moves(sems)
    me, place = where[0], where[1]
    width = n2.shape[1]
    total = wg.shape[1]
    units = total // copies
    slab = width // copies
    tokens = y_keep.shape[1]
    if blocks == 2:
        places = [
            (b_refs[0].at[:, :total], wg),
            (b_refs[0].at[:, total : 2 * total], wu),
            (b_refs[1], wd),
        ]
    else:
        places = []
        for r in range(copies):
            rows = slice(r * slab, (r + 1) * slab)
            places.append((b_refs[0].at[r, :slab, :total], wg.at[rows, :]))
            places.append((b_refs[0].at[r, :slab, total : 2 * total], wu.at[rows, :]))
            rows = slice(r * units, (r + 1) * units)
            places.append((b_refs[0].at[r, slab:, :width], wd.at[rows, :]))
    arriving = [moves.start(source, target) for source, target in places]
    arriving += [moves.start(n2_in, n2), moves.start(dy_in, dy)]
    moves.wait(*arriving)
    sums_in = [moves.start(gx_in, gx_more), moves.start(gg_in, gg), moves.start(y_in, y_more)]
    turned_in = moves.start(n2_turned_in, n2_turned)
    unit_tile(None, True, n2, dy, None, wg, wu, wd, y, gx, None, hidden_s, gate_s, up_s)
    moves.wait(*sums_in)
    for r, leaves, k in halves(bits_of(experts)):
        rows = rows_at(me ^ r, tokens)
        half = gx_send if leaves else gx_keep
        half[k, :, :width] = (gx[rows, :] + gx_more[rows, :]).astype(BF16)
        lane = lax.broadcasted_iota(jnp.int32, (tokens, LANES), 1)
        whole = gg[rows, :]
        coarse = whole.astype(BF16).astype(F32)
        half[k, :, width:] = (
            jnp.where(lane == me, coarse, 0.0)
            + jnp.where(lane == me + SLOTS, whole - coarse, 0.0)
        ).astype(BF16)
        half = y_send if leaves else y_keep
        half[k] = (y[rows, :] + y_more[rows, :]).astype(BF16)
    moves.start(gx_send, gx_send_out)
    moves.start(gx_keep, gx_keep_out)
    moves.start(y_send, y_send_out)
    moves.start(y_keep, y_keep_out)
    moves.wait(turned_in)
    grad_gate[...] = dot(n2_turned[...], gate_s[...])
    grad_up[...] = dot(n2_turned[...], up_s[...])
    grad_down[...] = t_dot(hidden_s[...], dy[...])
    for r, leaves, k in halves(bits_of(copies)):
        half = send if leaves else keep
        rows = rows_at(partner(me, place, r, 1), slab)
        half[k, :slab, :total] = grad_gate[rows, :].astype(BF16)
        half[k, :slab, total : 2 * total] = grad_up[rows, :].astype(BF16)
        rows = rows_at(partner(me, place, r, 1), units)
        half[k, slab:, :width] = grad_down[rows, :].astype(BF16)
        spare = half.shape[2] - width
        if spare:
            half[k, slab:, width:] = jnp.zeros((units, spare), BF16)
        spare = half.shape[2] - 2 * total
        if spare:
            half[k, :slab, 2 * total :] = jnp.zeros((slab, spare), BF16)
    moves.start(send, send_out)
    moves.start(keep, keep_out)
    moves.finish()


def expert_body(copies, last, *refs):
    where, n2_in, n2_turned_in, dy_in, gates_in, wg_in, wu_in, wd_in = refs[:8]
    refs = refs[8:]
    if last:
        y_in, gx_in, gg_in, down_in = refs[:4]
        refs = refs[4:]
    keep_out, send_out, y_out, gx_out, gg_out, down_out = refs[:6]
    refs = refs[6:]
    if last:
        down_send_out, refs = refs[0], refs[1:]
    n2, n2_turned, dy, gates, y, gx, gg, down, wg, wu, wd = refs[:11]
    hidden_s, gate_s, up_s, grad_gate, grad_up, keep, send = refs[11:18]
    if last:
        down_keep, down_send, gg_more = refs[18:21]
        gx_more, y_more = refs[21], refs[-2]
        roomy = y_more is not gx_more
    moves = Moves(refs[-1])
    me, place = where[0], where[1]
    slab = keep.shape[2]
    tile = wg.shape[2]
    hidden = wd_in.shape[0]
    steps = hidden // 2 // tile
    first = hidden // 2 if last else 0
    units = [slice(first + s * tile, first + (s + 1) * tile) for s in range(steps)]

    def fetch(step):
        slot = step % 2
        return [
            moves.start(wg_in.at[:, units[step]], wg.at[slot]),
            moves.start(wu_in.at[:, units[step]], wu.at[slot]),
            moves.start(wd_in.at[units[step], :], wd.at[slot]),
        ]

    weights = {0: fetch(0)}
    arriving = [moves.start(n2_in, n2), moves.start(dy_in, dy), moves.start(gates_in, gates)]
    gg[...] = jnp.zeros_like(gg)
    moves.wait(*arriving)
    turned_in = [moves.start(n2_turned_in, n2_turned)]
    weights[1] = fetch(1)
    if last:
        sums_in = [moves.start(gx_in, gx_more), moves.start(gg_in, gg_more)]
        if roomy:
            sums_in.append(moves.start(y_in, y_more))
        earlier = moves.start(down_in, down.at[: hidden // 2, :])
    leaving = {}
    for step in range(steps):
        slot = step % 2
        moves.wait(*weights[step])
        unit_tile(
            me, step == 0, n2, dy, gates, wg.at[slot], wu.at[slot], wd.at[slot],
            y, gx, gg, hidden_s, gate_s, up_s,
        )
        if 1 <= step and step + 1 < steps:
            weights[step + 1] = fetch(step + 1)
        elif step == 0 and steps > 2:
            weights[2] = fetch(2)
        if step == steps - 1:
            if last:
                moves.wait(*sums_in)
                gg[...] += gg_more[...]
                gx[...] += gx_more[...]
                if not roomy:
                    moves.wait(moves.start(y_in, y_more))
                y[...] += y_more[...]
            moves.start(y, y_out)
            moves.start(gx, gx_out)
            moves.start(gg, gg_out)
        moves.wait(*turned_in)
        turned_in = []
        grad_gate[...] = dot(n2_turned[...], gate_s[...])
        grad_up[...] = dot(n2_turned[...], up_s[...])
        down[units[step] if last else slice(step * tile, (step + 1) * tile), :] = t_dot(
            hidden_s[...], dy[...]
        ).astype(BF16)
        if step >= 2:
            moves.wait(*leaving[step - 2])
        for r, leaves, k in halves(bits_of(copies)):
            half = send if leaves else keep
            rows = rows_at(partner(me, place, r), slab)
            half[slot, k, :, :tile] = grad_gate[rows, :].astype(BF16)
            half[slot, k, :, tile:] = grad_up[rows, :].astype(BF16)
        at = slice(2 * step * tile, 2 * (step + 1) * tile)
        leaving[step] = [
            moves.start(send.at[slot], send_out.at[:, :, at]),
            moves.start(keep.at[slot], keep_out.at[:, :, at]),
        ]
    if last:
        moves.wait(earlier)
        per = hidden // copies
        for r, leaves, k in halves(bits_of(copies)):
            half = down_send if leaves else down_keep
            half[k] = down[rows_at(partner(me, place, r, 1), per), :]
        moves.start(down_send, down_send_out)
        moves.start(down_keep, down_out)
    else:
        moves.start(down, down_out)
    moves.finish()


def home_body(terms, *refs):
    vectors_in, parts = refs[1], refs[2 : 2 + terms]
    resid_in, n2_in, gates_in, cotangent_in, attended, grad_resid, sums = refs[2 + terms : 9 + terms]
    vectors, held, own_resid, own_n2, own_gates, cotangent, sems = refs[9 + terms :]
    moves = Moves(sems)
    pairs = [(part.at[0], held.at[i]) for i, part in enumerate(parts)]
    pairs += [(vectors_in, vectors), (resid_in, own_resid), (n2_in, own_n2)]
    pairs += [(gates_in, own_gates), (cotangent_in, cotangent)]
    moves.wait(*[moves.start(source, target) for source, target in pairs])
    width = own_n2.shape[1]
    total = held[0].astype(F32)
    for i in range(1, terms):
        total += held[i].astype(F32)
    grad_gates = total[:, width : width + SLOTS] + total[:, width + SLOTS : width + 2 * SLOTS]
    gates = own_gates[...]
    grad_logits = (
        gates * (grad_gates - jnp.sum(gates * grad_gates, -1, keepdims=True))
    ).astype(BF16)
    grad_normed = total[:, :width] + dot(
        grad_logits, vectors[SLOTS : 2 * SLOTS, :].astype(BF16)
    )
    unit, factor = normal(own_resid[...])
    sums[0:SLOTS, :] = jnp.broadcast_to(
        jnp.sum(grad_normed * unit, 0, keepdims=True), (SLOTS, width)
    )
    sums[SLOTS : 2 * SLOTS, :] = t_dot(grad_logits, own_n2[...])
    back = cotangent[...].astype(F32) + normal_back(grad_normed, unit, factor, vectors[1:2, :])
    grad_resid[...] = back
    attended[...] = back.astype(BF16)


def grad_share(matrix, start, me, count, experts):
    if count % 8 == 0:
        return matrix[pl.ds(pl.multiple_of(start + me * count, count), count), :]
    rows = matrix[pl.ds(pl.multiple_of(start, 8), count * experts), :]
    picked = rows[:count]
    for e in range(1, experts):
        picked = jnp.where(me == e, rows[e * count : (e + 1) * count], picked)
    return picked


def attend_back_body(experts, copies, *refs):
    where, cosine_in, sine_in, sums_in = refs[:4]
    a_refs = refs[4 : 4 + experts]
    m_refs = refs[4 + experts : 4 + 2 * experts]
    x_refs = refs[4 + 2 * experts : 4 + 3 * experts]
    refs = refs[4 + 3 * experts :]
    matrix_in, q_in, k_in, v_in, n1_in, weight_in, probs_in = refs[:7]
    keep_out, send_out, gn_keep_out, gn_send_out = refs[7:11]
    refs = refs[11:]
    cosine_table, sine_table, sums, attended, mixed, x, out_matrix, q, k, v, n1, weight, probs = refs[:13]
    grad_q, grad_k, grad_v, grad_projected, grad_out, grad_qkv, extra, side = refs[13:21]
    keep, send, gn_keep, gn_send, sems = refs[21:]
    moves = Moves(sems)
    me, place = where[0], where[1]
    tokens, width = x_refs[0].shape
    columns = q.shape[1]
    own_heads = columns // HEAD_DIM
    root = HEAD_DIM ** (-0.5)

    def fetch(block):
        seen = reach(block, experts, tokens)
        rows = slice(block * tokens, (block + 1) * tokens)
        return moves.start(
            probs_in.at[:, rows, :seen], probs.at[block % 2, :, :, :seen]
        )

    needed = [
        moves.start(a_refs[r], attended.at[rows_at(me ^ r, tokens), :]) for r in range(experts)
    ]
    needed += [moves.start(matrix_in, out_matrix)]
    needed += [moves.start(source, held) for source, held in ((v_in, v), (k_in, k), (q_in, q))]
    shares = {0: fetch(0), 1: fetch(1)}
    mixed_in = [moves.start(m_refs[j], mixed.at[j]) for j in range(experts)]
    later = [moves.start(weight_in, weight), moves.start(cosine_in, cosine_table)]
    later += [moves.start(sine_in, sine_table), moves.start(sums_in, sums)]
    x_in = [moves.start(x_refs[r], x.at[r]) for r in range(experts)]
    n1_move = moves.start(n1_in, n1)
    grad_k[...] = jnp.zeros_like(grad_k)
    grad_v[...] = jnp.zeros_like(grad_v)
    moves.wait(*needed)
    own_out = out_matrix[rows_at(me, columns), :]
    for block in range(experts):
        seen = reach(block, experts, tokens)
        rows = slice(block * tokens, (block + 1) * tokens)
        slot = block % 2
        grad_mixed = dot_t(attended[rows, :], own_out).astype(BF16)
        moves.wait(shares[block])
        for h in range(own_heads):
            head = slice(h * HEAD_DIM, (h + 1) * HEAD_DIM)
            gm = grad_mixed[:, head]
            share = probs[slot, h, :, :seen]
            wide = share.astype(F32)
            grad_probs = dot_t(gm, v[:seen, head])
            delta = jnp.sum(wide * grad_probs, -1, keepdims=True)
            grad_scores = (wide * (grad_probs - delta)).astype(BF16)
            grad_q[rows, head] = dot(grad_scores, k[:seen, head]) * root
            grad_k[:seen, head] += t_dot(grad_scores, q[rows, head])
            grad_v[:seen, head] += t_dot(share, gm)
        if block + 2 < experts:
            shares[block + 2] = fetch(block + 2)
    moves.wait(*later)
    gain_sum = jnp.zeros((1, width), F32)
    for r in list(range(1, experts, 2)) + list(range(0, experts, 2)):
        rows = rows_at(me ^ r, tokens)
        pair = jnp.concatenate([grad_q[rows, :], grad_k[rows, :]], 1)
        cosines = widened(cosine_table[rows, :], 2 * columns)
        sines = widened(sine_table[rows, :], 2 * columns)
        back = turned(pair, cosines, -sines).astype(BF16)
        grad_projected[rows, : 2 * columns] = back
        grad_projected[rows, 2 * columns :] = grad_v[rows, :].astype(BF16)
        grad_normed = dot_t(grad_projected[rows, :], weight[:, : 3 * columns])
        moves.wait(x_in[r])
        unit, _ = normal(x[r].astype(F32))
        gain_sum += jnp.sum(grad_normed * unit, 0, keepdims=True)
        _, leaves, spot = halves(bits_of(experts))[r]
        half, result = (gn_send, gn_send_out) if leaves else (gn_keep, gn_keep_out)
        half[spot] = grad_normed.astype(BF16)
        moves.start(half.at[spot], result.at[spot])
    moves.wait(n1_move, *mixed_in)
    for r in range(experts):
        grad_out[rows_at(me ^ r, columns), :] = t_dot(mixed[r], attended[...])
    grad_qkv[...] = t_dot(n1[...], grad_projected[...])
    extra[...] = jnp.zeros_like(extra)
    extra[0:1, :] = gain_sum
    extra[1:2, :] = sums[0:1, :]
    extra[SLOTS : 2 * SLOTS, :] = sums[SLOTS : 2 * SLOTS, :]
    side[...] = extra[...].T
    slab = width // copies
    share_rows = slab // experts
    spare = keep.shape[1] - slab
    for r, leaves, place_of in halves(bits_of(copies)):
        half = send if leaves else keep
        owner = partner(me, place, r)
        rows = rows_at(owner, slab)
        half[place_of, :slab, :LANES] = side[rows, :].astype(BF16)
        half[place_of, :slab, LANES : LANES + 3 * columns] = grad_qkv[rows, :].astype(BF16)
        block = grad_share(grad_out, owner * slab, me, share_rows, experts)
        if spare > share_rows:
            block = jnp.concatenate([block, jnp.zeros((spare - share_rows, width), F32)], 0)
        half[place_of, slab:, :width] = block.astype(BF16)
        if half.shape[2] > LANES + 3 * columns:
            half[place_of, :slab, LANES + 3 * columns :] = jnp.zeros(
                (slab, half.shape[2] - LANES - 3 * columns), BF16
            )
    moves.start(send, send_out)
    moves.start(keep, keep_out)
    moves.finish()


def finish_body(terms, *refs):
    where, vectors, x = refs[:3]
    parts = refs[3 : 3 + terms]
    grad_resid, result = refs[3 + terms :]
    total = added(parts)
    unit, factor = normal(x[...].astype(F32))
    back = normal_back(total, unit, factor, vectors[0:1, :])
    result[...] = (grad_resid[...] + back).astype(BF16)


def collect_body(tile, *refs):
    count = (len(refs) - 6) // 2
    where, terms = refs[0], refs[1 : 1 + 2 * count]
    gate_out, up_out, held, gate, up, sems = refs[1 + 2 * count :]
    moves = Moves(sems)
    arriving = [moves.start(term.at[0], held.at[i]) for i, term in enumerate(terms)]
    steps = gate.shape[1] // tile
    moves.wait(*arriving)
    for step in range(steps):
        which, at = divmod(step, steps // 2)
        for k, result in enumerate((gate, up)):
            lanes = slice((2 * at + k) * tile, (2 * at + k + 1) * tile)
            total = held[which * count, :, lanes].astype(F32)
            for i in range(1, count):
                total += held[which * count + i, :, lanes].astype(F32)
            result[:, step * tile : (step + 1) * tile] = total
    moves.start(gate, gate_out)
    moves.start(up, up_out)
    moves.finish()


def shares_body(experts, top, bottom, *refs):
    where, terms = refs[0], refs[1 : -4 - experts]
    pieces, rest_out = refs[-4 - experts : -4], refs[-4]
    held, total, sems = refs[-3:]
    moves = Moves(sems)
    me = where[0]
    arriving = [moves.start(term.at[0], held.at[i]) for i, term in enumerate(terms)]
    moves.wait(*arriving)
    whole = held[0].astype(F32)
    for i in range(1, len(terms)):
        whole += held[i].astype(F32)
    total[...] = whole
    rest_out[...] = total[top : top + bottom, : rest_out.shape[1]]
    count = top // experts
    for r in range(experts):
        block = total[rows_at(me ^ r, count), : pieces[r].shape[1]]
        pieces[r][...] = block.astype(BF16)


def assemble_body(experts, copies, *refs):
    where = refs[0]
    units_in, heads_in = refs[1 : 1 + experts], refs[1 + experts : 1 + 2 * experts]
    gate, up, qkv, gain1, gain2, router = refs[1 + 2 * experts :]
    total = units_in[0].shape[1] // 2
    units = total // copies
    columns = (heads_in[0].shape[1] - LANES) // 3
    width = qkv.shape[1] // 3
    side = heads_in[0][:, :LANES].astype(F32)
    for r in range(1, experts):
        side += heads_in[r][:, :LANES].astype(F32)
    rows = side.T
    gain1[...] = rows[0:1, :]
    gain2[...] = rows[1:2, :]
    router[...] = rows[SLOTS : SLOTS + experts, :]
    for e in range(experts):

        @pl.when(where[0] == e)
        def _():
            for k, result in enumerate((gate, up)):
                sources = [units_in[e ^ other][...].astype(F32) for other in range(experts)]
                parts = []
                for d in range(copies):
                    at = k * total + d * units
                    parts += [source[:, at : at + units] for source in sources]
                result[...] = jnp.concatenate(parts, 1)
            for i in range(3):
                at = LANES + i * columns
                parts = [
                    heads_in[e ^ other][:, at : at + columns].astype(F32)
                    for other in range(experts)
                ]
                qkv[:, i * width : (i + 1) * width] = jnp.concatenate(parts, 1)


def expert_half(operands, state, copies, tile, last):
    n2, wg = operands[1], operands[5]
    length, width = n2.shape
    hidden = wg.shape[1]
    slab, per = width // copies, hidden // copies
    half = (copies // 2, slab, hidden)
    sums = (length, width)
    outs = [(half, BF16), (half, BF16), (sums, F32), (sums, F32), ((length, LANES), F32)]
    down = (hidden if last else hidden // 2, width)
    slot = (2, copies // 2, slab, 2 * tile)
    scratch = [(sums, BF16), ((width, length), BF16), (sums, BF16), ((length, SLOTS), F32)]
    scratch += [(sums, F32)] * 2 + [((length, LANES), F32), (down, BF16)]
    scratch += [((2, width, tile), BF16)] * 2 + [((2, tile, width), BF16)]
    scratch += [((length, tile), BF16)] * 3 + [((width, tile), F32)] * 2 + [(slot, BF16)] * 2
    if last:
        final = [((copies // 2, per, width), BF16)] * 2
        outs += final
        scratch += final + [((length, LANES), F32)] + [(sums, F32)] * (2 if tile == 512 else 1)
    else:
        outs.append((down, BF16))
    steps = hidden // 2 // tile
    body = functools.partial(expert_body, copies, last)
    return moving(body, outs, scratch, 16 + 5 * steps)(*operands, *state)


def rows_to_owners(value):
    count = lax.axis_size("expert")
    me = lax.axis_index("expert")
    parts = value.reshape((count, value.shape[0] // count) + value.shape[1:])
    found = []
    for r in range(count):
        part = lax.dynamic_index_in_dim(parts, me ^ r, 0, keepdims=False)
        found.append((swap(part, "expert", r) if r else part)[None])
    return in_order(found, "expert")


def shards(
    inputs,
    norm1_gain,
    qkv_weight,
    out_weight,
    norm2_gain,
    router_weight,
    shared_gate,
    shared_up,
    shared_down,
    expert_gate,
    expert_up,
    expert_down,
    expert_ids,
    piece_starts,
    cotangent,
):
    tokens, width = inputs.shape[1:]
    heads = width // HEAD_DIM
    experts = lax.axis_size("expert")
    copies = lax.axis_size("dp")
    me = lax.axis_index("expert")
    place = lax.axis_index("dp")
    where = jnp.stack([me, place]).astype(jnp.int32)
    length = tokens * experts
    slab = width // copies
    own_heads = -(-heads // experts)
    columns = own_heads * HEAD_DIM
    padded = experts * columns
    units = shared_down.shape[0] // experts
    total = copies * units
    wide = max(2 * total, width)
    apart = slab % 16 == 0 and units % 16 == 0 and padded == width
    small = length <= 1024
    tile = 512 if small else 256

    first = local(
        functools.partial(pack_first_body, experts),
        [((slab, 3 * columns + VECTORS), BF16)],
        [((LANES, LANES), F32)],
    )(where, norm1_gain[None], norm2_gain[None], router_weight.T, qkv_weight)[0]
    x = far_blocks("expert", inputs[0])
    first = far_blocks("dp", first)
    named = jnp.any(
        expert_ids[0][:, :, None] == jnp.arange(LANES, dtype=jnp.int32)[None, None, :], 1
    ).astype(BF16)
    dy_own = jnp.concatenate([cotangent[0], named], 1)
    dy_far = far_blocks("expert", after(dy_own, x[2]))
    if apart:
        packed = local(
            functools.partial(pack_units_body, experts, copies), [((slab + units, wide), BF16)]
        )(where, shared_gate, shared_up, shared_down)[0]
        gate = [first[r] for r in first if r]
        first[6] = after(first[6], packed, dy_own)
        first = near_blocks("dp", first)
        gate += [first[1], x[2], packed]
        out_whole = lax.all_gather(after(out_weight, *gate), "dp", axis=0, tiled=True)
        out_blocks = [jnp.pad(out_whole, ((0, padded - width), (0, 0)))]
        shared_blocks = [lax.all_gather(packed, "dp", axis=0, tiled=False)]
    else:
        out_whole = lax.all_gather(out_weight, "dp", axis=0, tiled=True)
        out_blocks = [jnp.pad(out_whole, ((0, padded - width), (0, 0)))]

        def unit_columns(weight):
            split = weight.reshape(slab, copies, experts, units)
            split = lax.dynamic_index_in_dim(split, me, 2, keepdims=False)
            return split.reshape(slab, total)

        top = jnp.concatenate([unit_columns(shared_gate), unit_columns(shared_up)], 1)
        bottom = lax.dynamic_slice_in_dim(shared_down, me * units, units, 0)
        first = [in_order(near_blocks("dp", first), "dp")]
        shared_blocks = [lax.all_gather(part, "dp", axis=0, tiled=True) for part in (top, bottom)]
    x = near_blocks("expert", x)

    cosines, sines = rotary_tables(length)
    projected = [((length, width), BF16)] + [((length, columns), BF16)] * 3
    held = [
        ((length, columns), BF16),
        ((width, 3 * columns + VECTORS), BF16),
        ((VECTORS, width), F32),
    ]
    n1, q, k, v, probs, mixed, weight, vectors = moving(
        functools.partial(attend_body, experts, copies, len(first)),
        projected + [((own_heads, length, length), BF16)] + held,
        [((length, LANES), F32)] * 2
        + [((experts, tokens, width), BF16)]
        + projected
        + [((2, own_heads, tokens, length), BF16)]
        + held,
        len(first) + 2 * experts + 9,
        scalars=2,
    )(where, piece_starts, cosines, sines, *x, *first)
    mixed_blocks = near_blocks("expert", far_blocks("expert", mixed))
    dy_wide = near_blocks("expert", dy_far)
    n2, n2_turned, dy, gates, own_resid, own_n2, own_gates, out_whole = moving(
        functools.partial(settle_body, experts, len(out_blocks)),
        [
            ((length, width), BF16),
            ((width, length), BF16),
            ((length, width), BF16),
            ((length, SLOTS), F32),
            ((tokens, width), F32),
            ((tokens, width), BF16),
            ((tokens, SLOTS), F32),
            ((padded, width), BF16),
        ],
        [
            ((VECTORS, width), F32),
            ((experts, tokens, width), BF16),
            ((experts, tokens, width + LANES), BF16),
            ((experts, length, columns), BF16),
            ((padded, width), BF16),
            ((experts, tokens, width), BF16),
            ((experts, width, tokens), BF16),
            ((experts, tokens, SLOTS), F32),
            ((tokens, width), F32),
        ],
        len(out_blocks) + 7 * experts + 5,
    )(where, vectors, *x, *dy_wide, *mixed_blocks, *out_blocks)

    operands = [where, n2, n2_turned, dy, gates, expert_gate[0], expert_up[0], expert_down[0]]
    a_keep, a_send, y, gx, gg, down = expert_half(operands, (), copies, tile, False)
    far, across = bits_of(copies), bits_of(experts)
    a_sum = Halving(a_keep, a_send, "dp", far)
    b_keep, b_send, y, gx, gg, down_keep, down_send = expert_half(
        operands, (y, gx, gg, down), copies, tile, True
    )
    b_sum = Halving(b_keep, b_send, "dp", far)
    sent = a_sum.wait(b_send).exchange()
    half = ((copies // 2, slab + units, wide), BF16)
    both = [((length, width), F32)] * 2
    final = [
        ((experts // 2, tokens, lanes), BF16)
        for lanes in (width, width, width + LANES, width + LANES)
    ]
    s_keep, s_send, y_keep, y_send, gx_keep, gx_send = moving(
        functools.partial(shared_body, experts, copies, len(shared_blocks)),
        [half, half] + final,
        [((length, width), BF16), ((width, length), BF16), ((length, width), BF16)]
        + both * 2
        + [((length, LANES), F32)]
        + [((width, total), BF16)] * 2
        + [((total, width), BF16)]
        + [((length, total), BF16)] * 3
        + [((width, total), F32)] * 2
        + [((total, width), F32), half, half]
        + final,
        3 * copies + 12,
    )(after(where, sent), n2, n2_turned, dy, y, gx, gg, *shared_blocks)
    gx_sum = Halving(gx_keep, gx_send, "expert", across)
    gx_sent = gx_sum.wait(a_sum.wait(gx_send).exchange()).exchange()
    down_sum = Halving(down_keep, after(down_send, gx_send), "dp", far, 1)
    sent = [b_sum.wait(gx_sent).exchange()]
    gx_terms = gx_sum.rest()
    y_sum = Halving(y_keep, after(y_send, gx_terms[-1]), "expert", across)

    attended, grad_resid, sums = mixed_kernel(
        functools.partial(home_body, len(gx_terms)),
        [((tokens, width), BF16), ((tokens, width), F32), ((2 * SLOTS, width), F32)],
        [
            ((VECTORS, width), F32),
            ((len(gx_terms), tokens, width + LANES), BF16),
            ((tokens, width), F32),
            ((tokens, width), BF16),
            ((tokens, SLOTS), F32),
            ((tokens, width), BF16),
        ],
        len(gx_terms) + 5,
    )(after(where, *sent), vectors, *gx_terms, own_resid, own_n2, own_gates, cotangent[0])
    attended_blocks = near_blocks("expert", far_blocks("expert", attended))
    s_sum = Halving(s_keep, after(s_send, attended), "dp", far, 1)
    sent = [part.wait(attended_blocks[2]).exchange() for part in (b_sum, down_sum)]
    share = slab // experts
    last = ((copies // 2, slab + -(-share // 16) * 16, max(width, LANES + 3 * columns)), BF16)
    quarter = ((experts // 2, tokens, width), BF16)
    l_keep, l_send, gn_keep, gn_send = moving(
        functools.partial(attend_back_body, experts, copies),
        [last, last, quarter, quarter],
        [((length, LANES), F32)] * 2
        + [((2 * SLOTS, width), F32), ((length, width), BF16)]
        + [((experts, length, columns), BF16), ((experts, tokens, width), BF16)]
        + [((padded, width), BF16)]
        + [((length, columns), BF16)] * 3
        + [((length, width), BF16), ((width, 3 * columns + VECTORS), BF16)]
        + [((2, own_heads, tokens, length), BF16)]
        + [((length, columns), F32)] * 3
        + [((length, 3 * columns), BF16)]
        + [((padded, width), F32), ((width, 3 * columns), F32), ((LANES, width), F32)]
        + [((width, LANES), F32), last, last, quarter, quarter],
        5 * experts + 13,
    )(
        after(where, *sent), cosines, sines, sums, *attended_blocks, *mixed_blocks, *x,
        out_whole, q, k, v, n1, weight, probs,
    )
    last_sum = Halving(l_keep, l_send, "dp", far)
    gn_sum = Halving(gn_keep, gn_send, "expert", across)

    sent = down_sum.wait(l_send, a_sum.arrived(), b_sum.arrived()).exchange()
    s_sent = s_sum.wait(l_send).exchange()
    gn_sent = gn_sum.wait(sent, s_sent).exchange()
    last_sent = last_sum.wait(gn_sent).exchange()
    y_sent = y_sum.wait(last_sent).exchange()
    s_sum.wait(last_sent).exchange()
    last_sent = last_sum.wait(y_sent).exchange()
    gn_terms = gn_sum.wait(last_sent).rest()
    input_grad = local(
        functools.partial(finish_body, len(gn_terms)), [((tokens, width), BF16)]
    )(where, vectors, inputs[0], *gn_terms, grad_resid)[0]
    outputs = (own_resid + added(y_sum.wait(last_sent).rest())).astype(BF16)
    for part in (a_sum, b_sum, s_sum, down_sum):
        part.wait(last_sent)
    s_terms = s_sum.rest()
    hidden = expert_gate.shape[2]
    a_terms, b_terms = a_sum.rest(), b_sum.rest()
    gate_grad, up_grad = moving(
        functools.partial(collect_body, tile),
        [((slab, hidden), F32)] * 2,
        [((len(a_terms) + len(b_terms), slab, hidden), BF16)] + [((slab, hidden), F32)] * 2,
        len(a_terms) + len(b_terms) + 2,
    )(where, *a_terms, *b_terms)
    down_grad = added(down_sum.rest())
    if apart:

        def shares(terms, columns, bottom):
            rows, lanes = terms[0].shape[1:]
            *pieces, rest = mixed_kernel(
                functools.partial(shares_body, experts, slab, bottom),
                [((share, columns), BF16)] * experts + [((bottom, width), F32)],
                [((len(terms), rows, lanes), BF16), ((rows, lanes), F32)],
                len(terms),
            )(where, *terms)
            return [swap(p, "expert", r) if r else p for r, p in enumerate(pieces)], rest

        unit_pieces, sdown_grad = shares(s_terms, 2 * total, units)
        last_sum.wait(gate_grad, down_grad, input_grad, outputs, sdown_grad)
        head_pieces, out_grad = shares(last_sum.rest(), LANES + 3 * columns, share)
        sgate_grad, sup_grad, qkv_grad, gain1_grad, gain2_grad, router_grad = local(
            functools.partial(assemble_body, experts, copies),
            [
                ((share, experts * total), F32),
                ((share, experts * total), F32),
                ((share, 3 * width), F32),
                ((1, share), F32),
                ((1, share), F32),
                ((experts, share), F32),
            ],
        )(where, *unit_pieces, *head_pieces)
        gain1_grad, gain2_grad, router_grad = gain1_grad[0], gain2_grad[0], router_grad.T
    else:
        shared_sum, last_total = added(s_terms), added(last_sum.rest())
        sdown_grad, out_grad = shared_sum[slab:, :width], last_total[slab : slab + share, :width]
        pieces = rows_to_owners(shared_sum[:slab, : 2 * total].astype(BF16)).astype(F32)
        pieces = pieces.reshape(experts, share, 2, copies, units).transpose(2, 1, 3, 0, 4)
        sgate_grad, sup_grad = pieces.reshape(2, share, total * experts)
        pieces = rows_to_owners(last_total[:slab, : LANES + 3 * columns].astype(BF16)).astype(F32)
        qkv_grad = pieces[:, :, LANES:].reshape(experts, share, 3, columns)
        qkv_grad = qkv_grad.transpose(1, 2, 0, 3).reshape(share, 3, padded)[:, :, :width]
        qkv_grad = qkv_grad.reshape(share, 3 * width)
        vector_sums = jnp.sum(pieces[:, :, :LANES], 0)
        gain1_grad, gain2_grad = vector_sums[:, 0], vector_sums[:, 1]
        router_grad = vector_sums[:, SLOTS : SLOTS + experts]
    return (
        outputs[None],
        input_grad[None],
        gain1_grad,
        qkv_grad,
        out_grad,
        gain2_grad,
        router_grad,
        sgate_grad,
        sup_grad,
        sdown_grad,
        gate_grad[None],
        up_grad[None],
        down_grad[None],
    )


def solution(mesh):
    return jax.shard_map(
        shards,
        mesh=mesh,
        in_specs=(
            P("dp", "expert", None),
            P("dp"),
            P("dp", None),
            P("dp", None),
            P("dp"),
            P("dp", None),
            P("dp", None),
            P("dp", None),
            P("dp", None),
            P("expert", None, None),
            P("expert", None, None),
            P("expert", None, None),
            P("dp", "expert", None),
            P("dp", None),
            P("dp", "expert", None),
        ),
        out_specs=(
            P("dp", "expert", None),
            P("dp", "expert", None),
            P(("dp", "expert")),
            P(("dp", "expert"), None),
            P(("dp", "expert"), None),
            P(("dp", "expert")),
            P(("dp", "expert"), None),
            P(("dp", "expert"), None),
            P(("dp", "expert"), None),
            P(("dp", "expert"), None),
            P("expert", "dp", None),
            P("expert", "dp", None),
            P("expert", "dp", None),
        ),
        check_vma=False,
    )
```
